128 devices in a mesh: ctx: 64 (over x_hi, y, z, core), head: 2 (over x_lo).
Axes of the slice: x: 4 (x_hi: 2, x_lo: 2; x = x_hi * 2 + x_lo), y: 4, z: 4, core: 2. Of those that a mesh axis runs over, the one named last changes fastest.
Arguments:
- hidden_in: bfloat16 [16384, 768], P(('ctx', 'head')), may hold values from -6 to 6
- ln1_gain: bfloat16 [768], P('ctx'), may hold values from 0.099609375 to 1.8984375
- ln1_shift: bfloat16 [768], P('ctx'), may hold values from -1.5 to 1.5
- w_qkv: bfloat16 [768, 2304], P('ctx'), may hold values from -0.3125 to 0.3125
- qv_bias: bfloat16 [1536], P('ctx'), may hold values from -1.5 to 1.5
- w_out: bfloat16 [768, 768], P('ctx'), may hold values from -1.5 to 1.5
- out_bias: bfloat16 [768], P('ctx'), may hold values from -1.5 to 1.5
- ln2_gain: bfloat16 [768], P('ctx'), may hold values from 0.099609375 to 1.8984375
- ln2_shift: bfloat16 [768], P('ctx'), may hold values from -1.5 to 1.5
- w_fc: bfloat16 [768, 3072], P('ctx'), may hold values from -0.21875 to 0.21875
- fc_bias: bfloat16 [3072], P('ctx'), may hold values from -2.5 to 2.5
- w_proj: bfloat16 [3072, 768], P('ctx'), may hold values from -0.21875 to 0.21875
- proj_bias: bfloat16 [768], P('ctx'), may hold values from -1.5 to 1.5
- out_grad: bfloat16 [16384, 768], P(('ctx', 'head')), may hold values from -6 to 6
Outputs:
- hidden_out: bfloat16 [16384, 768], P(('ctx', 'head'))
- input_grad: float32 [16384, 768], P(('ctx', 'head'))
- ln1_gain_grad: float32 [768], P('ctx')
- ln1_shift_grad: float32 [768], P('ctx')
- w_qkv_grad: float32 [768, 2304], P('ctx')
- qv_bias_grad: float32 [1536], P('ctx')
- w_out_grad: float32 [768, 768], P('ctx')
- out_bias_grad: float32 [768], P('ctx')
- ln2_gain_grad: float32 [768], P('ctx')
- ln2_shift_grad: float32 [768], P('ctx')
- w_fc_grad: float32 [768, 3072], P('ctx')
- fc_bias_grad: float32 [3072], P('ctx')
- w_proj_grad: float32 [3072, 768], P('ctx')
- proj_bias_grad: float32 [768], P('ctx')
The draws below stay inside these ranges and needn't reach their ends.
All inputs are finite; a program needn't handle non-finite values.
Results may differ from the reference program's by a relative error of at most 0.018.
Values may be sent and summed in bfloat16 or wider, within the bound.
A program may use at most 256 MiB of HBM per device.

```python
import jax
import jax.numpy as jnp
from jax import lax

D = 768
HEADS = 12
HEAD_DIM = 64
FF = 3072
KEY_BLOCK = 512
TOKENS = 16384


def block_levels(key, extent, shards, low, largest):
    def one(position, parts):
        heights = jax.random.uniform(jax.random.fold_in(jax.random.fold_in(key, 6), position), (parts,), jnp.float32, low / len(shards), largest / len(shards))
        return jnp.repeat(jnp.exp(heights), extent[position] // parts).reshape((-1,) + (1,) * (len(extent) - position - 1))

    loudness = one(*shards[0])
    for cut in shards[1:]:
        loudness = loudness * one(*cut)
    return loudness


def noise(own_key, shape, scale, limit, split=(), kind=jnp.bfloat16):
    level = block_levels(own_key, shape, split, -0.22, 0.18) if split else 1.0
    drawn = jax.random.normal(own_key, shape, jnp.float32) * scale * level
    return jnp.minimum(jnp.maximum(drawn, -limit), limit).astype(kind)


def setup_inputs(seed: int = 0) -> dict:
    key_of = jax.random.split(jax.random.key(seed), 15)
    return {
        "hidden_in": noise(key_of[0], (TOKENS, D), 1.0, 6.0, ((0, 128),)),
        "ln1_gain": jnp.clip(1.0 + 0.18 * jax.random.normal(key_of[1], (D,), jnp.float32), 0.099609375, 1.8984375).astype(jnp.bfloat16),
        "ln1_shift": noise(key_of[2], (D,), 0.3, 1.5, ((0, 64),)),
        "w_qkv": noise(key_of[3], (D, 3 * D), (D // 2) ** -0.5, 0.3125, ((0, 64),)),
        "qv_bias": noise(key_of[4], (2 * D,), 0.3, 1.5, ((0, 64),)),
        "w_out": noise(key_of[5], (D, D), 16 ** -0.5, 1.5, ((0, 64),)),
        "out_bias": noise(key_of[6], (D,), 0.3, 1.5, ((0, 64),)),
        "ln2_gain": jnp.clip(1.0 + 0.18 * jax.random.normal(key_of[7], (D,), jnp.float32), 0.099609375, 1.8984375).astype(jnp.bfloat16),
        "ln2_shift": noise(key_of[8], (D,), 0.3, 1.5, ((0, 64),)),
        "w_fc": noise(key_of[9], (D, FF), D ** -0.5, 0.21875, ((0, 64),)),
        "fc_bias": noise(key_of[10], (FF,), 0.5, 2.5, ((0, 64),)),
        "w_proj": noise(key_of[11], (FF, D), (FF // 4) ** -0.5, 0.21875, ((0, 64),)),
        "proj_bias": noise(key_of[12], (D,), 0.3, 1.5, ((0, 64),)),
        "out_grad": noise(key_of[13], (TOKENS, D), 1.0, 6.0, ((0, 128),)),
    }


EPS = 1e-05
NEG = -1e+30
HIGH = lax.Precision.HIGHEST

@jax.custom_vjp
def low(v):
    return lax.optimization_barrier(v.astype(jnp.bfloat16)).astype(jnp.float32)

@jax.custom_vjp
def low_back(v):
    return v

def low_keep(v):
    return (low(v), None)

def low_pass(kept, grad):
    return (grad,)

def back_keep(v):
    return (v, None)

def back_low(kept, grad):
    return (low(grad),)
low.defvjp(low_keep, low_pass)
low_back.defvjp(back_keep, back_low)

def layer_norm(values, gain, shift):
    mean = lax.optimization_barrier(jnp.mean(values, axis=-1, keepdims=True))
    centred = values - mean
    spread = lax.optimization_barrier(jnp.mean(centred * centred, axis=-1, keepdims=True))
    return centred * lax.rsqrt(spread + EPS) * gain + shift

def matmul(left, right):
    return jnp.dot(left, right, precision=HIGH)

def head_attention(triple):
    queries, keys, values = triple
    seq = queries.shape[0]
    count = seq // KEY_BLOCK
    blocks = queries.reshape(count, KEY_BLOCK, HEAD_DIM)
    key_pos = jnp.arange(seq, dtype=jnp.int32)

    @jax.checkpoint
    def one_block(pair):
        query_blk, index = pair
        scores = jnp.einsum('qd,kd->qk', query_blk, keys, precision=HIGH) * HEAD_DIM ** (-0.5)
        scores = low_back(scores)
        query_pos = index * KEY_BLOCK + jnp.arange(KEY_BLOCK, dtype=jnp.int32)
        allowed = key_pos[None, :] <= query_pos[:, None]
        scores = jnp.where(allowed, scores, NEG)
        top = lax.optimization_barrier(jnp.max(scores, axis=-1, keepdims=True))
        expd = jnp.exp(scores - top)
        probs = low(expd / lax.optimization_barrier(jnp.sum(expd, axis=-1, keepdims=True)))
        return jnp.einsum('qk,kd->qd', probs, values, precision=HIGH)
    result = lax.map(one_block, (blocks, jnp.arange(count, dtype=jnp.int32)))
    return result.reshape(seq, HEAD_DIM)

def forward(hidden, gain1, shift1, w_qkv, qv_bias, w_out, out_bias, gain2, shift2, w_fc, fc_bias, w_proj, proj_bias):
    seq = hidden.shape[0]
    normed1 = low(layer_norm(hidden, gain1, shift1))
    bias_full = jnp.concatenate([qv_bias[:D], jnp.zeros((D,), jnp.float32), qv_bias[D:]])
    qkv = low(low_back(matmul(normed1, w_qkv) + bias_full))

    def split_heads(block):
        return block.reshape(seq, HEADS, HEAD_DIM).transpose(1, 0, 2)
    queries = split_heads(qkv[:, :D])
    keys = split_heads(qkv[:, D:2 * D])
    values = split_heads(qkv[:, 2 * D:])
    attended = lax.map(head_attention, (queries, keys, values))
    attended = attended.transpose(1, 0, 2).reshape(seq, D)
    attended = low(low_back(attended))
    mid = hidden + low_back(matmul(attended, w_out) + out_bias)
    normed2 = low(layer_norm(mid, gain2, shift2))
    pre_fc = low_back(matmul(normed2, w_fc) + fc_bias)
    act = low(jax.nn.gelu(pre_fc, approximate=True))
    return mid + matmul(act, w_proj) + proj_bias

def reference(hidden_in, ln1_gain, ln1_shift, w_qkv, qv_bias, w_out, out_bias, ln2_gain, ln2_shift, w_fc, fc_bias, w_proj, proj_bias, out_grad):
    inputs = [arr.astype(jnp.float32) for arr in (hidden_in, ln1_gain, ln1_shift, w_qkv, qv_bias, w_out, out_bias, ln2_gain, ln2_shift, w_fc, fc_bias, w_proj, proj_bias)]
    output, pullback = jax.vjp(forward, *inputs)
    grads = pullback(out_grad.astype(jnp.float32))
    return (output.astype(jnp.bfloat16), grads[0], grads[1], grads[2], grads[3], grads[4], grads[5], grads[6], grads[7], grads[8], grads[9], grads[10], grads[11], grads[12])
```

```python
import jax
import jax.numpy as jnp
from jax import lax
from jax.experimental import pallas as pl
from jax.experimental.pallas import tpu as pltpu
from jax.sharding import Mesh
from jax.sharding import PartitionSpec as P

D = 768
HEAD_DIM = 64
EPS = 1e-05
NEG = -1e30
LOG2E = 1.4426950408889634
F32 = jnp.float32
BF16 = jnp.bfloat16
HALF = 256
GROUPS = 32
BLOCKS = 2 * GROUPS
LOCAL = 192
VMEM_BYTES = 48 * 1024 * 1024
TEAM = ("c", "h")
SWAP = [(0, 1), (1, 0)]
MIRROR = [(i, GROUPS - 1 - i) for i in range(GROUPS)]
SMALL = (12, 12, 24, 12, 12, 12, 48, 12)


def matmul(left, right):
    return jnp.dot(left, right, preferred_element_type=F32)


def trans_left(left, right):
    return lax.dot_general(left, right, (((0,), (0,)), ((), ())), preferred_element_type=F32)


def trans_right(left, right):
    return lax.dot_general(left, right, (((1,), (1,)), ((), ())), preferred_element_type=F32)


def layer_norm(values, gain, shift):
    mean = jnp.mean(values, axis=-1, keepdims=True)
    centred = values - mean
    spread = jnp.mean(centred * centred, axis=-1, keepdims=True)
    return centred * lax.rsqrt(spread + EPS) * gain + shift


def gelu_tanh(values):
    return jax.nn.gelu(values, approximate=True)


def team_others(parts):
    return (
        lax.ppermute(parts[0], "h", SWAP),
        lax.ppermute(parts[1], "c", SWAP),
        lax.ppermute(parts[2], TEAM, [(i, 3 - i) for i in range(4)]),
    )


def team_gather(own):
    c, h = lax.axis_index("c"), lax.axis_index("h")
    by_h, by_c, by_both = team_others((own, own, own))
    near = (jnp.where(h == 0, own, by_h), jnp.where(h == 0, by_h, own))
    far = (jnp.where(h == 0, by_c, by_both), jnp.where(h == 0, by_both, by_c))
    low = [jnp.where(c == 0, a, b) for a, b in zip(near, far)]
    high = [jnp.where(c == 0, b, a) for a, b in zip(near, far)]
    return low + high


def team_scatter_sum(partial):
    rank = 2 * lax.axis_index("c") + lax.axis_index("h")
    rows = partial.shape[0] // 4

    def piece(k):
        return lax.dynamic_slice_in_dim(partial, (rank ^ k) * rows, rows, 0)

    others = team_others(tuple(piece(k).astype(BF16) for k in (1, 2, 3)))
    return piece(0) + sum(o.astype(F32) for o in others)


def block_row(b):
    return pl.multiple_of(512 * (b % GROUPS) + HALF * (b // GROUPS), HALF)


def nt(left, right):
    return lax.dot_general(left, right, (((1,), (1,)), ((), ())), preferred_element_type=F32)


def diagonal():
    key = lax.broadcasted_iota(jnp.int32, (HALF, HALF), 0)
    query = lax.broadcasted_iota(jnp.int32, (HALF, HALF), 1)
    return key <= query


def forward_kernel(g_ref, q_ref, kv_ref, att_ref, lse_ref, top, total, accum):
    g = g_ref[0]
    for slot, own in ((0, g), (1, BLOCKS - 1 - g)):
        top[...] = jnp.full_like(top, NEG)
        total[...] = jnp.zeros_like(total)
        accum[...] = jnp.zeros_like(accum)
        span = pl.ds(slot * HALF, HALF)

        def tile(b, masked):
            rows = pl.ds(block_row(b), HALF)
            first, second, third = (kv_ref[rows, pl.ds(128 * k, 128)] for k in range(3))
            second_t, third_t = second.T, third.T
            values = (second_t[64:], third_t[:64], third_t[64:])
            for h, keys in enumerate((first, first, second)):
                scores = nt(keys, q_ref[h, span, :])
                if masked:
                    scores = jnp.where(diagonal(), scores, NEG)
                line = pl.ds(h, 1)
                old = top[line, :]
                new = jnp.maximum(old, jnp.max(scores, axis=0, keepdims=True))
                weights = jnp.exp(scores - new)
                fade = jnp.exp(old - new)
                top[line, :] = new
                total[line, :] = total[line, :] * fade + jnp.sum(weights, axis=0, keepdims=True)
                accum[h] = accum[h] * fade + matmul(values[h], weights.astype(BF16))

        lax.fori_loop(0, own, lambda b, _: (tile(b, False), 0)[1], 0)
        tile(own, True)
        for h in range(3):
            line = pl.ds(h, 1)
            att_ref[slot, pl.ds(64 * h, 64), :] = accum[h] / total[line, :]
        lse_ref[:, span] = (top[...] + jnp.log(jnp.maximum(total[...], 1e-30))) * LOG2E


def query_kernel(g_ref, q_ref, do_ref, st_ref, kv_ref, dq_ref, accum):
    g = g_ref[0]
    for slot, own in ((0, g), (1, BLOCKS - 1 - g)):
        accum[...] = jnp.zeros_like(accum)
        span = pl.ds(slot * HALF, HALF)

        def tile(b, masked):
            rows = pl.ds(block_row(b), HALF)
            first, second, third = (kv_ref[rows, pl.ds(128 * k, 128)] for k in range(3))
            first_t, second_t = first.T, second.T
            keys_t = (first_t[:64], first_t[64:], second_t[:64])
            for h, (keys, values) in enumerate(
                ((first, second), (first, third), (second, third))
            ):
                scores = nt(keys, q_ref[h, span, :]) * LOG2E - st_ref[pl.ds(h, 1), span]
                if masked:
                    scores = jnp.where(diagonal(), scores, NEG)
                pull = nt(values, do_ref[h, span, :]) - st_ref[pl.ds(3 + h, 1), span]
                grad = (jnp.exp2(scores) * pull).astype(BF16)
                accum[h] += matmul(keys_t[h], grad)

        lax.fori_loop(0, own, lambda b, _: (tile(b, False), 0)[1], 0)
        tile(own, True)
        for h in range(3):
            dq_ref[slot, pl.ds(64 * h, 64), :] = accum[h] * 0.125


def key_kernel(g_ref, k_ref, v_ref, q_ref, do_ref, st_ref, dk_ref, dv_ref, acc_k, acc_v):
    g = g_ref[0]
    for slot, own in ((0, g), (1, BLOCKS - 1 - g)):
        acc_k[...] = jnp.zeros_like(acc_k)
        acc_v[...] = jnp.zeros_like(acc_v)
        span = pl.ds(slot * HALF, HALF)

        def tile(b, masked):
            rows = pl.ds(block_row(b), HALF)
            device = jnp.where(b < GROUPS, b, BLOCKS - 1 - b)
            lanes = pl.ds(pl.multiple_of((b // GROUPS) * HALF, HALF), HALF)
            stats = st_ref[device, :, lanes]
            for h in range(3):
                part, width = (pl.ds(0, 128), 128) if h < 2 else (pl.ds(128, 64), 64)
                queries, grads = q_ref[rows, part], do_ref[rows, part]
                keys, values = k_ref[h, span, :width], v_ref[h, span, :width]
                scores = nt(keys, queries) * LOG2E - stats[h : h + 1]
                if masked:
                    scores = jnp.where(diagonal(), scores, NEG)
                weights = jnp.exp2(scores)
                pull = nt(values, grads) - stats[3 + h : 4 + h]
                acc_v[h, :, :width] += matmul(weights.astype(BF16), grads)
                acc_k[h, :, :width] += matmul((weights * pull).astype(BF16), queries)

        tile(own, True)
        lax.fori_loop(own + 1, BLOCKS, lambda b, _: (tile(b, False), 0)[1], 0)
        left = lax.broadcasted_iota(jnp.int32, (HALF, 128), 1) < 64
        for out, acc in ((dk_ref, acc_k), (dv_ref, acc_v)):
            out[span, pl.ds(0, 128)] = jnp.where(left, acc[0], acc[1]).astype(BF16)
            out[span, pl.ds(128, 64)] = acc[2, :, :64].astype(BF16)


def attention_call(kernel, outs, scratch, matmuls, *args):
    tiles = 65 * 3 * HALF * HALF
    count = len(args)
    return pl.pallas_call(
        kernel,
        out_shape=outs,
        in_specs=[pl.BlockSpec(memory_space=pltpu.SMEM)]
        + [pl.BlockSpec(memory_space=pltpu.VMEM)] * (count - 1),
        out_specs=[pl.BlockSpec(memory_space=pltpu.VMEM)] * len(outs),
        scratch_shapes=scratch,
        compiler_params=pltpu.CompilerParams(vmem_limit_bytes=VMEM_BYTES),
        cost_estimate=pl.CostEstimate(
            flops=tiles * 512 * matmuls,
            bytes_accessed=sum(a.size * a.dtype.itemsize for a in args),
            transcendentals=tiles,
        ),
    )(*args)


def swap_upper(value):
    return jnp.concatenate(
        [value[:HALF], lax.ppermute(value[HALF:], "g", MIRROR)], axis=0
    )


def side(value, h, right):
    part = value[:, 64 * h : 64 * h + 64]
    blank = jnp.zeros_like(part)
    return jnp.concatenate([blank, part] if right else [part, blank], axis=1)


def sides(value, places):
    return jnp.stack([side(value, h, right) for h, right in enumerate(places)])


def one_hot(rows, columns, row_of_column):
    row = lax.broadcasted_iota(jnp.int32, (rows, columns), 0)
    column = lax.broadcasted_iota(jnp.int32, (rows, columns), 1)
    return (row == row_of_column(column)).astype(BF16)


def natural_of(column):
    g, rest = column // 24, column % 24
    return 12 * (GROUPS * (rest // 12) + g) + rest % 12


def on_device(
    hidden_in,
    ln1_gain,
    ln1_shift,
    w_qkv,
    qv_bias,
    w_out,
    out_bias,
    ln2_gain,
    ln2_shift,
    w_fc,
    fc_bias,
    w_proj,
    proj_bias,
    out_grad,
):
    c, g, h = lax.axis_index("c"), lax.axis_index("g"), lax.axis_index("h")
    rank = 2 * c + h
    where_am_i = g.astype(jnp.int32)[None]

    tokens = jnp.concatenate(team_gather(jnp.concatenate([hidden_in, out_grad], axis=1)), axis=0)
    resid, cotangent = tokens[:, :D].astype(F32), tokens[:, D:]

    reorder = one_hot(D, D, natural_of)
    pick_units = one_hot(1536, D, lambda k: 48 * (k // 24) + 24 * h + k % 24)
    small = jnp.concatenate(
        [ln1_gain, ln1_shift, qv_bias, out_bias, ln2_gain, ln2_shift, fc_bias, proj_bias]
    )
    small = jnp.pad(small.reshape(12, 12), ((0, 0), (0, 116)))
    units = matmul(jnp.concatenate([w_fc[:, :1536], w_fc[:, 1536:]], axis=0), pick_units)
    units = units.astype(BF16)

    def columns_for(of_c):
        r = 2 * of_c + h
        qkv = [lax.dynamic_slice_in_dim(w_qkv, D * k + LOCAL * r, LOCAL, 1) for k in range(3)]
        fc = lax.dynamic_slice_in_dim(units, 12 * of_c, 12, 0)
        return jnp.concatenate([*qkv, small], axis=1), jnp.concatenate([fc, w_out], axis=1)

    mine, theirs = columns_for(c), columns_for(1 - c)

    def both(own, sent):
        other = lax.ppermute(sent, "c", SWAP)
        return jnp.concatenate(
            [jnp.where(c == 0, own, other), jnp.where(c == 0, other, own)], axis=0
        )

    first = lax.all_gather(both(mine[0], theirs[0]), "g", axis=0, tiled=True)
    proj_rows = lax.dynamic_slice_in_dim(w_proj, 24 * h, 24, 0)
    second = lax.all_gather(
        jnp.concatenate([both(mine[1], theirs[1]), proj_rows], axis=1), "g", axis=0, tiled=True
    )
    w_qkv_t = matmul(reorder, first[:, : 3 * LOCAL]).astype(BF16)
    rest = matmul(reorder, second[:, : 2 * D]).astype(BF16)
    w_fc_t, w_out_all, w_proj_t = rest[:, :D], rest[:, D:], second[:, 2 * D :]

    vectors = first[:, 3 * LOCAL : 3 * LOCAL + 12].reshape(GROUPS, 2, 144).astype(F32)
    vectors = vectors.transpose(1, 0, 2)
    cut, at = [], 0
    for width in SMALL:
        cut.append(vectors[:, :, at : at + width])
        at += width
    gain_one, shift_one, bias_qv, bias_out, gain_two, shift_two = (
        v.reshape(-1) for v in cut[:6]
    )
    bias_proj = cut[7].reshape(-1)
    bias_fc = lax.dynamic_slice_in_dim(
        lax.dynamic_index_in_dim(cut[6], c, 0, False), 24 * h, 24, 1
    ).reshape(-1)
    bias_q = lax.dynamic_slice_in_dim(bias_qv, LOCAL * rank, LOCAL, 0)
    bias_v = lax.dynamic_slice_in_dim(bias_qv, D + LOCAL * rank, LOCAL, 0)
    bias_here = jnp.concatenate([bias_q, jnp.zeros_like(bias_q), bias_v])

    normed1 = layer_norm(resid, gain_one, shift_one).astype(BF16)
    qkv = (matmul(normed1, w_qkv_t) + bias_here).astype(BF16)
    queries = qkv[:, :LOCAL] * jnp.asarray(0.125, BF16)
    kv_all = lax.all_gather(qkv[:, LOCAL:], "g", axis=0, tiled=True)
    query_all = lax.all_gather(queries, "g", axis=0, tiled=True)
    query_zz = sides(swap_upper(queries), (False, True, False))
    att_t, lse = attention_call(
        forward_kernel,
        [
            jax.ShapeDtypeStruct((2, LOCAL, HALF), F32),
            jax.ShapeDtypeStruct((8, 512), F32),
        ],
        [
            pltpu.VMEM((8, HALF), F32),
            pltpu.VMEM((8, HALF), F32),
            pltpu.VMEM((3, 64, HALF), F32),
        ],
        2,
        where_am_i,
        query_zz,
        kv_all,
    )
    attended = att_t.transpose(0, 2, 1).reshape(512, LOCAL).astype(BF16)
    attended = jnp.concatenate(team_gather(swap_upper(attended)), axis=1)

    mid = resid + matmul(attended, w_out_all) + bias_out
    normed2 = layer_norm(mid, gain_two, shift_two).astype(BF16)
    pre_fc = matmul(normed2, w_fc_t) + bias_fc
    activ = gelu_tanh(pre_fc).astype(BF16)
    grad_activ = trans_right(cotangent, w_proj_t)
    grad_pre = jax.vjp(gelu_tanh, pre_fc)[1](grad_activ)[0].astype(BF16)
    grad_norm2 = team_scatter_sum(trans_right(grad_pre, w_fc_t))
    own_rows = lambda v: lax.dynamic_slice_in_dim(v, 128 * rank, 128, 0)
    mid_own = own_rows(mid)
    grad_mid_ln, grad_gain2, grad_shift2 = jax.vjp(layer_norm, mid_own, gain_two, shift_two)[1](
        grad_norm2
    )
    grad_output = out_grad.astype(F32)
    grad_mid = grad_output + grad_mid_ln
    grad_attn = grad_mid.astype(BF16)
    grad_attn_all = jnp.concatenate(team_gather(grad_attn), axis=0)
    w_out_rows = lax.dynamic_slice_in_dim(w_out_all, LOCAL * rank, LOCAL, 0)
    grad_heads = trans_right(grad_attn_all, w_out_rows).astype(BF16)
    grad_heads_all = lax.all_gather(grad_heads, "g", axis=0, tiled=True)
    grad_zz = swap_upper(grad_heads)
    grad_zz_t = grad_zz.reshape(2, HALF, LOCAL).transpose(0, 2, 1)
    delta = jnp.sum((grad_zz_t.astype(F32) * att_t).reshape(2, 3, 64, HALF), axis=2)
    delta = delta.transpose(1, 0, 2).reshape(3, 512)
    stats = jnp.concatenate([lse[:3], delta, jnp.zeros((2, 512), F32)], axis=0)
    stats_all = lax.all_gather(stats, "g", axis=0, tiled=False)

    output = mid_own + bias_proj + team_scatter_sum(matmul(activ, w_proj_t))
    hidden_out = output.astype(BF16)

    (dq_t,) = attention_call(
        query_kernel,
        [jax.ShapeDtypeStruct((2, LOCAL, HALF), F32)],
        [pltpu.VMEM((3, 64, HALF), F32)],
        3,
        where_am_i,
        query_zz,
        sides(grad_zz, (True, False, True)),
        stats,
        kv_all,
    )
    def kv_rows(b):
        return lax.dynamic_slice_in_dim(kv_all, 512 * (b % GROUPS) + HALF * (b // GROUPS), HALF, 0)

    kv_zz = jnp.concatenate([kv_rows(g), kv_rows(BLOCKS - 1 - g)], axis=0)
    dk, dv = attention_call(
        key_kernel,
        [jax.ShapeDtypeStruct((512, LOCAL), BF16)] * 2,
        [pltpu.VMEM((3, HALF, 128), F32)] * 2,
        4,
        where_am_i,
        sides(kv_zz[:, :LOCAL], (False, True, False)),
        sides(kv_zz[:, LOCAL:], (False, True, False)),
        query_all,
        grad_heads_all,
        stats_all,
    )
    grad_q = swap_upper(dq_t.transpose(0, 2, 1).reshape(512, LOCAL).astype(BF16))
    grad_kv = swap_upper(jnp.concatenate([dk, dv], axis=1))
    grad_qkv = jnp.concatenate([grad_q, grad_kv], axis=1)
    grad_norm1 = team_scatter_sum(trans_right(grad_qkv, w_qkv_t))
    resid_own = hidden_in.astype(F32)
    grad_in_ln, grad_gain1, grad_shift1 = jax.vjp(layer_norm, resid_own, gain_one, shift_one)[1](
        grad_norm1
    )
    input_grad = grad_mid + grad_in_ln

    def reordered(v):
        return matmul(v, reorder).astype(BF16)

    grad_wfc = trans_left(reordered(normed2), grad_pre)
    grad_attn_cols = lax.dynamic_slice_in_dim(grad_attn_all, LOCAL * rank, LOCAL, 1)
    grad_wout = trans_left(reordered(attended), grad_attn_cols)
    grad_wproj = trans_left(activ, cotangent)
    grad_wqkv = trans_left(reordered(normed1), grad_qkv)

    def sum_over_g(value):
        lines = value.astype(BF16).reshape(GROUPS, 24, value.shape[-1])
        lines = lax.all_to_all(lines, "g", 0, 0, tiled=True)
        return jnp.sum(lines.astype(F32), axis=0)

    late = jnp.concatenate([grad_wfc, grad_wout, grad_wproj], axis=1)
    late = sum_over_g(late)

    def spread(vector):
        return vector.reshape(2, GROUPS, -1)

    grad_qkv_sum = jnp.sum(grad_qkv.astype(F32), axis=0)
    qv_sums = jnp.zeros((2, 4, LOCAL), F32)
    qv_sums = lax.dynamic_update_slice(
        qv_sums,
        jnp.stack([grad_qkv_sum[:LOCAL], grad_qkv_sum[2 * LOCAL :]])[:, None],
        (0, rank, 0),
    ).reshape(-1)
    fc_sums = jnp.sum(grad_pre.astype(F32), axis=0).reshape(1, GROUPS, 24)
    fc_sums = lax.dynamic_update_slice(
        jnp.zeros((2, GROUPS, 48), F32), fc_sums, (c, jnp.int32(0), 24 * h)
    )
    small_sums = jnp.concatenate(
        [
            spread(grad_gain1),
            spread(grad_shift1),
            spread(qv_sums),
            spread(jnp.sum(grad_attn.astype(F32), axis=0)),
            spread(grad_gain2),
            spread(grad_shift2),
            fc_sums,
            spread(jnp.sum(grad_output, axis=0)),
        ],
        axis=2,
    )
    small_sums = small_sums.transpose(1, 0, 2).reshape(GROUPS * 24, 12)
    small_sums = jnp.pad(small_sums, ((0, 0), (0, 52)))
    early = sum_over_g(jnp.concatenate([grad_wqkv, small_sums], axis=1))

    final = jnp.concatenate([early, late], axis=1).astype(BF16)
    pieces = [p.astype(F32) for p in team_gather(final)]
    mine = [lax.dynamic_slice_in_dim(p, 12 * c, 12, 0) for p in pieces]
    total_wqkv = jnp.concatenate(
        [mine[t][:, LOCAL * k : LOCAL * (k + 1)] for k in range(3) for t in range(4)], axis=1
    )
    total_small = sum(mine)[:, 576:588].reshape(144)
    fc_pieces = jnp.stack([m[:, 640 : 640 + D] for m in mine])
    total_wfc = fc_pieces.reshape(2, 2, 12, GROUPS, 24).transpose(2, 0, 3, 1, 4).reshape(12, 3072)
    total_wout = jnp.concatenate([m[:, 640 + D : 640 + D + LOCAL] for m in mine], axis=1)
    proj_pieces = jnp.stack([p[:, 640 + D + LOCAL :] for p in pieces])
    total_wproj = lax.dynamic_slice_in_dim(proj_pieces, 2 * c, 2, 0).reshape(48, D)
    smalls, at = [], 0
    for width in SMALL:
        smalls.append(total_small[at : at + width])
        at += width
    return (
        hidden_out,
        input_grad,
        smalls[0],
        smalls[1],
        total_wqkv,
        smalls[2],
        total_wout,
        smalls[3],
        smalls[4],
        smalls[5],
        total_wfc,
        smalls[6],
        total_wproj,
        smalls[7],
    )


def solution(mesh):
    cut = Mesh(mesh.devices.reshape(2, GROUPS, 2), ("c", "g", "h"))
    tokens, rows, line = P(("c", "g", "h"), None), P(("c", "g"), None), P(("c", "g"))
    in_specs = (
        tokens, line, line, rows, line, rows, line, line, line, rows, line, rows, line, tokens,
    )
    out_specs = (
        tokens, tokens, line, line, rows, line, rows, line, line, line, rows, line, rows, line,
    )
    return jax.shard_map(
        on_device, mesh=cut, in_specs=in_specs, out_specs=out_specs, check_vma=False
    )
```

```python
import jax
import jax.numpy as jnp
from jax import lax
from jax.experimental import pallas as pl
from jax.experimental.pallas import tpu as pltpu
from jax.sharding import Mesh
from jax.sharding import PartitionSpec as P

D = 768
HEAD_DIM = 64
EPS = 1e-05
NEG = -1e30
LOG2E = 1.4426950408889634
F32 = jnp.float32
BF16 = jnp.bfloat16
HALF = 256
GROUPS = 32
TOKENS = 16384
BLOCKS = 2 * GROUPS
LOCAL = 192
VMEM_BYTES = 48 * 1024 * 1024
TEAM = ("c", "h")
SWAP = [(0, 1), (1, 0)]
MIRROR = [(i, GROUPS - 1 - i) for i in range(GROUPS)]
MESH = pl.DeviceIdType.MESH
GELU_ROOT = 0.7978845608028654
GELU_CUBE = 0.044715
SMALL = (12, 12, 24, 12, 12, 12, 48, 12)


def matmul(left, right):
    return jnp.dot(left, right, preferred_element_type=F32)


def trans_left(left, right):
    return lax.dot_general(left, right, (((0,), (0,)), ((), ())), preferred_element_type=F32)


def trans_right(left, right):
    return lax.dot_general(left, right, (((1,), (1,)), ((), ())), preferred_element_type=F32)


def layer_norm(values, gain, shift):
    mean = jnp.mean(values, axis=-1, keepdims=True)
    centred = values - mean
    spread = jnp.mean(centred * centred, axis=-1, keepdims=True)
    return centred * lax.rsqrt(spread + EPS) * gain + shift


def gelu_tanh(values):
    return jax.nn.gelu(values, approximate=True)


def team_others(parts):
    return (
        lax.ppermute(parts[0], "h", SWAP),
        lax.ppermute(parts[1], "c", SWAP),
        lax.ppermute(parts[2], TEAM, [(i, 3 - i) for i in range(4)]),
    )


def team_gather(own):
    c, h = lax.axis_index("c"), lax.axis_index("h")
    by_h, by_c, by_both = team_others((own, own, own))
    near = (jnp.where(h == 0, own, by_h), jnp.where(h == 0, by_h, own))
    far = (jnp.where(h == 0, by_c, by_both), jnp.where(h == 0, by_both, by_c))
    low = [jnp.where(c == 0, a, b) for a, b in zip(near, far)]
    high = [jnp.where(c == 0, b, a) for a, b in zip(near, far)]
    return low + high


def team_scatter_sum(partial):
    rank = 2 * lax.axis_index("c") + lax.axis_index("h")
    rows = partial.shape[0] // 4

    def piece(k):
        return lax.dynamic_slice_in_dim(partial, (rank ^ k) * rows, rows, 0)

    others = team_others(tuple(piece(k).astype(BF16) for k in (1, 2, 3)))
    return piece(0) + sum(o.astype(F32) for o in others)


def block_row(b):
    return pl.multiple_of(512 * (b % GROUPS) + HALF * (b // GROUPS), HALF)


def nt(left, right):
    return lax.dot_general(left, right, (((1,), (1,)), ((), ())), preferred_element_type=F32)


def diagonal():
    key = lax.broadcasted_iota(jnp.int32, (HALF, HALF), 0)
    query = lax.broadcasted_iota(jnp.int32, (HALF, HALF), 1)
    return key <= query


def span_loop(start, stop, width, tile):
    count = stop - start
    full = count // width
    lax.fori_loop(0, full, lambda i, _: (tile([start + width * i + k for k in range(width)], False), 0)[1], 0)
    if width > 1:
        lax.fori_loop(start + full * width, stop, lambda b, _: (tile([b], False), 0)[1], 0)

def cat(parts, axis=0):
    return parts[0] if len(parts) == 1 else jnp.concatenate(parts, axis=axis)

def query_kernel(g_ref, q_ref, do_ref, st_ref, kv_ref, dq_ref, accum, whole):
    g = g_ref[0]
    for slot, own in ((0, g), (1, BLOCKS - 1 - g)):
        accum[...] = jnp.zeros_like(accum)
        span = pl.ds(slot * HALF, HALF)

        def tile(blocks, masked):
            rows = [pl.ds(block_row(b), HALF) for b in blocks]
            first, second, third = (
                cat([kv_ref[r, pl.ds(128 * k, 128)] for r in rows]) for k in range(3)
            )
            first_t, second_t = first.T, second.T
            keys_t = (first_t[:64], first_t[64:], second_t[:64])
            raw = [
                (nt(keys, q_ref[h, span, :]), nt(values, do_ref[h, span, :]))
                for h, (keys, values) in enumerate(
                    ((first, second), (first, third), (second, third))
                )
            ]
            grads = []
            for h, (scores, pull) in enumerate(raw):
                scores = scores * LOG2E - st_ref[pl.ds(h, 1), span]
                if masked:
                    scores = jnp.where(diagonal(), scores, NEG)
                pull = pull - st_ref[pl.ds(3 + h, 1), span]
                grads.append((jnp.exp2(scores) * pull).astype(BF16))
            for h in range(3):
                accum[h] += matmul(keys_t[h], grads[h])

        span_loop(0, own, 2, tile)
        tile([own], True)
        for h in range(3):
            whole[pl.ds(64 * h, 64), :] = accum[h] * 0.125
        dq_ref[span, :] = whole[...].T.astype(BF16)


def key_kernel(g_ref, k_ref, v_ref, q_ref, do_ref, st_ref, dk_ref, dv_ref, acc_k, acc_v):
    g = g_ref[0]
    parts = ((0, 128), (0, 128), (128, 64))
    for slot, own in ((0, g), (1, BLOCKS - 1 - g)):
        acc_k[...] = jnp.zeros_like(acc_k)
        acc_v[...] = jnp.zeros_like(acc_v)
        span = pl.ds(slot * HALF, HALF)

        def tile(blocks, masked):
            rows = [pl.ds(block_row(b), HALF) for b in blocks]
            stats = cat(
                [
                    st_ref[
                        jnp.where(b < GROUPS, b, BLOCKS - 1 - b),
                        :,
                        pl.ds(pl.multiple_of((b // GROUPS) * HALF, HALF), HALF),
                    ]
                    for b in blocks
                ],
                1,
            )
            lanes = [pl.ds(at, width) for at, width in parts[1:]]
            queries = [cat([q_ref[r, p] for r in rows]) for p in lanes]
            grads = [cat([do_ref[r, p] for r in rows]) for p in lanes]
            queries, grads = [queries[0]] + queries, [grads[0]] + grads
            raw = [
                (nt(k_ref[h, span, :width], queries[h]), nt(v_ref[h, span, :width], grads[h]))
                for h, (_, width) in enumerate(parts)
            ]
            ready = []
            for h, (scores, pull) in enumerate(raw):
                scores = scores * LOG2E - stats[h : h + 1]
                if masked:
                    scores = jnp.where(diagonal(), scores, NEG)
                weights = jnp.exp2(scores)
                pull = weights * (pull - stats[3 + h : 4 + h])
                ready.append((weights.astype(BF16), pull.astype(BF16)))
            for h, (weights, pull) in enumerate(ready):
                width = parts[h][1]
                acc_v[h, :, :width] += matmul(weights, grads[h])
                acc_k[h, :, :width] += matmul(pull, queries[h])

        tile([own], True)
        span_loop(own + 1, BLOCKS, 4, tile)
        left = lax.broadcasted_iota(jnp.int32, (HALF, 128), 1) < 64
        for out, acc in ((dk_ref, acc_k), (dv_ref, acc_v)):
            out[span, pl.ds(0, 128)] = jnp.where(left, acc[0], acc[1]).astype(BF16)
            out[span, pl.ds(128, 64)] = acc[2, :, :64].astype(BF16)


def attention_call(kernel, outs, scratch, matmuls, *args):
    tiles = 65 * 3 * HALF * HALF
    count = len(args)
    return pl.pallas_call(
        kernel,
        out_shape=outs,
        in_specs=[pl.BlockSpec(memory_space=pltpu.SMEM)]
        + [pl.BlockSpec(memory_space=pltpu.VMEM)] * (count - 1),
        out_specs=[pl.BlockSpec(memory_space=pltpu.VMEM)] * len(outs),
        scratch_shapes=scratch,
        compiler_params=pltpu.CompilerParams(vmem_limit_bytes=VMEM_BYTES),
        cost_estimate=pl.CostEstimate(
            flops=tiles * 512 * matmuls,
            bytes_accessed=sum(a.size * a.dtype.itemsize for a in args),
            transcendentals=tiles,
        ),
    )(*args)


def swap_upper(value):
    return jnp.concatenate(
        [value[:HALF], lax.ppermute(value[HALF:], "g", MIRROR)], axis=0
    )


def side(value, h, right):
    part = value[:, 64 * h : 64 * h + 64]
    blank = jnp.zeros_like(part)
    return jnp.concatenate([blank, part] if right else [part, blank], axis=1)


def sides(value, places):
    return jnp.stack([side(value, h, right) for h, right in enumerate(places)])


def one_hot(rows, columns, row_of_column):
    row = lax.broadcasted_iota(jnp.int32, (rows, columns), 0)
    column = lax.broadcasted_iota(jnp.int32, (rows, columns), 1)
    return (row == row_of_column(column)).astype(BF16)


def natural_of(column):
    g, rest = column // 24, column % 24
    return 12 * (GROUPS * (rest // 12) + g) + rest % 12


def team_peer(c, h, k):
    return lax.rem(c + k // 2, 2), lax.rem(h + k % 2, 2)


def greet(devices):
    barrier = pltpu.get_barrier_semaphore()
    for device in devices:
        pl.semaphore_signal(barrier, inc=1, device_id=device, device_id_type=MESH)
    pl.semaphore_wait(barrier, len(devices))


def send(src, dst, sems, slot, device):
    copy = pltpu.make_async_remote_copy(
        src_ref=src,
        dst_ref=dst,
        send_sem=sems.at[0, slot],
        recv_sem=sems.at[1, slot],
        device_id=device,
        device_id_type=MESH,
    )
    copy.start()
    return copy


def middle_kernel(
    att_ref,
    hid_ref,
    cot_ref,
    w_out_ref,
    rows_ref,
    w_fc_ref,
    w_fc_t_ref,
    w_proj_ref,
    w_proj_t_ref,
    vec_ref,
    hidden_ref,
    grad_mid_ref,
    grad_attn_ref,
    grad_pre_ref,
    normed_ref,
    activ_ref,
    attended_ref,
    grad_ref,
    upper_ref,
    norm_ref,
    att,
    mid,
    grad_activ,
    whole_out,
    norm_out,
    norm_in,
    out_out,
    out_in,
    attn,
    upper,
    att_sems,
    norm_sems,
    out_sems,
    attn_sems,
    upper_sems,
):
    c, g, h = lax.axis_index("c"), lax.axis_index("g"), lax.axis_index("h")
    rank = 2 * c + h
    mirror = GROUPS - 1 - g
    peers = [team_peer(c, h, k) for k in range(4)]
    team = [(pc, g, ph) for pc, ph in peers[1:]]
    across = [(pc, mirror, ph) for pc, ph in peers]
    greet(team + across)

    low, high = pl.ds(0, HALF), pl.ds(HALF, HALF)
    copies = [
        send(att_ref.at[low], att.at[rank, low], att_sems, k, device)
        for k, device in enumerate(team)
    ]
    copies += [
        send(att_ref.at[high], att.at[rank, high], att_sems, 3 + k, device)
        for k, device in enumerate(across)
    ]
    att[rank, low, :] = att_ref[low, :]

    cotangent = cot_ref[...]
    thirds = [pl.ds(256 * k, 256) for k in range(3)]
    for part in thirds:
        grad_activ[:, part] = matmul(cotangent, w_proj_t_ref[:, part])
    for copy in copies:
        copy.wait_recv()

    bias_out, gain, shift, bias_fc, bias_proj = (vec_ref[k : k + 1, :] for k in range(5))

    total = hid_ref[...].astype(F32) + bias_out
    for t in range(4):
        total += matmul(att[t], w_out_ref[pl.ds(LOCAL * t, LOCAL), :])
    mid[...] = total
    normed_ref[...] = layer_norm(total, gain, shift).astype(BF16)
    normed = normed_ref[...]
    for part in thirds:
        pre = matmul(normed, w_fc_ref[:, part]) + bias_fc[:, part.start : part.start + 256]
        square = pre * pre
        bend = jnp.tanh(GELU_ROOT * pre * (1.0 + GELU_CUBE * square))
        activ_ref[:, part] = (0.5 * pre * (1.0 + bend)).astype(BF16)
        slope = 0.5 * (1.0 + bend) + 0.5 * pre * (1.0 - bend * bend) * GELU_ROOT * (
            1.0 + 3.0 * GELU_CUBE * square
        )
        grad_pre_ref[:, part] = (grad_activ[:, part] * slope).astype(BF16)

    def spread_out(left, right_ref, whole, out, into, sems):
        left = left[...]
        for part in thirds:
            whole[:, part] = matmul(left, right_ref[:, part])
        copies = []
        for k, (pc, ph) in enumerate(peers):
            if k:
                rows = pl.ds(pl.multiple_of(128 * (2 * pc + ph), 128), 128)
                out[k] = whole[rows, :].astype(BF16)
                copies.append(send(out.at[k], into.at[k], sems, k, team[k - 1]))
        return copies

    norm_copies = spread_out(grad_pre_ref, w_fc_t_ref, grad_activ, norm_out, norm_in, norm_sems)
    out_copies = spread_out(activ_ref, w_proj_ref, whole_out, out_out, out_in, out_sems)
    own = pl.ds(pl.multiple_of(128 * rank, 128), 128)
    for copy in norm_copies:
        copy.wait_recv()
    grad_norm = grad_activ[own, :]
    for k in (1, 2, 3):
        grad_norm += norm_in[k].astype(F32)
    own_mid = mid[own, :]
    centred = own_mid - jnp.mean(own_mid, axis=-1, keepdims=True)
    scale = lax.rsqrt(jnp.mean(centred * centred, axis=-1, keepdims=True) + EPS)
    hat = centred * scale
    pull = grad_norm * gain
    pull = pull - jnp.mean(pull, axis=-1, keepdims=True)
    pull = pull - hat * jnp.mean(pull * hat, axis=-1, keepdims=True)
    grad_mid = cot_ref[own, :].astype(F32) + scale * pull
    grad_mid_ref[...] = grad_mid
    attn[rank] = grad_mid.astype(BF16)
    attn_copies = [
        send(attn.at[rank], attn.at[rank], attn_sems, k, device) for k, device in enumerate(team)
    ]
    norm_ref[...] = jnp.zeros_like(norm_ref)
    norm_ref[0:1, :] = jnp.sum(grad_norm * hat, axis=0, keepdims=True)
    norm_ref[1:2, :] = jnp.sum(grad_norm, axis=0, keepdims=True)
    for copy in out_copies:
        copy.wait_recv()
    output = own_mid + bias_proj + whole_out[own, :]
    for k in (1, 2, 3):
        output += out_in[k].astype(F32)
    hidden_ref[...] = output.astype(BF16)
    for t in range(4):
        attended_ref[t] = att[t]
    for copy in attn_copies:
        copy.wait_recv()
    for t in (2, 3, 0, 1):
        rows = pl.ds(128 * t, 128)
        block = attn[t]
        grad_attn_ref[rows, :] = block
        grad_ref[rows, :] = trans_right(block, rows_ref[...]).astype(BF16)
        if t == 3:
            upper_copy = send(
                grad_ref.at[high], upper, upper_sems, 0, (c, mirror, h)
            )
    upper_copy.wait_recv()
    upper_ref[...] = upper[...]
    for copy in copies + norm_copies + out_copies + attn_copies + [upper_copy]:
        copy.wait_send()


def middle(*args):
    def out(shape, dtype):
        return jax.ShapeDtypeStruct(shape, dtype)

    vmem = pl.BlockSpec(memory_space=pltpu.VMEM)
    outs = [
        out((128, D), BF16),
        out((128, D), F32),
        out((512, D), BF16),
        out((512, D), BF16),
        out((512, D), BF16),
        out((512, D), BF16),
        out((4, 512, LOCAL), BF16),
        out((512, LOCAL), BF16),
        out((HALF, LOCAL), BF16),
        out((8, D), F32),
    ]
    return pl.pallas_call(
        middle_kernel,
        out_shape=outs,
        in_specs=[vmem] * len(args),
        out_specs=[vmem] * len(outs),
        scratch_shapes=[
            pltpu.VMEM((4, 512, LOCAL), BF16),
            pltpu.VMEM((512, D), F32),
            pltpu.VMEM((512, D), F32),
            pltpu.VMEM((512, D), F32),
            pltpu.VMEM((4, 128, D), BF16),
            pltpu.VMEM((4, 128, D), BF16),
            pltpu.VMEM((4, 128, D), BF16),
            pltpu.VMEM((4, 128, D), BF16),
            pltpu.VMEM((4, 128, D), BF16),
            pltpu.VMEM((HALF, LOCAL), BF16),
            pltpu.SemaphoreType.DMA((2, 7)),
            pltpu.SemaphoreType.DMA((2, 4)),
            pltpu.SemaphoreType.DMA((2, 4)),
            pltpu.SemaphoreType.DMA((2, 3)),
            pltpu.SemaphoreType.DMA((2, 1)),
        ],
        compiler_params=pltpu.CompilerParams(
            vmem_limit_bytes=VMEM_BYTES, collective_id=1, has_side_effects=True
        ),
        cost_estimate=pl.CostEstimate(
            flops=9 * 512 * D * D, bytes_accessed=16 * 512 * D, transcendentals=512 * D
        ),
    )(*args)


def wrap(value, size):
    return lax.rem(value + size, size)


class Plane:
    def __init__(self, c, g, h):
        self.c, self.g, self.h = c, g, h
        self.y, self.z, self.core = g // 8, (g // 2) % 4, g % 2

    def place(self, first, second, core):
        dz = first * (1 - core) + second * core
        dy = first * core + second * (1 - core)
        return 8 * wrap(self.y + dy, 4) + 2 * wrap(self.z + dz, 4) + core

    def device(self, first, second):
        return (self.c, self.place(first, second, self.core), self.h)

    def sibling(self):
        return (self.c, self.g + 1 - 2 * self.core, self.h)


def shift_of(index):
    return ((index + 1) % 3 + 1) * jnp.minimum(index, 1)


def travel(plane, held, near_sems, pair_sems):
    def halves():
        return (pl.ds(0, HALF), pl.ds(HALF, HALF))

    def source(d, e, core):
        return plane.place(shift_of(d), shift_of(e), core)

    def copy(n, half, slot, first, second):
        rows = halves()[half]
        return pltpu.make_async_remote_copy(
            src_ref=held.at[slot, rows],
            dst_ref=held.at[slot, rows],
            send_sem=near_sems.at[0, half, n],
            recv_sem=near_sems.at[1, half, n],
            device_id=plane.device(first, second),
            device_id_type=MESH,
        )

    def across(n, slot):
        return pltpu.make_async_remote_copy(
            src_ref=held.at[slot],
            dst_ref=held.at[slot],
            send_sem=pair_sems.at[0, n],
            recv_sem=pair_sems.at[1, n],
            device_id=plane.sibling(),
            device_id_type=MESH,
        )

    def each(n, act):
        d, e = n % 4, n // 4
        slot = source(d, e, plane.core)
        act(across(n, slot))

        @pl.when(n == 0)
        def _():
            for half in (0, 1):
                act(copy(1, half, slot, 1, 0))
                act(copy(2, half, slot, 3, 0))

        @pl.when(n == 1)
        def _():
            act(copy(3, 0, slot, 1, 0))

        @pl.when(n == 2)
        def _():
            act(copy(3, 1, slot, 3, 0))

        @pl.when(e == 0)
        def _():
            for half in (0, 1):
                act(copy(4 + d, half, slot, 0, 1))
                act(copy(8 + d, half, slot, 0, 3))

        @pl.when(e == 1)
        def _():
            act(copy(12 + d, 0, slot, 0, 1))

        @pl.when(e == 2)
        def _():
            act(copy(12 + d, 1, slot, 0, 3))

    def depart(n):
        each(n, lambda c: c.start())

    def arrive(n):
        for half in (0, 1):
            copy(n, half, source(n % 4, n // 4, plane.core), 0, 1).wait_recv()
        depart(n)

    def arrive_across(n):
        across(n, source(n % 4, n // 4, 1 - plane.core)).wait_recv()

    def finish():
        def sent(n, carry):
            each(n, lambda c: c.wait_send())
            return carry

        lax.fori_loop(0, 16, sent, 0)

    def place_of(n, other):
        return source(n % 4, n // 4, plane.core + other - 2 * plane.core * other)

    return depart, arrive, arrive_across, place_of, finish


def fused_forward_kernel(
    q_ref, kv_ref, att_ref, nat_ref, lse_ref, all_ref, held, qz, upper, top, total, accum,
    near_sems, pair_sems, upper_sems, out_sems,
):
    c, g, h = lax.axis_index("c"), lax.axis_index("g"), lax.axis_index("h")
    plane = Plane(c, g, h)
    mirror = (c, GROUPS - 1 - g, h)
    greet(
        [plane.sibling(), plane.device(1, 0), plane.device(3, 0)]
        + [plane.device(0, 1), plane.device(0, 3), mirror]
    )
    swap = send(q_ref.at[pl.ds(HALF, HALF)], upper, upper_sems, 0, mirror)
    held[g] = kv_ref[...]
    depart, arrive, arrive_across, place_of, finish = travel(plane, held, near_sems, pair_sems)
    top[...] = jnp.full_like(top, NEG)
    total[...] = jnp.zeros_like(total)
    accum[...] = jnp.zeros_like(accum)
    left = lax.broadcasted_iota(jnp.int32, (HALF, 128), 1) < 64

    def place_queries(slot, block):
        span = pl.ds(slot * HALF, HALF)
        pair = block[:, :128].astype(F32)
        qz[0, span, :] = jnp.where(left, pair, 0.0).astype(BF16)
        qz[1, span, :] = jnp.where(left, 0.0, pair).astype(BF16)
        qz[2, span, :] = jnp.concatenate(
            [block[:, 128:], jnp.zeros((HALF, 64), BF16)], axis=1
        )

    place_queries(0, q_ref[pl.ds(0, HALF), :])

    def tiles(device, units):
        chains = []
        for slot, halves, masked in units:
            rows = pl.ds(halves[0] * HALF, len(halves) * HALF)
            span = pl.ds(slot * HALF, HALF)
            first, second, third = (held[device, rows, pl.ds(128 * k, 128)] for k in range(3))
            second_t, third_t = second.T, third.T
            values = (second_t[64:], third_t[:64], third_t[64:])
            for n, keys in enumerate((first, first, second)):
                scores = nt(keys, qz[n, span, :])
                if masked:
                    scores = jnp.where(diagonal(), scores, NEG)
                chains.append((slot, n, values[n], scores))
        ready = []
        for slot, n, value, scores in chains:
            line = pl.ds(8 * slot + n, 1)
            old = top[line, :]
            new = jnp.maximum(old, jnp.max(scores, axis=0, keepdims=True))
            weights = jnp.exp(scores - new)
            fade = jnp.exp(old - new)
            top[line, :] = new
            total[line, :] = total[line, :] * fade + jnp.sum(weights, axis=0, keepdims=True)
            ready.append((slot, n, value, weights.astype(BF16), fade))
        for slot, n, value, weights, fade in ready:
            accum[slot, n] = accum[slot, n] * fade + matmul(value, weights)

    def keep(slot):
        return pltpu.make_async_copy(held.at[slot], all_ref.at[slot], out_sems.at[slot])

    def work(device):
        keep(device).start()

        low, high = device < g, device < GROUPS - 1 - g

        @pl.when(low & high)
        def _():
            tiles(device, [(0, (0,), False), (1, (0, 1), False)])

        @pl.when(low & ~high)
        def _():
            tiles(device, [(0, (0,), False), (1, (0,), False)])

        @pl.when(~low & high)
        def _():
            tiles(device, [(1, (0, 1), False)])

        @pl.when(~low & ~high)
        def _():
            tiles(device, [(1, (0,), False)])

        @pl.when(device == g)
        def _():
            tiles(device, [(0, (0,), True)])

        @pl.when(device == GROUPS - 1 - g)
        def _():
            tiles(device, [(1, (1,), True)])

    lax.fori_loop(0, 1, lambda n, carry: (depart(n), carry)[1], 0)
    swap.wait_recv()
    place_queries(1, upper[...])

    def step(m, carry):
        n, other = m // 2, m % 2

        @pl.when((other == 0) & (n > 0))
        def _():
            arrive(n)

        @pl.when(other == 1)
        def _():
            arrive_across(n)

        work(place_of(n, other))
        return carry

    lax.fori_loop(0, 32, step, 0)
    for slot in range(2):
        for n in range(3):
            line = pl.ds(8 * slot + n, 1)
            att_ref[slot, pl.ds(64 * n, 64), :] = accum[slot, n] / total[line, :]
        span = pl.ds(slot * HALF, HALF)
        nat_ref[span, :] = att_ref[slot].T.astype(BF16)
        lines = pl.ds(8 * slot, 8)
        lse_ref[:, span] = (top[lines, :] + jnp.log(jnp.maximum(total[lines, :], 1e-30))) * LOG2E
    swap.wait_send()
    finish()
    for slot in range(GROUPS):
        keep(slot).wait()


def fused_forward(queries, kv):
    vmem = pl.BlockSpec(memory_space=pltpu.VMEM)
    return pl.pallas_call(
        fused_forward_kernel,
        out_shape=[
            jax.ShapeDtypeStruct((2, LOCAL, HALF), F32),
            jax.ShapeDtypeStruct((512, LOCAL), BF16),
            jax.ShapeDtypeStruct((8, 512), F32),
            jax.ShapeDtypeStruct((GROUPS, 512, 2 * LOCAL), BF16),
        ],
        in_specs=[vmem, vmem],
        out_specs=[vmem, vmem, vmem, pl.BlockSpec(memory_space=pl.ANY)],
        scratch_shapes=[
            pltpu.VMEM((GROUPS, 512, 2 * LOCAL), BF16),
            pltpu.VMEM((3, 512, 128), BF16),
            pltpu.VMEM((HALF, LOCAL), BF16),
            pltpu.VMEM((16, HALF), F32),
            pltpu.VMEM((16, HALF), F32),
            pltpu.VMEM((2, 3, 64, HALF), F32),
            pltpu.SemaphoreType.DMA((2, 2, 16)),
            pltpu.SemaphoreType.DMA((2, 16)),
            pltpu.SemaphoreType.DMA((2, 1)),
            pltpu.SemaphoreType.DMA((GROUPS,)),
        ],
        compiler_params=pltpu.CompilerParams(
            vmem_limit_bytes=VMEM_BYTES, collective_id=2, has_side_effects=True
        ),
        cost_estimate=pl.CostEstimate(
            flops=65 * 3 * HALF * HALF * 1024, bytes_accessed=32 << 20, transcendentals=65 * 3 * HALF * HALF
        ),
    )(queries, kv)


def on_device(
    hidden_in,
    ln1_gain,
    ln1_shift,
    w_qkv,
    qv_bias,
    w_out,
    out_bias,
    ln2_gain,
    ln2_shift,
    w_fc,
    fc_bias,
    w_proj,
    proj_bias,
    out_grad,
):
    c, g, h = lax.axis_index("c"), lax.axis_index("g"), lax.axis_index("h")
    rank = 2 * c + h
    where_am_i = g.astype(jnp.int32)[None]

    tokens = jnp.concatenate(team_gather(hidden_in), axis=0)
    resid = tokens.astype(F32)
    cotangent = jnp.concatenate(team_gather(out_grad), axis=0)

    reorder = one_hot(D, D, natural_of)
    pick_units = one_hot(1536, D, lambda k: 48 * (k // 24) + 24 * h + k % 24)
    small = jnp.concatenate(
        [ln1_gain, ln1_shift, qv_bias, out_bias, ln2_gain, ln2_shift, fc_bias, proj_bias]
    )
    small = jnp.pad(small.reshape(12, 12), ((0, 0), (0, 116)))
    units = matmul(jnp.concatenate([w_fc[:, :1536], w_fc[:, 1536:]], axis=0), pick_units)
    units = units.astype(BF16)

    def columns_for(of_c):
        r = 2 * of_c + h
        qkv = [lax.dynamic_slice_in_dim(w_qkv, D * k + LOCAL * r, LOCAL, 1) for k in range(3)]
        fc = lax.dynamic_slice_in_dim(units, 12 * of_c, 12, 0)
        return jnp.concatenate([*qkv, small], axis=1), jnp.concatenate([fc, w_out], axis=1)

    mine, theirs = columns_for(c), columns_for(1 - c)

    def both(own, sent):
        other = lax.ppermute(sent, "c", SWAP)
        return jnp.concatenate(
            [jnp.where(c == 0, own, other), jnp.where(c == 0, other, own)], axis=0
        )

    first = lax.all_gather(both(mine[0], theirs[0]), "g", axis=0, tiled=True)
    proj_rows = lax.dynamic_slice_in_dim(w_proj, 24 * h, 24, 0)
    second = lax.all_gather(
        jnp.concatenate([both(mine[1], theirs[1]), proj_rows], axis=1), "g", axis=0, tiled=True
    )
    w_qkv_t = matmul(reorder, first[:, : 3 * LOCAL]).astype(BF16)
    rest = matmul(reorder, second[:, : 2 * D]).astype(BF16)
    w_fc_t, w_out_all, w_proj_t = rest[:, :D], rest[:, D:], second[:, 2 * D :]

    vectors = first[:, 3 * LOCAL : 3 * LOCAL + 12].reshape(GROUPS, 2, 144).astype(F32)
    vectors = vectors.transpose(1, 0, 2)
    cut, at = [], 0
    for width in SMALL:
        cut.append(vectors[:, :, at : at + width])
        at += width
    gain_one, shift_one, bias_qv, bias_out, gain_two, shift_two = (
        v.reshape(-1) for v in cut[:6]
    )
    bias_proj = cut[7].reshape(-1)
    bias_fc = lax.dynamic_slice_in_dim(
        lax.dynamic_index_in_dim(cut[6], c, 0, False), 24 * h, 24, 1
    ).reshape(-1)
    bias_q = lax.dynamic_slice_in_dim(bias_qv, LOCAL * rank, LOCAL, 0)
    bias_v = lax.dynamic_slice_in_dim(bias_qv, D + LOCAL * rank, LOCAL, 0)
    bias_here = jnp.concatenate([bias_q, jnp.zeros_like(bias_q), bias_v])

    normed1 = layer_norm(resid, gain_one, shift_one).astype(BF16)
    qkv = (matmul(normed1, w_qkv_t) + bias_here).astype(BF16)
    queries = qkv[:, :LOCAL] * jnp.asarray(0.125, BF16)
    query_all = lax.all_gather(queries, "g", axis=0, tiled=True)
    att_t, attended_zz, lse, kv_all = fused_forward(queries, qkv[:, LOCAL:])
    kv_all = kv_all.reshape(TOKENS, 2 * LOCAL)
    query_zz = sides(swap_upper(queries), (False, True, False))
    w_out_rows = lax.dynamic_slice_in_dim(w_out_all, LOCAL * rank, LOCAL, 0)
    vec = jnp.stack([bias_out, gain_two, shift_two, bias_fc, bias_proj])
    (
        hidden_out,
        grad_mid,
        grad_attn_all,
        grad_pre,
        normed2,
        activ,
        attended,
        grad_heads,
        grad_upper,
        norm_sums,
    ) = middle(
        attended_zz,
        tokens,
        cotangent,
        w_out_all,
        w_out_rows,
        w_fc_t,
        w_fc_t.T,
        w_proj_t,
        w_proj_t.T,
        jnp.concatenate([vec, jnp.zeros((3, D), F32)], axis=0),
    )
    attended = jnp.concatenate([attended[t] for t in range(4)], axis=1)
    grad_gain2, grad_shift2 = norm_sums[0], norm_sums[1]
    grad_attn = lax.dynamic_slice_in_dim(grad_attn_all, 128 * rank, 128, 0)
    grad_output = out_grad.astype(F32)
    grad_heads_all = lax.all_gather(grad_heads, "g", axis=0, tiled=True)
    grad_zz = jnp.concatenate([grad_heads[:HALF], grad_upper], axis=0)
    grad_zz_t = grad_zz.reshape(2, HALF, LOCAL).transpose(0, 2, 1)
    delta = jnp.sum((grad_zz_t.astype(F32) * att_t).reshape(2, 3, 64, HALF), axis=2)
    delta = delta.transpose(1, 0, 2).reshape(3, 512)
    stats = jnp.concatenate([lse[:3], delta, jnp.zeros((2, 512), F32)], axis=0)
    stats_all = lax.all_to_all(
        jnp.broadcast_to(stats[None], (GROUPS, 8, 512)), "g", 0, 0, tiled=True
    )

    (dq,) = attention_call(
        query_kernel,
        [jax.ShapeDtypeStruct((512, LOCAL), BF16)],
        [pltpu.VMEM((3, 64, HALF), F32), pltpu.VMEM((LOCAL, HALF), F32)],
        3,
        where_am_i,
        query_zz,
        sides(grad_zz, (True, False, True)),
        stats,
        kv_all,
    )
    def kv_rows(b):
        return lax.dynamic_slice_in_dim(kv_all, 512 * (b % GROUPS) + HALF * (b // GROUPS), HALF, 0)

    kv_zz = jnp.concatenate([kv_rows(g), kv_rows(BLOCKS - 1 - g)], axis=0)
    dk, dv = attention_call(
        key_kernel,
        [jax.ShapeDtypeStruct((512, LOCAL), BF16)] * 2,
        [pltpu.VMEM((3, HALF, 128), F32)] * 2,
        4,
        where_am_i,
        sides(kv_zz[:, :LOCAL], (False, True, False)),
        sides(kv_zz[:, LOCAL:], (False, True, False)),
        query_all,
        grad_heads_all,
        stats_all,
    )
    grad_q = swap_upper(dq)
    grad_kv = swap_upper(jnp.concatenate([dk, dv], axis=1))
    grad_qkv = jnp.concatenate([grad_q, grad_kv], axis=1)
    grad_norm1 = team_scatter_sum(trans_right(grad_qkv, w_qkv_t))
    resid_own = hidden_in.astype(F32)
    grad_in_ln, grad_gain1, grad_shift1 = jax.vjp(layer_norm, resid_own, gain_one, shift_one)[1](
        grad_norm1
    )
    input_grad = grad_mid + grad_in_ln

    def reordered(v):
        return matmul(v, reorder).astype(BF16)

    grad_wfc = trans_left(reordered(normed2), grad_pre)
    grad_attn_cols = lax.dynamic_slice_in_dim(grad_attn_all, LOCAL * rank, LOCAL, 1)
    grad_wout = trans_left(reordered(attended), grad_attn_cols)
    grad_wproj = trans_left(activ, cotangent)
    grad_wqkv = trans_left(reordered(normed1), grad_qkv)

    def sum_over_g(value):
        lines = value.astype(BF16).reshape(GROUPS, 24, value.shape[-1])
        lines = lax.all_to_all(lines, "g", 0, 0, tiled=True)
        return jnp.sum(lines.astype(F32), axis=0)

    late = jnp.concatenate([grad_wfc, grad_wout, grad_wproj], axis=1)
    late = sum_over_g(late)

    def spread(vector):
        return vector.reshape(2, GROUPS, -1)

    grad_qkv_sum = jnp.sum(grad_qkv.astype(F32), axis=0)
    qv_sums = jnp.zeros((2, 4, LOCAL), F32)
    qv_sums = lax.dynamic_update_slice(
        qv_sums,
        jnp.stack([grad_qkv_sum[:LOCAL], grad_qkv_sum[2 * LOCAL :]])[:, None],
        (0, rank, 0),
    ).reshape(-1)
    fc_sums = jnp.sum(grad_pre.astype(F32), axis=0).reshape(1, GROUPS, 24)
    fc_sums = lax.dynamic_update_slice(
        jnp.zeros((2, GROUPS, 48), F32), fc_sums, (c, jnp.int32(0), 24 * h)
    )
    small_sums = jnp.concatenate(
        [
            spread(grad_gain1),
            spread(grad_shift1),
            spread(qv_sums),
            spread(jnp.sum(grad_attn.astype(F32), axis=0)),
            spread(grad_gain2),
            spread(grad_shift2),
            fc_sums,
            spread(jnp.sum(grad_output, axis=0)),
        ],
        axis=2,
    )
    small_sums = small_sums.transpose(1, 0, 2).reshape(GROUPS * 24, 12)
    small_sums = jnp.pad(small_sums, ((0, 0), (0, 52)))
    early = sum_over_g(jnp.concatenate([grad_wqkv, small_sums], axis=1))

    final = jnp.concatenate([early, late], axis=1).astype(BF16)
    pieces = [p.astype(F32) for p in team_gather(final)]
    mine = [lax.dynamic_slice_in_dim(p, 12 * c, 12, 0) for p in pieces]
    total_wqkv = jnp.concatenate(
        [mine[t][:, LOCAL * k : LOCAL * (k + 1)] for k in range(3) for t in range(4)], axis=1
    )
    total_small = sum(mine)[:, 576:588].reshape(144)
    fc_pieces = jnp.stack([m[:, 640 : 640 + D] for m in mine])
    total_wfc = fc_pieces.reshape(2, 2, 12, GROUPS, 24).transpose(2, 0, 3, 1, 4).reshape(12, 3072)
    total_wout = jnp.concatenate([m[:, 640 + D : 640 + D + LOCAL] for m in mine], axis=1)
    proj_pieces = jnp.stack([p[:, 640 + D + LOCAL :] for p in pieces])
    total_wproj = lax.dynamic_slice_in_dim(proj_pieces, 2 * c, 2, 0).reshape(48, D)
    smalls, at = [], 0
    for width in SMALL:
        smalls.append(total_small[at : at + width])
        at += width
    return (
        hidden_out,
        input_grad,
        smalls[0],
        smalls[1],
        total_wqkv,
        smalls[2],
        total_wout,
        smalls[3],
        smalls[4],
        smalls[5],
        total_wfc,
        smalls[6],
        total_wproj,
        smalls[7],
    )


def solution(mesh):
    cut = Mesh(mesh.devices.reshape(2, GROUPS, 2), ("c", "g", "h"))
    tokens, rows, line = P(("c", "g", "h"), None), P(("c", "g"), None), P(("c", "g"))
    in_specs = (
        tokens, line, line, rows, line, rows, line, line, line, rows, line, rows, line, tokens,
    )
    out_specs = (
        tokens, tokens, line, line, rows, line, rows, line, line, line, rows, line, rows, line,
    )
    return jax.shard_map(
        on_device, mesh=cut, in_specs=in_specs, out_specs=out_specs, check_vma=False
    )
```

```python
import jax
import jax.numpy as jnp
from jax import lax
from jax.experimental import pallas as pl
from jax.experimental.pallas import tpu as pltpu
from jax.sharding import Mesh
from jax.sharding import PartitionSpec as P

D = 768
HEAD_DIM = 64
EPS = 1e-05
NEG = -1e30
LOG2E = 1.4426950408889634
F32 = jnp.float32
BF16 = jnp.bfloat16
HALF = 256
TALL = HALF + 32
CARGO = HALF + 96
GROUPS = 32
TOKENS = 16384
BLOCKS = 2 * GROUPS
LOCAL = 192
VMEM_BYTES = 48 * 1024 * 1024
TEAM = ("c", "h")
SWAP = [(0, 1), (1, 0)]
MIRROR = [(i, GROUPS - 1 - i) for i in range(GROUPS)]
MESH = pl.DeviceIdType.MESH
GELU_ROOT = 0.7978845608028654
GELU_CUBE = 0.044715
SMALL = (12, 12, 24, 12, 12, 12, 48, 12)


def matmul(left, right):
    return jnp.dot(left, right, preferred_element_type=F32)


def trans_left(left, right):
    return lax.dot_general(left, right, (((0,), (0,)), ((), ())), preferred_element_type=F32)


def trans_left_of(left, right):
    return lax.dot_general(left, right, (((0,), (1,)), ((), ())), preferred_element_type=F32)


def trans_right(left, right):
    return lax.dot_general(left, right, (((1,), (1,)), ((), ())), preferred_element_type=F32)


def layer_norm(values, gain, shift):
    mean = jnp.mean(values, axis=-1, keepdims=True)
    centred = values - mean
    spread = jnp.mean(centred * centred, axis=-1, keepdims=True)
    return centred * lax.rsqrt(spread + EPS) * gain + shift


def gelu_tanh(values):
    return jax.nn.gelu(values, approximate=True)


def team_others(parts):
    return (
        lax.ppermute(parts[0], "h", SWAP),
        lax.ppermute(parts[1], "c", SWAP),
        lax.ppermute(parts[2], TEAM, [(i, 3 - i) for i in range(4)]),
    )


def team_gather(own):
    c, h = lax.axis_index("c"), lax.axis_index("h")
    by_h, by_c, by_both = team_others((own, own, own))
    near = (jnp.where(h == 0, own, by_h), jnp.where(h == 0, by_h, own))
    far = (jnp.where(h == 0, by_c, by_both), jnp.where(h == 0, by_both, by_c))
    low = [jnp.where(c == 0, a, b) for a, b in zip(near, far)]
    high = [jnp.where(c == 0, b, a) for a, b in zip(near, far)]
    return low + high


def team_scatter_sum(partial):
    rank = 2 * lax.axis_index("c") + lax.axis_index("h")
    rows = partial.shape[0] // 4

    def piece(k):
        return lax.dynamic_slice_in_dim(partial, (rank ^ k) * rows, rows, 0)

    others = team_others(tuple(piece(k).astype(BF16) for k in (1, 2, 3)))
    return piece(0) + sum(o.astype(F32) for o in others)


def nt(left, right):
    return lax.dot_general(left, right, (((1,), (1,)), ((), ())), preferred_element_type=F32)


def diagonal():
    key = lax.broadcasted_iota(jnp.int32, (HALF, HALF), 0)
    query = lax.broadcasted_iota(jnp.int32, (HALF, HALF), 1)
    return key <= query


def cat(parts, axis=0):
    return parts[0] if len(parts) == 1 else jnp.concatenate(parts, axis=axis)

def swap_upper(value):
    return jnp.concatenate(
        [value[:HALF], lax.ppermute(value[HALF:], "g", MIRROR)], axis=0
    )


def one_hot(rows, columns, row_of_column):
    row = lax.broadcasted_iota(jnp.int32, (rows, columns), 0)
    column = lax.broadcasted_iota(jnp.int32, (rows, columns), 1)
    return (row == row_of_column(column)).astype(BF16)


def natural_of(column):
    g, rest = column // 24, column % 24
    return 12 * (GROUPS * (rest // 12) + g) + rest % 12


def team_peer(c, h, k):
    return lax.rem(c + k // 2, 2), lax.rem(h + k % 2, 2)


def greet(devices):
    barrier = pltpu.get_barrier_semaphore()
    for device in devices:
        pl.semaphore_signal(barrier, inc=1, device_id=device, device_id_type=MESH)
    pl.semaphore_wait(barrier, len(devices))


def send(src, dst, sems, slot, device):
    copy = pltpu.make_async_remote_copy(
        src_ref=src,
        dst_ref=dst,
        send_sem=sems.at[0, slot],
        recv_sem=sems.at[1, slot],
        device_id=device,
        device_id_type=MESH,
    )
    copy.start()
    return copy


def middle_kernel(
    att_ref,
    hid_ref,
    cot_ref,
    w_out_ref,
    rows_ref,
    w_fc_ref,
    w_fc_t_ref,
    w_proj_ref,
    w_proj_t_ref,
    vec_ref,
    hidden_ref,
    grad_mid_ref,
    grad_attn_ref,
    grad_pre_ref,
    normed_ref,
    activ_ref,
    attended_ref,
    grad_ref,
    upper_ref,
    norm_ref,
    att,
    mid,
    grad_activ,
    whole_out,
    norm_out,
    norm_in,
    out_out,
    out_in,
    attn,
    upper,
    att_sems,
    norm_sems,
    out_sems,
    attn_sems,
    upper_sems,
):
    c, g, h = lax.axis_index("c"), lax.axis_index("g"), lax.axis_index("h")
    rank = 2 * c + h
    mirror = GROUPS - 1 - g
    peers = [team_peer(c, h, k) for k in range(4)]
    team = [(pc, g, ph) for pc, ph in peers[1:]]
    across = [(pc, mirror, ph) for pc, ph in peers]
    greet(team + across)

    low, high = pl.ds(0, HALF), pl.ds(HALF, HALF)
    copies = [
        send(att_ref.at[low], att.at[rank, low], att_sems, k, device)
        for k, device in enumerate(team)
    ]
    copies += [
        send(att_ref.at[high], att.at[rank, high], att_sems, 3 + k, device)
        for k, device in enumerate(across)
    ]
    att[rank, low, :] = att_ref[low, :]

    cotangent = cot_ref[...]
    thirds = [pl.ds(256 * k, 256) for k in range(3)]
    for part in thirds:
        grad_activ[:, part] = matmul(cotangent, w_proj_t_ref[:, part])
    for copy in copies:
        copy.wait_recv()

    bias_out, gain, shift, bias_fc, bias_proj = (vec_ref[k : k + 1, :] for k in range(5))

    total = hid_ref[...].astype(F32) + bias_out
    for t in range(4):
        total += matmul(att[t], w_out_ref[pl.ds(LOCAL * t, LOCAL), :])
    mid[...] = total
    normed_ref[...] = layer_norm(total, gain, shift).astype(BF16)
    normed = normed_ref[...]
    for part in thirds:
        pre = matmul(normed, w_fc_ref[:, part]) + bias_fc[:, part.start : part.start + 256]
        square = pre * pre
        bend = jnp.tanh(GELU_ROOT * pre * (1.0 + GELU_CUBE * square))
        activ_ref[:, part] = (0.5 * pre * (1.0 + bend)).astype(BF16)
        slope = 0.5 * (1.0 + bend) + 0.5 * pre * (1.0 - bend * bend) * GELU_ROOT * (
            1.0 + 3.0 * GELU_CUBE * square
        )
        grad_pre_ref[:, part] = (grad_activ[:, part] * slope).astype(BF16)

    def spread_out(left, right_ref, whole, out, into, sems):
        left = left[...]
        for part in thirds:
            whole[:, part] = matmul(left, right_ref[:, part])
        copies = []
        for k, (pc, ph) in enumerate(peers):
            if k:
                rows = pl.ds(pl.multiple_of(128 * (2 * pc + ph), 128), 128)
                out[k] = whole[rows, :].astype(BF16)
                copies.append(send(out.at[k], into.at[k], sems, k, team[k - 1]))
        return copies

    norm_copies = spread_out(grad_pre_ref, w_fc_t_ref, grad_activ, norm_out, norm_in, norm_sems)
    out_copies = spread_out(activ_ref, w_proj_ref, whole_out, out_out, out_in, out_sems)
    own = pl.ds(pl.multiple_of(128 * rank, 128), 128)
    for copy in norm_copies:
        copy.wait_recv()
    grad_norm = grad_activ[own, :]
    for k in (1, 2, 3):
        grad_norm += norm_in[k].astype(F32)
    own_mid = mid[own, :]
    centred = own_mid - jnp.mean(own_mid, axis=-1, keepdims=True)
    scale = lax.rsqrt(jnp.mean(centred * centred, axis=-1, keepdims=True) + EPS)
    hat = centred * scale
    pull = grad_norm * gain
    pull = pull - jnp.mean(pull, axis=-1, keepdims=True)
    pull = pull - hat * jnp.mean(pull * hat, axis=-1, keepdims=True)
    grad_mid = cot_ref[own, :].astype(F32) + scale * pull
    grad_mid_ref[...] = grad_mid
    attn[rank] = grad_mid.astype(BF16)
    attn_copies = [
        send(attn.at[rank], attn.at[rank], attn_sems, k, device) for k, device in enumerate(team)
    ]
    norm_ref[...] = jnp.zeros_like(norm_ref)
    norm_ref[0:1, :] = jnp.sum(grad_norm * hat, axis=0, keepdims=True)
    norm_ref[1:2, :] = jnp.sum(grad_norm, axis=0, keepdims=True)
    for copy in out_copies:
        copy.wait_recv()
    output = own_mid + bias_proj + whole_out[own, :]
    for k in (1, 2, 3):
        output += out_in[k].astype(F32)
    hidden_ref[...] = output.astype(BF16)
    for t in range(4):
        attended_ref[t] = att[t]
    for copy in attn_copies:
        copy.wait_recv()
    for t in (2, 3, 0, 1):
        rows = pl.ds(128 * t, 128)
        block = attn[t]
        grad_attn_ref[rows, :] = block
        grad_ref[rows, :] = trans_right(block, rows_ref[...]).astype(BF16)
        if t == 3:
            upper_copy = send(
                grad_ref.at[high], upper, upper_sems, 0, (c, mirror, h)
            )
    upper_copy.wait_recv()
    upper_ref[...] = upper[...]
    for copy in copies + norm_copies + out_copies + attn_copies + [upper_copy]:
        copy.wait_send()


def middle(*args):
    def out(shape, dtype):
        return jax.ShapeDtypeStruct(shape, dtype)

    vmem = pl.BlockSpec(memory_space=pltpu.VMEM)
    outs = [
        out((128, D), BF16),
        out((128, D), F32),
        out((512, D), BF16),
        out((512, D), BF16),
        out((512, D), BF16),
        out((512, D), BF16),
        out((4, 512, LOCAL), BF16),
        out((512, LOCAL), BF16),
        out((HALF, LOCAL), BF16),
        out((8, D), F32),
    ]
    return pl.pallas_call(
        middle_kernel,
        out_shape=outs,
        in_specs=[vmem] * len(args),
        out_specs=[vmem] * len(outs),
        scratch_shapes=[
            pltpu.VMEM((4, 512, LOCAL), BF16),
            pltpu.VMEM((512, D), F32),
            pltpu.VMEM((512, D), F32),
            pltpu.VMEM((512, D), F32),
            pltpu.VMEM((4, 128, D), BF16),
            pltpu.VMEM((4, 128, D), BF16),
            pltpu.VMEM((4, 128, D), BF16),
            pltpu.VMEM((4, 128, D), BF16),
            pltpu.VMEM((4, 128, D), BF16),
            pltpu.VMEM((HALF, LOCAL), BF16),
            pltpu.SemaphoreType.DMA((2, 7)),
            pltpu.SemaphoreType.DMA((2, 4)),
            pltpu.SemaphoreType.DMA((2, 4)),
            pltpu.SemaphoreType.DMA((2, 3)),
            pltpu.SemaphoreType.DMA((2, 1)),
        ],
        compiler_params=pltpu.CompilerParams(
            vmem_limit_bytes=VMEM_BYTES, collective_id=1, has_side_effects=True
        ),
        cost_estimate=pl.CostEstimate(
            flops=9 * 512 * D * D, bytes_accessed=16 * 512 * D, transcendentals=512 * D
        ),
    )(*args)


def wrap(value, size):
    return lax.rem(value + size, size)


class Plane:
    def __init__(self, c, g, h):
        self.c, self.g, self.h = c, g, h
        self.y, self.z, self.core = g // 8, (g // 2) % 4, g % 2

    def place(self, first, second, core):
        dz = first * (1 - core) + second * core
        dy = first * core + second * (1 - core)
        return 8 * wrap(self.y + dy, 4) + 2 * wrap(self.z + dz, 4) + core

    def device(self, first, second):
        return (self.c, self.place(first, second, self.core), self.h)

    def sibling(self):
        return (self.c, self.g + 1 - 2 * self.core, self.h)


def shift_of(index):
    return ((index + 1) % 3 + 1) * jnp.minimum(index, 1)


def travel(plane, held, near_sems, pair_sems, tall):
    def halves():
        return (pl.ds(0, tall), pl.ds(tall, tall))

    def source(d, e, core):
        return plane.place(shift_of(d), shift_of(e), core)

    def copy(n, half, slot, first, second):
        rows = halves()[half]
        return pltpu.make_async_remote_copy(
            src_ref=held.at[slot, rows],
            dst_ref=held.at[slot, rows],
            send_sem=near_sems.at[0, half, n],
            recv_sem=near_sems.at[1, half, n],
            device_id=plane.device(first, second),
            device_id_type=MESH,
        )

    def across(n, slot):
        return pltpu.make_async_remote_copy(
            src_ref=held.at[slot],
            dst_ref=held.at[slot],
            send_sem=pair_sems.at[0, n],
            recv_sem=pair_sems.at[1, n],
            device_id=plane.sibling(),
            device_id_type=MESH,
        )

    def each(n, act):
        d, e = n % 4, n // 4
        slot = source(d, e, plane.core)
        act(across(n, slot))

        @pl.when(n == 0)
        def _():
            for half in (0, 1):
                act(copy(1, half, slot, 1, 0))
                act(copy(2, half, slot, 3, 0))

        @pl.when(n == 1)
        def _():
            act(copy(3, 0, slot, 1, 0))

        @pl.when(n == 2)
        def _():
            act(copy(3, 1, slot, 3, 0))

        @pl.when(e == 0)
        def _():
            for half in (0, 1):
                act(copy(4 + d, half, slot, 0, 1))
                act(copy(8 + d, half, slot, 0, 3))

        @pl.when(e == 1)
        def _():
            act(copy(12 + d, 0, slot, 0, 1))

        @pl.when(e == 2)
        def _():
            act(copy(12 + d, 1, slot, 0, 3))

    def depart(n):
        each(n, lambda c: c.start())

    def arrive(n):
        for half in (0, 1):
            copy(n, half, source(n % 4, n // 4, plane.core), 0, 1).wait_recv()
        depart(n)

    def arrive_across(n):
        across(n, source(n % 4, n // 4, 1 - plane.core)).wait_recv()

    def finish():
        def sent(n, carry):
            each(n, lambda c: c.wait_send())
            return carry

        lax.fori_loop(0, 16, sent, 0)

    def place_of(n, other):
        return source(n % 4, n // 4, plane.core + other - 2 * plane.core * other)

    return depart, arrive, arrive_across, place_of, finish


def fused_forward_kernel(
    q_ref, kv_ref, cot_ref, att_ref, nat_ref, lse_ref, far_ref, cot_all_ref, all_ref,
    held, qz, upper, cot, top, total, accum, near_sems, pair_sems, upper_sems, team_sems, out_sems,
):
    c, g, h = lax.axis_index("c"), lax.axis_index("g"), lax.axis_index("h")
    plane = Plane(c, g, h)
    mirror = (c, GROUPS - 1 - g, h)
    rank = 2 * c + h
    team = [(pc, g, ph) for pc, ph in (team_peer(c, h, k) for k in (1, 2, 3))]
    greet(
        team
        + [plane.sibling(), plane.device(1, 0), plane.device(3, 0)]
        + [plane.device(0, 1), plane.device(0, 3), mirror]
    )
    swap = send(q_ref.at[pl.ds(HALF, HALF)], upper, upper_sems, 0, mirror)
    held[g] = kv_ref[...]
    depart, arrive, arrive_across, place_of, finish = travel(plane, held, near_sems, pair_sems, CARGO)
    top[...] = jnp.full_like(top, NEG)
    total[...] = jnp.zeros_like(total)
    accum[...] = jnp.zeros_like(accum)
    left = lax.broadcasted_iota(jnp.int32, (HALF, 128), 1) < 64

    def place_queries(slot, block):
        span = pl.ds(slot * HALF, HALF)
        pair = block[:, :128].astype(F32)
        qz[0, span, :] = jnp.where(left, pair, 0.0).astype(BF16)
        qz[1, span, :] = jnp.where(left, 0.0, pair).astype(BF16)
        qz[2, span, :] = jnp.concatenate(
            [block[:, 128:], jnp.zeros((HALF, 64), BF16)], axis=1
        )

    place_queries(0, q_ref[pl.ds(0, HALF), :])

    def tiles(device, units):
        chains = []
        for slot, halves, masked in units:
            span = pl.ds(slot * HALF, HALF)
            first, second, third = (
                cat([held[device, pl.ds(CARGO * x, HALF), pl.ds(128 * k, 128)] for x in halves])
                for k in range(3)
            )
            second_t, third_t = second.T, third.T
            values = (second_t[64:], third_t[:64], third_t[64:])
            for n, keys in enumerate((first, first, second)):
                scores = nt(keys, qz[n, span, :])
                if masked:
                    scores = jnp.where(diagonal(), scores, NEG)
                chains.append((slot, n, values[n], scores))
        ready = []
        for slot, n, value, scores in chains:
            line = pl.ds(8 * slot + n, 1)
            old = top[line, :]
            new = jnp.maximum(old, jnp.max(scores, axis=0, keepdims=True))
            weights = jnp.exp(scores - new)
            fade = jnp.exp(old - new)
            top[line, :] = new
            total[line, :] = total[line, :] * fade + jnp.sum(weights, axis=0, keepdims=True)
            ready.append((slot, n, value, weights.astype(BF16), fade))
        for slot, n, value, weights, fade in ready:
            accum[slot, n] = accum[slot, n] * fade + matmul(value, weights)

    def keep(slot):
        return pltpu.make_async_copy(held.at[slot], all_ref.at[slot], out_sems.at[slot])

    def work(device):
        keep(device).start()

        low, high = device < g, device < GROUPS - 1 - g

        @pl.when(low & high)
        def _():
            tiles(device, [(0, (0,), False), (1, (0, 1), False)])

        @pl.when(low & ~high)
        def _():
            tiles(device, [(0, (0,), False), (1, (0,), False)])

        @pl.when(~low & high)
        def _():
            tiles(device, [(1, (0, 1), False)])

        @pl.when(~low & ~high)
        def _():
            tiles(device, [(1, (0,), False)])

        @pl.when(device == g)
        def _():
            tiles(device, [(0, (0,), True)])

        @pl.when(device == GROUPS - 1 - g)
        def _():
            tiles(device, [(1, (1,), True)])

    lax.fori_loop(0, 1, lambda n, carry: (depart(n), carry)[1], 0)
    cot_copies = [send(cot_ref, cot.at[rank], team_sems, k, device) for k, device in enumerate(team)]
    swap.wait_recv()
    place_queries(1, upper[...])
    far_ref[...] = upper[...]

    def step(m, carry):
        n, other = m // 2, m % 2

        @pl.when((other == 0) & (n > 0))
        def _():
            arrive(n)

        @pl.when(other == 1)
        def _():
            arrive_across(n)

        work(place_of(n, other))
        return carry

    lax.fori_loop(0, 32, step, 0)
    for slot in range(2):
        for n in range(3):
            line = pl.ds(8 * slot + n, 1)
            att_ref[slot, pl.ds(64 * n, 64), :] = accum[slot, n] / total[line, :]
        span = pl.ds(slot * HALF, HALF)
        nat_ref[span, :] = att_ref[slot].T.astype(BF16)
        lines = pl.ds(8 * slot, 8)
        lse_ref[:, span] = (top[lines, :] + jnp.log(jnp.maximum(total[lines, :], 1e-30))) * LOG2E
    cot[rank] = cot_ref[...]
    for copy in cot_copies:
        copy.wait_recv()
    for t in range(4):
        cot_all_ref[pl.ds(128 * t, 128), :] = cot[t]
    for copy in cot_copies + [swap]:
        copy.wait_send()
    finish()
    for slot in range(GROUPS):
        keep(slot).wait()


def fused_forward(*args):
    vmem = pl.BlockSpec(memory_space=pltpu.VMEM)
    return pl.pallas_call(
        fused_forward_kernel,
        out_shape=[
            jax.ShapeDtypeStruct((2, LOCAL, HALF), F32),
            jax.ShapeDtypeStruct((512, LOCAL), BF16),
            jax.ShapeDtypeStruct((8, 512), F32),
            jax.ShapeDtypeStruct((HALF, LOCAL), BF16),
            jax.ShapeDtypeStruct((512, D), BF16),
            jax.ShapeDtypeStruct((GROUPS, 2 * CARGO, 2 * LOCAL), BF16),
        ],
        in_specs=[vmem, vmem, vmem],
        out_specs=[vmem, vmem, vmem, vmem, vmem, pl.BlockSpec(memory_space=pl.ANY)],
        scratch_shapes=[
            pltpu.VMEM((GROUPS, 2 * CARGO, 2 * LOCAL), BF16),
            pltpu.VMEM((3, 512, 128), BF16),
            pltpu.VMEM((HALF, LOCAL), BF16),
            pltpu.VMEM((4, 128, D), BF16),
            pltpu.VMEM((16, HALF), F32),
            pltpu.VMEM((16, HALF), F32),
            pltpu.VMEM((2, 3, 64, HALF), F32),
            pltpu.SemaphoreType.DMA((2, 2, 16)),
            pltpu.SemaphoreType.DMA((2, 16)),
            pltpu.SemaphoreType.DMA((2, 1)),
            pltpu.SemaphoreType.DMA((2, 3)),
            pltpu.SemaphoreType.DMA((GROUPS,)),
        ],
        compiler_params=pltpu.CompilerParams(
            vmem_limit_bytes=VMEM_BYTES, collective_id=2, has_side_effects=True
        ),
        cost_estimate=pl.CostEstimate(
            flops=65 * 3 * HALF * HALF * 1024, bytes_accessed=32 << 20, transcendentals=65 * 3 * HALF * HALF
        ),
    )(*args)


def place_sides(first, second, span, block):
    left = lax.broadcasted_iota(jnp.int32, (HALF, 128), 1) < 64
    a, b, c = (block[:, 128 * k : 128 * k + 128].astype(F32) for k in range(3))
    for refs, n, part, side in (
        (first, 0, a, left),
        (first, 1, a, ~left),
        (first, 2, b, left),
        (second, 0, b, ~left),
        (second, 1, c, left),
        (second, 2, c, ~left),
    ):
        refs[n, span, :] = jnp.where(side, part, 0.0).astype(BF16)


def backward_kernel(
    mine_ref, att_ref, lse_ref, kv_ref, dq_ref, dkv_ref,
    held, stats, qz, dz, kz, vz, acc_q, acc_k, acc_v, whole, near_sems, pair_sems,
):
    c, g, h = lax.axis_index("c"), lax.axis_index("g"), lax.axis_index("h")
    plane = Plane(c, g, h)
    greet(
        [plane.sibling(), plane.device(1, 0), plane.device(3, 0)]
        + [plane.device(0, 1), plane.device(0, 3)]
    )
    low_rows, high_rows = pl.ds(0, HALF), pl.ds(HALF, HALF)
    for slot, span in enumerate((low_rows, high_rows)):
        block = mine_ref[span, :]
        held[g, pl.ds(TALL * slot, HALF), :] = block
        place_sides(qz, dz, span, block)
        grads = block[:, LOCAL:].astype(F32).T
        product = grads * att_ref[slot]
        delta = [jnp.sum(product[64 * n : 64 * n + 64], axis=0, keepdims=True) for n in range(3)]
        lines = jnp.concatenate([lse_ref[0:3, span], *delta, jnp.zeros((2, HALF), F32)], axis=0)
        stats[:, span] = lines
        head = lines.astype(BF16).astype(F32)
        body = (lines - head).astype(BF16).astype(F32)
        tail = lines - head - body
        packed = jnp.concatenate([head, body, tail, jnp.zeros_like(tail)], axis=0)
        held[g, pl.ds(TALL * slot + HALF, 32), pl.ds(0, HALF)] = packed.astype(BF16)
    depart, arrive, arrive_across, place_of, finish = travel(
        plane, held, near_sems, pair_sems, TALL
    )
    lax.fori_loop(0, 1, lambda n, carry: (depart(n), carry)[1], 0)
    place_sides(kz, vz, low_rows, kv_ref[g, low_rows, :])
    place_sides(kz, vz, high_rows, kv_ref[GROUPS - 1 - g, pl.ds(CARGO, HALF), :])
    for ref in (acc_q, acc_k, acc_v):
        ref[...] = jnp.zeros_like(ref)

    def groups(block_of):
        return [block_of(pl.ds(128 * k, 128)) for k in range(3)]

    def query_tiles(device, units):
        chains = []
        for slot, halves, masked in units:
            span = pl.ds(slot * HALF, HALF)

            def rows_of(lanes):
                return cat([kv_ref[device, pl.ds(CARGO * x, HALF), lanes] for x in halves])

            a, b, c = groups(rows_of)
            a_t, b_t = a.T, b.T
            for n, (keys, values, keys_t) in enumerate(
                ((a, b, a_t[:64]), (a, c, a_t[64:]), (b, c, b_t[:64]))
            ):
                chains.append(
                    (slot, n, masked, keys_t, nt(keys, qz[n, span, :]), nt(values, dz[n, span, :]))
                )
        ready = []
        for slot, n, masked, keys_t, scores, pull in chains:
            span = pl.ds(slot * HALF, HALF)
            scores = scores * LOG2E - stats[pl.ds(n, 1), span]
            if masked:
                scores = jnp.where(diagonal(), scores, NEG)
            pull = pull - stats[pl.ds(3 + n, 1), span]
            ready.append((slot, n, keys_t, (jnp.exp2(scores) * pull).astype(BF16)))
        for slot, n, keys_t, grad in ready:
            acc_q[slot, n] += matmul(keys_t, grad)

    def key_tiles(device, units):
        chains = []
        for slot, halves, masked in units:
            span = pl.ds(slot * HALF, HALF)

            def rows_of(lanes):
                return cat([held[device, pl.ds(TALL * half, HALF), lanes] for half in halves])

            a, b, c = groups(rows_of)
            lines = cat(
                [
                    held[device, pl.ds(TALL * half + HALF, 32), pl.ds(0, HALF)].astype(F32)
                    for half in halves
                ],
                1,
            )
            lines = lines[0:8] + lines[8:16] + lines[16:24]
            for n, (queries, grads) in enumerate(((a, b), (a, c), (b, c))):
                chains.append(
                    (
                        slot,
                        n,
                        masked,
                        queries,
                        grads,
                        lines,
                        nt(kz[n, span, :], queries),
                        nt(vz[n, span, :], grads),
                    )
                )
        ready = []
        for slot, n, masked, queries, grads, lines, scores, pull in chains:
            scores = scores * LOG2E - lines[n : n + 1]
            if masked:
                scores = jnp.where(diagonal(), scores, NEG)
            weights = jnp.exp2(scores)
            pull = weights * (pull - lines[3 + n : 4 + n])
            ready.append((slot, n, queries, grads, weights.astype(BF16), pull.astype(BF16)))
        for slot, n, queries, grads, weights, pull in ready:
            acc_v[slot, n] += matmul(weights, grads)
            acc_k[slot, n] += matmul(pull, queries)

    def step(m, carry):
        n, other = m // 2, m % 2

        @pl.when((other == 0) & (n > 0))
        def _():
            arrive(n)

        @pl.when(other == 1)
        def _():
            arrive_across(n)

        device = place_of(n, other)
        low, high = device < g, device < GROUPS - 1 - g

        @pl.when(low & high)
        def _():
            query_tiles(device, [(0, (0,), False), (1, (0, 1), False)])

        @pl.when(low & ~high)
        def _():
            query_tiles(device, [(0, (0,), False), (1, (0,), False)])

        @pl.when(~low & high)
        def _():
            query_tiles(device, [(1, (0, 1), False)])

        @pl.when(~low & ~high)
        def _():
            query_tiles(device, [(1, (0,), False)])

        @pl.when(device == GROUPS - 1 - g)
        def _():
            query_tiles(device, [(1, (1,), True)])

        @pl.when(device > g)
        def _():
            key_tiles(device, [(0, (0, 1), False)])

        @pl.when(device < g)
        def _():
            key_tiles(device, [(0, (1,), False), (1, (1,), False)])

        @pl.when(device == g)
        def _():
            query_tiles(device, [(0, (0,), True)])
            key_tiles(device, [(0, (0,), True), (1, (1,), True)])
            key_tiles(device, [(0, (1,), False)])

        return carry

    lax.fori_loop(0, 32, step, 0)
    left = lax.broadcasted_iota(jnp.int32, (HALF, 128), 1) < 64
    for slot, span in enumerate((low_rows, high_rows)):
        for n in range(3):
            whole[pl.ds(64 * n, 64), :] = acc_q[slot, n] * 0.125
        dq_ref[span, :] = whole[...].T.astype(BF16)
        for k, (one, two) in enumerate(
            (
                (acc_k[slot, 0], acc_k[slot, 1]),
                (acc_k[slot, 2], acc_v[slot, 0]),
                (acc_v[slot, 1], acc_v[slot, 2]),
            )
        ):
            dkv_ref[span, pl.ds(128 * k, 128)] = jnp.where(left, one, two).astype(BF16)
    finish()


def backward(mine, att, lse, kv):
    vmem = pl.BlockSpec(memory_space=pltpu.VMEM)
    sides_shape = pltpu.VMEM((3, 512, 128), BF16)
    return pl.pallas_call(
        backward_kernel,
        out_shape=[
            jax.ShapeDtypeStruct((512, LOCAL), BF16),
            jax.ShapeDtypeStruct((512, 2 * LOCAL), BF16),
        ],
        in_specs=[vmem] * 4,
        out_specs=[vmem] * 2,
        scratch_shapes=[
            pltpu.VMEM((GROUPS, 2 * TALL, 2 * LOCAL), BF16),
            pltpu.VMEM((8, 512), F32),
            sides_shape,
            sides_shape,
            sides_shape,
            sides_shape,
            pltpu.VMEM((2, 3, 64, HALF), F32),
            pltpu.VMEM((2, 3, HALF, 128), F32),
            pltpu.VMEM((2, 3, HALF, 128), F32),
            pltpu.VMEM((LOCAL, HALF), F32),
            pltpu.SemaphoreType.DMA((2, 2, 16)),
            pltpu.SemaphoreType.DMA((2, 16)),
        ],
        compiler_params=pltpu.CompilerParams(
            vmem_limit_bytes=VMEM_BYTES, collective_id=3, has_side_effects=True
        ),
        cost_estimate=pl.CostEstimate(
            flops=65 * 3 * HALF * HALF * 3584,
            bytes_accessed=32 << 20,
            transcendentals=2 * 65 * 3 * HALF * HALF,
        ),
    )(mine, att, lse, kv)


def head_kernel(
    hid_ref, mine_ref, theirs_ref, mine_two_ref, theirs_two_ref, hid_all_ref, first_ref, second_ref,
    hid, other, other_two, held, team_sems, near_sems, pair_sems,
):
    c, g, h = lax.axis_index("c"), lax.axis_index("g"), lax.axis_index("h")
    rank = 2 * c + h
    plane = Plane(c, g, h)
    team = [(pc, g, ph) for pc, ph in (team_peer(c, h, k) for k in (1, 2, 3))]
    greet(
        team
        + [plane.sibling(), plane.device(1, 0), plane.device(3, 0)]
        + [plane.device(0, 1), plane.device(0, 3)]
    )
    swaps = [
        send(theirs_ref, other, team_sems, 3, team[1]),
        send(theirs_two_ref, other_two, team_sems, 4, team[1]),
    ]
    copies = [send(hid_ref, hid.at[rank], team_sems, k, device) for k, device in enumerate(team)]
    own_rows = pl.ds(pl.multiple_of(16 * c, 16), 16)
    other_rows = pl.ds(pl.multiple_of(16 - 16 * c, 16), 16)
    held[g, own_rows, :] = mine_ref[...]
    second_ref[own_rows, :] = mine_two_ref[...]
    swaps[0].wait_recv()
    held[g, other_rows, :] = other[...]
    depart, arrive, arrive_across, place_of, finish = travel(plane, held, near_sems, pair_sems, 16)
    lax.fori_loop(0, 1, lambda n, carry: (depart(n), carry)[1], 0)
    lax.fori_loop(1, 16, lambda n, carry: (arrive(n), carry)[1], 0)
    hid[rank] = hid_ref[...]
    for copy in copies:
        copy.wait_recv()
    for t in range(4):
        hid_all_ref[pl.ds(128 * t, 128), :] = hid[t]
    swaps[1].wait_recv()
    second_ref[other_rows, :] = other_two[...]
    lax.fori_loop(0, 16, lambda n, carry: (arrive_across(n), carry)[1], 0)
    first_ref[...] = held[...]
    for copy in copies + swaps:
        copy.wait_send()
    finish()


def head(*args):
    vmem = pl.BlockSpec(memory_space=pltpu.VMEM)
    return pl.pallas_call(
        head_kernel,
        out_shape=[
            jax.ShapeDtypeStruct((512, D), BF16),
            jax.ShapeDtypeStruct((GROUPS, 32, 640), BF16),
            jax.ShapeDtypeStruct((32, 2 * D), BF16),
        ],
        in_specs=[vmem] * 5,
        out_specs=[vmem] * 3,
        scratch_shapes=[
            pltpu.VMEM((4, 128, D), BF16),
            pltpu.VMEM((16, 640), BF16),
            pltpu.VMEM((16, 2 * D), BF16),
            pltpu.VMEM((GROUPS, 32, 640), BF16),
            pltpu.SemaphoreType.DMA((2, 5)),
            pltpu.SemaphoreType.DMA((2, 2, 16)),
            pltpu.SemaphoreType.DMA((2, 16)),
        ],
        compiler_params=pltpu.CompilerParams(
            vmem_limit_bytes=VMEM_BYTES, collective_id=4, has_side_effects=True
        ),
        cost_estimate=pl.CostEstimate(flops=0, bytes_accessed=4 << 20, transcendentals=0),
    )(*args)


def tail_kernel(
    dq_ref, dkv_ref, wq_ref, wkv_ref, norm_t_ref, hid_ref, mid_ref, vec_ref,
    mask_ref, gain_ref, shift_ref, mask_q_ref, put_q_ref, mask_kv_ref, put_kv_ref,
    grad_ref, total_ref, small_ref,
    up_q, up_kv, part, part_out, part_in, out, into, small_out, small_in, team_small, gathered,
    swap_sems, part_sems, out_sems, small_sems, gather_sems, last_sems,
):
    c, g, h = lax.axis_index("c"), lax.axis_index("g"), lax.axis_index("h")
    rank = 2 * c + h
    peers = [team_peer(c, h, k) for k in range(4)]
    team = [(pc, g, ph) for pc, ph in peers[1:]]

    def other(k):
        return (c, lax.rem(g + k, GROUPS), h)

    barrier = pltpu.get_barrier_semaphore()

    def hello(k, carry):
        pl.semaphore_signal(barrier, inc=1, device_id=other(k), device_id_type=MESH)
        return carry

    lax.fori_loop(1, GROUPS, hello, 0)
    for device in team:
        pl.semaphore_signal(barrier, inc=1, device_id=device, device_id_type=MESH)
    pl.semaphore_wait(barrier, GROUPS + 2)

    low, high = pl.ds(0, HALF), pl.ds(HALF, HALF)
    mirror = (c, GROUPS - 1 - g, h)
    swaps = [
        send(dq_ref.at[high], up_q, swap_sems, 0, mirror),
        send(dkv_ref.at[high], up_kv, swap_sems, 1, mirror),
    ]
    dq_low, dkv_low = dq_ref[low, :], dkv_ref[low, :]
    part[low, :] = matmul(dq_low, wq_ref[...]) + matmul(dkv_low, wkv_ref[...])
    for swap in swaps:
        swap.wait_recv()
    dq_high, dkv_high = up_q[...], up_kv[...]
    part[high, :] = matmul(dq_high, wq_ref[...]) + matmul(dkv_high, wkv_ref[...])
    part_copies = []
    for k, (pc, ph) in enumerate(peers):
        if k:
            rows = pl.ds(pl.multiple_of(128 * (2 * pc + ph), 128), 128)
            part_out[k] = part[rows, :].astype(BF16)
            part_copies.append(send(part_out.at[k], part_in.at[k], part_sems, k, team[k - 1]))

    for j in range(4):
        rows = pl.ds(256 * j, 256)
        before, after = norm_t_ref[rows, low], norm_t_ref[rows, high]
        kv = matmul(before, dkv_low) + matmul(after, dkv_high)
        q = matmul(before, dq_low) + matmul(after, dq_high)
        span = pl.ds(8 * j, 8)
        out[span, :, pl.ds(0, 2 * LOCAL)] = kv.reshape(8, 32, 2 * LOCAL).astype(BF16)
        out[span, :, pl.ds(2 * LOCAL, LOCAL)] = q.reshape(8, 32, LOCAL).astype(BF16)

    def out_copy(k):
        return pltpu.make_async_remote_copy(
            src_ref=out.at[lax.rem(g + k, GROUPS)],
            dst_ref=into.at[k],
            send_sem=out_sems.at[0, k],
            recv_sem=out_sems.at[1, k],
            device_id=other(k),
            device_id_type=MESH,
        )

    def small_copy(k):
        return pltpu.make_async_remote_copy(
            src_ref=small_out.at[lax.rem(g + k, GROUPS)],
            dst_ref=small_in.at[k],
            send_sem=small_sems.at[0, k],
            recv_sem=small_sems.at[1, k],
            device_id=other(k),
            device_id_type=MESH,
        )

    def for_others(act):
        lax.fori_loop(1, GROUPS, lambda k, carry: (act(k), carry)[1], 0)

    for_others(lambda k: out_copy(k).start())

    own = pl.ds(pl.multiple_of(128 * rank, 128), 128)
    for copy in part_copies:
        copy.wait_recv()
    grad_norm = part[own, :]
    for k in (1, 2, 3):
        grad_norm += part_in[k].astype(F32)
    resid = hid_ref[...].astype(F32)
    centred = resid - jnp.mean(resid, axis=-1, keepdims=True)
    scale = lax.rsqrt(jnp.mean(centred * centred, axis=-1, keepdims=True) + EPS)
    hat = centred * scale
    pull = grad_norm * vec_ref[0:1, :]
    pull = pull - jnp.mean(pull, axis=-1, keepdims=True)
    pull = pull - hat * jnp.mean(pull * hat, axis=-1, keepdims=True)
    grad_ref[...] = mid_ref[...] + scale * pull

    def lay(line, mask, put):
        top = line.astype(BF16).astype(F32)
        both = [jnp.where(mask > 0, jnp.broadcast_to(v, mask.shape), 0.0) for v in (top, line - top)]
        return sum(matmul(v.astype(BF16), put) for v in both)

    def column_sum(value):
        return jnp.sum(value, axis=0, keepdims=True)

    sum_q = column_sum(dq_low.astype(F32)) + column_sum(dq_high.astype(F32))
    sum_kv = column_sum(dkv_low.astype(F32)) + column_sum(dkv_high.astype(F32))
    lines = (
        lay(column_sum(grad_norm * hat), mask_ref[...], gain_ref[...])
        + lay(column_sum(grad_norm), mask_ref[...], shift_ref[...])
        + lay(sum_q, mask_q_ref[...], put_q_ref[...])
        + lay(sum_kv, mask_kv_ref[...], put_kv_ref[...])
    )
    for k in range(GROUPS):
        small_out[k] = jnp.broadcast_to(lines[k : k + 1], (8, 128))
    for_others(lambda k: small_copy(k).start())

    for_others(lambda k: out_copy(k).wait_recv())
    total = lax.fori_loop(
        1, GROUPS, lambda k, sofar: sofar + into[k].astype(F32), out[g].astype(F32)
    )
    gathered[rank] = total.astype(BF16)
    gather_copies = [
        send(gathered.at[rank], gathered.at[rank], gather_sems, k, device)
        for k, device in enumerate(team)
    ]
    for_others(lambda k: small_copy(k).wait_recv())
    team_small[rank] = lax.fori_loop(
        1, GROUPS, lambda k, sofar: sofar + small_in[k], small_out[g]
    )
    last_copies = [
        send(team_small.at[rank], team_small.at[rank], last_sems, k, device)
        for k, device in enumerate(team)
    ]
    for copy in gather_copies + last_copies:
        copy.wait_recv()
    total_ref[...] = gathered[...]
    small_ref[...] = team_small[0] + team_small[1] + team_small[2] + team_small[3]
    for copy in swaps + part_copies + gather_copies + last_copies:
        copy.wait_send()
    for_others(lambda k: out_copy(k).wait_send())
    for_others(lambda k: small_copy(k).wait_send())


def tail(*args):
    vmem = pl.BlockSpec(memory_space=pltpu.VMEM)
    dma = pltpu.SemaphoreType.DMA
    return pl.pallas_call(
        tail_kernel,
        out_shape=[
            jax.ShapeDtypeStruct((128, D), F32),
            jax.ShapeDtypeStruct((4, 32, 3 * LOCAL), BF16),
            jax.ShapeDtypeStruct((8, 128), F32),
        ],
        in_specs=[vmem] * len(args),
        out_specs=[vmem] * 3,
        scratch_shapes=[
            pltpu.VMEM((HALF, LOCAL), BF16),
            pltpu.VMEM((HALF, 2 * LOCAL), BF16),
            pltpu.VMEM((512, D), F32),
            pltpu.VMEM((4, 128, D), BF16),
            pltpu.VMEM((4, 128, D), BF16),
            pltpu.VMEM((GROUPS, 32, 3 * LOCAL), BF16),
            pltpu.VMEM((GROUPS, 32, 3 * LOCAL), BF16),
            pltpu.VMEM((GROUPS, 8, 128), F32),
            pltpu.VMEM((GROUPS, 8, 128), F32),
            pltpu.VMEM((4, 8, 128), F32),
            pltpu.VMEM((4, 32, 3 * LOCAL), BF16),
            dma((2, 2)),
            dma((2, 4)),
            dma((2, GROUPS)),
            dma((2, GROUPS)),
            dma((2, 3)),
            dma((2, 3)),
        ],
        compiler_params=pltpu.CompilerParams(
            vmem_limit_bytes=VMEM_BYTES, collective_id=5, has_side_effects=True
        ),
        cost_estimate=pl.CostEstimate(
            flops=4 * 512 * D * 3 * LOCAL, bytes_accessed=8 << 20, transcendentals=0
        ),
    )(*args)


def padded_feature(column):
    g, c, r = column // 32, (column // 16) % 2, column % 16
    return jnp.where(r < 12, 12 * (GROUPS * c + g) + r, -1)


def on_device(
    hidden_in,
    ln1_gain,
    ln1_shift,
    w_qkv,
    qv_bias,
    w_out,
    out_bias,
    ln2_gain,
    ln2_shift,
    w_fc,
    fc_bias,
    w_proj,
    proj_bias,
    out_grad,
):
    c, g, h = lax.axis_index("c"), lax.axis_index("g"), lax.axis_index("h")
    rank = 2 * c + h

    spread_places = one_hot(D, 1024, padded_feature)
    drop_pad = one_hot(D, 1024, lambda k: jnp.where(k % 32 < 24, 24 * (k // 32) + k % 32, -1))
    reorder = one_hot(D, D, natural_of)
    pick_units = one_hot(1536, D, lambda k: 48 * (k // 24) + 24 * h + k % 24)
    small = jnp.concatenate(
        [ln1_gain, ln1_shift, qv_bias, out_bias, ln2_gain, ln2_shift, fc_bias, proj_bias]
    )
    small = jnp.pad(small.reshape(12, 12), ((0, 0), (0, 52)))
    units = matmul(jnp.concatenate([w_fc[:, :1536], w_fc[:, 1536:]], axis=0), pick_units)
    units = units.astype(BF16)

    def columns_for(of_c):
        r = 2 * of_c + h
        qkv = [lax.dynamic_slice_in_dim(w_qkv, D * k + LOCAL * r, LOCAL, 1) for k in range(3)]
        fc = lax.dynamic_slice_in_dim(units, 12 * of_c, 12, 0)
        parts = (jnp.concatenate([*qkv, small], axis=1), jnp.concatenate([fc, w_out], axis=1))
        return tuple(jnp.pad(p, ((0, 4), (0, 0))) for p in parts)

    mine, theirs = columns_for(c), columns_for(1 - c)
    tokens, first, second = head(hidden_in, mine[0], theirs[0], mine[1], theirs[1])
    resid = tokens.astype(F32)
    proj_rows = lax.dynamic_slice_in_dim(w_proj, 24 * h, 24, 0)
    cargo = jnp.concatenate([second, jnp.pad(proj_rows, ((0, 8), (0, 0)))], axis=1)
    cargo = [cargo[:, 384 * k : 384 * k + 384] for k in range(6)]
    first = first.reshape(1024, 640)
    w_qkv_t = matmul(spread_places, first[:, : 3 * LOCAL]).astype(BF16)

    vectors = first[:, 3 * LOCAL : 3 * LOCAL + 12].reshape(GROUPS, 2, 16, 12)[:, :, :12]
    vectors = vectors.reshape(GROUPS, 2, 144).astype(F32)
    vectors = vectors.transpose(1, 0, 2)
    cut, at = [], 0
    for width in SMALL:
        cut.append(vectors[:, :, at : at + width])
        at += width
    gain_one, shift_one, bias_qv, bias_out, gain_two, shift_two = (
        v.reshape(-1) for v in cut[:6]
    )
    bias_proj = cut[7].reshape(-1)
    bias_fc = lax.dynamic_slice_in_dim(
        lax.dynamic_index_in_dim(cut[6], c, 0, False), 24 * h, 24, 1
    ).reshape(-1)
    bias_q = lax.dynamic_slice_in_dim(bias_qv, LOCAL * rank, LOCAL, 0)
    bias_v = lax.dynamic_slice_in_dim(bias_qv, D + LOCAL * rank, LOCAL, 0)
    bias_here = jnp.concatenate([bias_q, jnp.zeros_like(bias_q), bias_v])

    normed1 = layer_norm(resid, gain_one, shift_one).astype(BF16)
    qkv = (matmul(normed1, w_qkv_t) + bias_here).astype(BF16)
    queries = qkv[:, :LOCAL] * jnp.asarray(0.125, BF16)
    keys_values = qkv[:, LOCAL:]
    load = jnp.concatenate(
        [keys_values[:HALF], *cargo[:3], keys_values[HALF:], *cargo[3:]], axis=0
    )
    att_t, attended_zz, lse, query_far, cotangent, kv_all = fused_forward(queries, load, out_grad)

    def brought(k):
        at = HALF + 32 * k if k < 3 else CARGO + HALF + 32 * (k - 3)
        return kv_all[:, at : at + 32].reshape(1024, 384)

    def brought_pair(k):
        return jnp.concatenate([brought(k), brought(k + 1)], axis=1)

    w_fc_t = matmul(spread_places, brought_pair(0)).astype(BF16)
    w_out_all = matmul(spread_places, brought_pair(2)).astype(BF16)
    w_proj_t = matmul(drop_pad, brought_pair(4)).astype(BF16)
    w_out_rows = lax.dynamic_slice_in_dim(w_out_all, LOCAL * rank, LOCAL, 0)
    vec = jnp.stack([bias_out, gain_two, shift_two, bias_fc, bias_proj])
    (
        hidden_out,
        grad_mid,
        grad_attn_all,
        grad_pre,
        normed2,
        activ,
        attended,
        grad_heads,
        grad_upper,
        norm_sums,
    ) = middle(
        attended_zz,
        tokens,
        cotangent,
        w_out_all,
        w_out_rows,
        w_fc_t,
        w_fc_t.T,
        w_proj_t,
        w_proj_t.T,
        jnp.concatenate([vec, jnp.zeros((3, D), F32)], axis=0),
    )
    attended = jnp.concatenate([attended[t] for t in range(4)], axis=1)
    grad_gain2, grad_shift2 = norm_sums[0], norm_sums[1]
    grad_attn = lax.dynamic_slice_in_dim(grad_attn_all, 128 * rank, 128, 0)
    grad_output = out_grad.astype(F32)
    mine = jnp.concatenate(
        [
            jnp.concatenate([queries[:HALF], query_far], axis=0),
            jnp.concatenate([grad_heads[:HALF], grad_upper], axis=0),
        ],
        axis=1,
    )
    dq, dkv = backward(mine, att_t, lse, kv_all)
    def ones(rows, columns, test):
        row = lax.broadcasted_iota(jnp.int32, (rows, columns), 0)
        column = lax.broadcasted_iota(jnp.int32, (rows, columns), 1)
        return test(row, column)

    def mask(columns, group_of):
        return ones(GROUPS, columns, lambda r, k: r == group_of(k)).astype(F32)

    def put(rows, lane_of):
        return ones(rows, 128, lambda k, lane: lane == lane_of(k)).astype(BF16)

    normed1_t = trans_left_of(spread_places, normed1).astype(BF16)
    w_back = w_qkv_t.T
    input_grad, total_qkv, total_first = tail(
        dq,
        dkv,
        w_back[:LOCAL],
        w_back[LOCAL:],
        normed1_t,
        hidden_in,
        grad_mid,
        jnp.concatenate([gain_one[None], jnp.zeros((7, D), F32)], axis=0),
        mask(D, lambda k: (k // 12) % GROUPS),
        put(D, lambda k: 12 * (k // 384) + k % 12),
        put(D, lambda k: 24 + 12 * (k // 384) + k % 12),
        mask(LOCAL, lambda k: 8 * rank + k // 24),
        put(LOCAL, lambda k: 48 + k % 24),
        mask(2 * LOCAL, lambda k: jnp.where(k < LOCAL, -1, 8 * rank + (k - LOCAL) // 24)),
        put(2 * LOCAL, lambda k: 72 + k % 24),
    )

    def reordered(v):
        return matmul(v, reorder).astype(BF16)

    grad_wfc = trans_left(reordered(normed2), grad_pre)
    grad_attn_cols = lax.dynamic_slice_in_dim(grad_attn_all, LOCAL * rank, LOCAL, 1)
    grad_wout = trans_left(reordered(attended), grad_attn_cols)
    grad_wproj = trans_left(activ, cotangent)

    def sum_over_g(value):
        lines = value.astype(BF16).reshape(GROUPS, 24, value.shape[-1])
        lines = lax.all_to_all(lines, "g", 0, 0, tiled=True)
        return jnp.sum(lines.astype(F32), axis=0)

    def spread(vector):
        return vector.reshape(2, GROUPS, -1)

    fc_sums = jnp.sum(grad_pre.astype(F32), axis=0).reshape(1, GROUPS, 24)
    fc_sums = lax.dynamic_update_slice(
        jnp.zeros((2, GROUPS, 48), F32), fc_sums, (c, jnp.int32(0), 24 * h)
    )
    small_sums = jnp.concatenate(
        [
            spread(jnp.sum(grad_attn.astype(F32), axis=0)),
            spread(grad_gain2),
            spread(grad_shift2),
            fc_sums,
            spread(jnp.sum(grad_output, axis=0)),
        ],
        axis=2,
    )
    small_sums = small_sums.transpose(1, 0, 2).reshape(GROUPS * 24, 8)
    small_sums = jnp.pad(small_sums, ((0, 0), (0, 56)))
    late = sum_over_g(jnp.concatenate([grad_wfc, grad_wproj, grad_wout, small_sums], axis=1))
    pieces = [p.astype(F32) for p in team_gather(late.astype(BF16))]
    own = [lax.dynamic_slice_in_dim(p, 12 * c, 12, 0) for p in pieces]
    fc_pieces = jnp.stack([m[:, :D] for m in own])
    total_wfc = fc_pieces.reshape(2, 2, 12, GROUPS, 24).transpose(2, 0, 3, 1, 4).reshape(12, 3072)
    proj_pieces = jnp.stack([p[:, D : 2 * D] for p in pieces])
    total_wproj = lax.dynamic_slice_in_dim(proj_pieces, 2 * c, 2, 0).reshape(48, D)
    total_wout = jnp.concatenate([m[:, 2 * D : 2 * D + LOCAL] for m in own], axis=1)
    total_late = sum(own)[:, 2 * D + LOCAL : 2 * D + LOCAL + 8].reshape(96)

    qkv_rows = lax.dynamic_slice_in_dim(total_qkv, 16 * c, 16, 1)[:, :12].astype(F32)
    total_wqkv = jnp.concatenate(
        [qkv_rows[t, :, at : at + LOCAL] for at in (2 * LOCAL, 0, LOCAL) for t in range(4)], axis=1
    )

    def first_part(at, width):
        return lax.dynamic_slice_in_dim(total_first[0], at + width * c, width, 0)

    smalls = (
        first_part(0, 12),
        first_part(24, 12),
        first_part(48, 24),
        total_late[:12],
        total_late[12:24],
        total_late[24:36],
        total_late[36:84],
        total_late[84:],
    )
    return (
        hidden_out,
        input_grad,
        smalls[0],
        smalls[1],
        total_wqkv,
        smalls[2],
        total_wout,
        smalls[3],
        smalls[4],
        smalls[5],
        total_wfc,
        smalls[6],
        total_wproj,
        smalls[7],
    )


def solution(mesh):
    cut = Mesh(mesh.devices.reshape(2, GROUPS, 2), ("c", "g", "h"))
    tokens, rows, line = P(("c", "g", "h"), None), P(("c", "g"), None), P(("c", "g"))
    in_specs = (
        tokens, line, line, rows, line, rows, line, line, line, rows, line, rows, line, tokens,
    )
    out_specs = (
        tokens, tokens, line, line, rows, line, rows, line, line, line, rows, line, rows, line,
    )
    return jax.shard_map(
        on_device, mesh=cut, in_specs=in_specs, out_specs=out_specs, check_vma=False
    )
```

```python
import jax
import jax.numpy as jnp
from jax import lax
from jax.experimental import pallas as pl
from jax.experimental.pallas import tpu as pltpu
from jax.sharding import Mesh
from jax.sharding import PartitionSpec as P

D = 768
HEAD_DIM = 64
EPS = 1e-05
NEG = -1e30
LOG2E = 1.4426950408889634
F32 = jnp.float32
BF16 = jnp.bfloat16
HALF = 256
TALL = HALF + 32
CARGO = HALF + 96
GROUPS = 32
TOKENS = 16384
BLOCKS = 2 * GROUPS
LOCAL = 192
VMEM_BYTES = 56 * 1024 * 1024
TEAM = ("c", "h")
SWAP = [(0, 1), (1, 0)]
MIRROR = [(i, GROUPS - 1 - i) for i in range(GROUPS)]
MESH = pl.DeviceIdType.MESH
GELU_ROOT = 0.7978845608028654
GELU_CUBE = 0.044715
SMALL = (12, 12, 24, 12, 12, 12, 48, 12)


def matmul(left, right):
    return jnp.dot(left, right, preferred_element_type=F32)


def trans_left(left, right):
    return lax.dot_general(left, right, (((0,), (0,)), ((), ())), preferred_element_type=F32)


def trans_left_of(left, right):
    return lax.dot_general(left, right, (((0,), (1,)), ((), ())), preferred_element_type=F32)


def trans_right(left, right):
    return lax.dot_general(left, right, (((1,), (1,)), ((), ())), preferred_element_type=F32)


def layer_norm(values, gain, shift):
    mean = jnp.mean(values, axis=-1, keepdims=True)
    centred = values - mean
    spread = jnp.mean(centred * centred, axis=-1, keepdims=True)
    return centred * lax.rsqrt(spread + EPS) * gain + shift


def gelu_tanh(values):
    return jax.nn.gelu(values, approximate=True)


def nt(left, right):
    return lax.dot_general(left, right, (((1,), (1,)), ((), ())), preferred_element_type=F32)


def diagonal():
    key = lax.broadcasted_iota(jnp.int32, (HALF, HALF), 0)
    query = lax.broadcasted_iota(jnp.int32, (HALF, HALF), 1)
    return key <= query


def cat(parts, axis=0):
    return parts[0] if len(parts) == 1 else jnp.concatenate(parts, axis=axis)

def one_hot(rows, columns, row_of_column):
    row = lax.broadcasted_iota(jnp.int32, (rows, columns), 0)
    column = lax.broadcasted_iota(jnp.int32, (rows, columns), 1)
    return (row == row_of_column(column)).astype(BF16)


def lay(line, mask, put):
    top = line.astype(BF16).astype(F32)
    both = [jnp.where(mask > 0, jnp.broadcast_to(v, mask.shape), 0.0) for v in (top, line - top)]
    return sum(matmul(v.astype(BF16), put) for v in both)


def column_sum(value):
    return jnp.sum(value, axis=0, keepdims=True)


def team_peer(c, h, k):
    return lax.rem(c + k // 2, 2), lax.rem(h + k % 2, 2)


def greet(devices):
    barrier = pltpu.get_barrier_semaphore()
    for device in devices:
        pl.semaphore_signal(barrier, inc=1, device_id=device, device_id_type=MESH)
    pl.semaphore_wait(barrier, len(devices))


def send(src, dst, sems, slot, device):
    copy = pltpu.make_async_remote_copy(
        src_ref=src,
        dst_ref=dst,
        send_sem=sems.at[0, slot],
        recv_sem=sems.at[1, slot],
        device_id=device,
        device_id_type=MESH,
    )
    copy.start()
    return copy


def middle_kernel(
    att_ref,
    hid_ref,
    cot_ref,
    all_ref,
    places_ref,
    drop_ref,
    vec_ref,
    mask_ref,
    gain_ref,
    shift_ref,
    bias_ref,
    mask_fc_ref,
    put_fc_ref,
    grad_ref,
    late_ref,
    attended_ref,
    mid_parts_ref,
    mid_own_ref,
    out_parts_ref,
    out_own_ref,
    att,
    mid,
    work,
    low_own,
    z_out,
    z_in,
    w_out_ref,
    w_fc_ref,
    w_proj_ref,
    brought,
    norm_ref,
    grad_pre_ref,
    normed_ref,
    activ_ref,
    att_sems,
    z_sems,
    brought_sems,
):
    c, g, h = lax.axis_index("c"), lax.axis_index("g"), lax.axis_index("h")
    rank = 2 * c + h
    mirror = GROUPS - 1 - g
    peers = [team_peer(c, h, k) for k in range(4)]
    ranks = [2 * pc + ph for pc, ph in peers]
    team = [(pc, g, ph) for pc, ph in peers[1:]]
    across = [(pc, mirror, ph) for pc, ph in peers]
    fetches = []
    for k in range(6):
        at = HALF + 32 * k if k < 3 else CARGO + HALF + 32 * (k - 3)
        fetches.append(
            pltpu.make_async_copy(
                all_ref.at[:, pl.ds(at, 32), :], brought.at[k], brought_sems.at[k]
            )
        )
        fetches[k].start()
    greet(team + across)

    low, high = pl.ds(0, HALF), pl.ds(HALF, HALF)
    copies = [
        send(att_ref.at[low], att.at[rank, low], att_sems, k, device)
        for k, device in enumerate(team)
    ]
    copies += [
        send(att_ref.at[high], att.at[rank, high], att_sems, 3 + k, device)
        for k, device in enumerate(across)
    ]
    att[rank, low, :] = att_ref[low, :]

    for k, (put_ref, w_ref) in enumerate(
        ((places_ref, w_fc_ref), (places_ref, w_out_ref), (drop_ref, w_proj_ref))
    ):
        for half in (0, 1):
            fetches[2 * k + half].wait()
            block = brought[2 * k + half].reshape(1024, 384)
            w_ref[:, pl.ds(384 * half, 384)] = matmul(put_ref[...], block).astype(BF16)

    cotangent = cot_ref[...]
    thirds = [pl.ds(256 * k, 256) for k in range(3)]
    for part in thirds:
        work[:, part] = trans_right(cotangent, w_proj_ref[part, :])
    for copy in copies:
        copy.wait_recv()

    bias_out, gain, shift, bias_fc, bias_proj = (vec_ref[k : k + 1, :] for k in range(5))

    total = hid_ref[...].astype(F32) + bias_out
    for t in range(4):
        total += matmul(att[t], w_out_ref[pl.ds(LOCAL * t, LOCAL), :])
    mid[...] = total
    normed_ref[...] = layer_norm(total, gain, shift).astype(BF16)
    normed = normed_ref[...]
    for part in thirds:
        pre = matmul(normed, w_fc_ref[:, part]) + bias_fc[:, part.start : part.start + 256]
        square = pre * pre
        bend = jnp.tanh(GELU_ROOT * pre * (1.0 + GELU_CUBE * square))
        activ_ref[:, part] = (0.5 * pre * (1.0 + bend)).astype(BF16)
        slope = 0.5 * (1.0 + bend) + 0.5 * pre * (1.0 - bend * bend) * GELU_ROOT * (
            1.0 + 3.0 * GELU_CUBE * square
        )
        grad_pre_ref[:, part] = (work[:, part] * slope).astype(BF16)

    grad_pre = grad_pre_ref[...]
    for part in thirds:
        work[:, part] = trans_right(grad_pre, w_fc_ref[part, :])
    own = pl.ds(pl.multiple_of(128 * rank, 128), 128)
    norm_ref[...] = jnp.zeros_like(norm_ref)
    for t in range(4):
        rows = pl.ds(128 * t, 128)
        here = mid[rows, :]
        centred = here - jnp.mean(here, axis=-1, keepdims=True)
        scale = lax.rsqrt(jnp.mean(centred * centred, axis=-1, keepdims=True) + EPS)
        hat = centred * scale
        grad_norm = work[rows, :]
        norm_ref[0:1, :] += jnp.sum(grad_norm * hat, axis=0, keepdims=True)
        norm_ref[1:2, :] += jnp.sum(grad_norm, axis=0, keepdims=True)
        pull = grad_norm * gain
        pull = pull - jnp.mean(pull, axis=-1, keepdims=True)
        pull = pull - hat * jnp.mean(pull * hat, axis=-1, keepdims=True)
        work[rows, :] = scale * pull
    work[own, :] += cot_ref[own, :].astype(F32)

    part_low = work[...].astype(BF16)
    z_copies = []
    for k in (1, 2, 3, 0):
        w_rows = w_out_ref[pl.ds(pl.multiple_of(LOCAL * ranks[k], 16), LOCAL), :]
        z = trans_right(part_low, w_rows)
        z_out[k] = z.astype(BF16)
        if k:
            z_copies.append(send(z_out.at[k, low], z_in.at[k, low], z_sems, k, team[k - 1]))
        else:
            low_own[...] = z[:HALF]
        z_copies.append(send(z_out.at[k, high], z_in.at[k, high], z_sems, 4 + k, across[k]))

    mid_own_ref[...] = work[own, :]
    for k in (1, 2, 3):
        rows = pl.ds(pl.multiple_of(128 * ranks[k], 128), 128)
        mid_parts_ref[k] = work[rows, :].astype(BF16)
    activ = activ_ref[...]
    for part in thirds:
        work[:, part] = matmul(activ, w_proj_ref[:, part])
    out_own_ref[...] = mid[own, :] + bias_proj + work[own, :]
    for k in (1, 2, 3):
        rows = pl.ds(pl.multiple_of(128 * ranks[k], 128), 128)
        out_parts_ref[k] = work[rows, :].astype(BF16)
    mid_parts_ref[0] = jnp.zeros((128, D), BF16)
    out_parts_ref[0] = jnp.zeros((128, D), BF16)
    for t in range(4):
        attended_ref[t] = att[t]

    def weight_gradient(left, right, at):
        for j in range(4):
            block = trans_left(left[:, 256 * j : 256 * j + 256], right)
            late_ref[pl.ds(8 * j, 8), pl.ds(at, 32), :] = block.reshape(8, 32, D).astype(BF16)

    weight_gradient(matmul(normed_ref[...], places_ref[...]).astype(BF16), grad_pre_ref[...], 0)
    weight_gradient(matmul(activ, drop_ref[...]).astype(BF16), cot_ref[...], 32)
    mask = mask_ref[...]
    lines = (
        lay(norm_ref[0:1, :], mask, gain_ref[...])
        + lay(norm_ref[1:2, :], mask, shift_ref[...])
        + lay(column_sum(cot_ref[own, :].astype(F32)), mask, bias_ref[...])
        + lay(column_sum(grad_pre_ref[...].astype(F32)), mask_fc_ref[...], put_fc_ref[...])
    )
    for k in range(GROUPS):
        late_ref[k, pl.ds(48, 16), pl.ds(0, 128)] = jnp.concatenate(
            [
                late_ref[k, pl.ds(48, 16), pl.ds(0, 128)].astype(F32)[:8],
                jnp.broadcast_to(lines[k : k + 1], (8, 128)),
            ],
            axis=0,
        ).astype(BF16)
    for copy in z_copies:
        copy.wait_recv()
    grad_low = low_own[...]
    grad_high = z_in[0, high].astype(F32)
    for k in (1, 2, 3):
        grad_low += z_in[k, low].astype(F32)
        grad_high += z_in[k, high].astype(F32)
    grad_ref[low, :] = grad_low.astype(BF16)
    grad_ref[high, :] = grad_high.astype(BF16)
    for copy in copies + z_copies:
        copy.wait_send()


def middle(*args):
    def out(shape, dtype):
        return jax.ShapeDtypeStruct(shape, dtype)

    vmem = pl.BlockSpec(memory_space=pltpu.VMEM)
    outs = [
        out((512, LOCAL), BF16),
        out((GROUPS, 64, D), BF16),
        out((4, 512, LOCAL), BF16),
        out((4, 128, D), BF16),
        out((128, D), F32),
        out((4, 128, D), BF16),
        out((128, D), F32),
    ]
    return pl.pallas_call(
        middle_kernel,
        out_shape=outs,
        in_specs=[vmem] * 3 + [pl.BlockSpec(memory_space=pl.ANY)] + [vmem] * (len(args) - 4),
        out_specs=[vmem] * len(outs),
        scratch_shapes=[
            pltpu.VMEM((4, 512, LOCAL), BF16),
            pltpu.VMEM((512, D), F32),
            pltpu.VMEM((512, D), F32),
            pltpu.VMEM((HALF, LOCAL), F32),
            pltpu.VMEM((4, 512, LOCAL), BF16),
            pltpu.VMEM((4, 512, LOCAL), BF16),
            pltpu.VMEM((D, D), BF16),
            pltpu.VMEM((D, D), BF16),
            pltpu.VMEM((D, D), BF16),
            pltpu.VMEM((6, GROUPS, 32, 384), BF16),
            pltpu.VMEM((8, D), F32),
            pltpu.VMEM((512, D), BF16),
            pltpu.VMEM((512, D), BF16),
            pltpu.VMEM((512, D), BF16),
            pltpu.SemaphoreType.DMA((2, 7)),
            pltpu.SemaphoreType.DMA((2, 8)),
            pltpu.SemaphoreType.DMA((6,)),
        ],
        compiler_params=pltpu.CompilerParams(
            vmem_limit_bytes=VMEM_BYTES, collective_id=1, has_side_effects=True
        ),
        cost_estimate=pl.CostEstimate(
            flops=12 * 512 * D * D, bytes_accessed=16 * 512 * D, transcendentals=512 * D
        ),
    )(*args)


def wrap(value, size):
    return lax.rem(value + size, size)


class Plane:
    def __init__(self, c, g, h):
        self.c, self.g, self.h = c, g, h
        self.y, self.z, self.core = g // 8, (g // 2) % 4, g % 2

    def place(self, first, second, core):
        dz = first * (1 - core) + second * core
        dy = first * core + second * (1 - core)
        return 8 * wrap(self.y + dy, 4) + 2 * wrap(self.z + dz, 4) + core

    def device(self, first, second):
        return (self.c, self.place(first, second, self.core), self.h)

    def sibling(self):
        return (self.c, self.g + 1 - 2 * self.core, self.h)


def shift_of(index):
    return ((index + 1) % 3 + 1) * jnp.minimum(index, 1)


def travel(plane, held, near_sems, pair_sems, tall):
    def halves():
        return (pl.ds(0, tall), pl.ds(tall, tall))

    def source(d, e, core):
        return plane.place(shift_of(d), shift_of(e), core)

    def copy(n, half, slot, first, second):
        rows = halves()[half]
        return pltpu.make_async_remote_copy(
            src_ref=held.at[slot, rows],
            dst_ref=held.at[slot, rows],
            send_sem=near_sems.at[0, half, n],
            recv_sem=near_sems.at[1, half, n],
            device_id=plane.device(first, second),
            device_id_type=MESH,
        )

    def across(n, slot):
        return pltpu.make_async_remote_copy(
            src_ref=held.at[slot],
            dst_ref=held.at[slot],
            send_sem=pair_sems.at[0, n],
            recv_sem=pair_sems.at[1, n],
            device_id=plane.sibling(),
            device_id_type=MESH,
        )

    def each(n, act):
        d, e = n % 4, n // 4
        slot = source(d, e, plane.core)
        act(across(n, slot))

        @pl.when(n == 0)
        def _():
            for half in (0, 1):
                act(copy(1, half, slot, 1, 0))
                act(copy(2, half, slot, 3, 0))

        @pl.when(n == 1)
        def _():
            act(copy(3, 0, slot, 1, 0))

        @pl.when(n == 2)
        def _():
            act(copy(3, 1, slot, 3, 0))

        @pl.when(e == 0)
        def _():
            for half in (0, 1):
                act(copy(4 + d, half, slot, 0, 1))
                act(copy(8 + d, half, slot, 0, 3))

        @pl.when(e == 1)
        def _():
            act(copy(12 + d, 0, slot, 0, 1))

        @pl.when(e == 2)
        def _():
            act(copy(12 + d, 1, slot, 0, 3))

    def depart(n):
        each(n, lambda c: c.start())

    def arrive(n):
        for half in (0, 1):
            copy(n, half, source(n % 4, n // 4, plane.core), 0, 1).wait_recv()
        depart(n)

    def arrive_across(n):
        across(n, source(n % 4, n // 4, 1 - plane.core)).wait_recv()

    def finish():
        def sent(n, carry):
            each(n, lambda c: c.wait_send())
            return carry

        lax.fori_loop(0, 16, sent, 0)

    def place_of(n, other):
        return source(n % 4, n // 4, plane.core + other - 2 * plane.core * other)

    return depart, arrive, arrive_across, place_of, finish


def fused_forward_kernel(
    q_ref, kv_ref, cot_ref, att_ref, nat_ref, lse_ref, far_ref, cot_all_ref, all_ref,
    held, qz, upper, cot, top, total, accum, near_sems, pair_sems, upper_sems, team_sems, out_sems,
):
    c, g, h = lax.axis_index("c"), lax.axis_index("g"), lax.axis_index("h")
    plane = Plane(c, g, h)
    mirror = (c, GROUPS - 1 - g, h)
    rank = 2 * c + h
    team = [(pc, g, ph) for pc, ph in (team_peer(c, h, k) for k in (1, 2, 3))]
    greet(
        team
        + [plane.sibling(), plane.device(1, 0), plane.device(3, 0)]
        + [plane.device(0, 1), plane.device(0, 3), mirror]
    )
    swap = send(q_ref.at[pl.ds(HALF, HALF)], upper, upper_sems, 0, mirror)
    held[g] = kv_ref[...]
    depart, arrive, arrive_across, place_of, finish = travel(plane, held, near_sems, pair_sems, CARGO)
    top[...] = jnp.full_like(top, NEG)
    total[...] = jnp.zeros_like(total)
    accum[...] = jnp.zeros_like(accum)
    left = lax.broadcasted_iota(jnp.int32, (HALF, 128), 1) < 64

    def place_queries(slot, block):
        span = pl.ds(slot * HALF, HALF)
        pair = block[:, :128].astype(F32)
        qz[0, span, :] = jnp.where(left, pair, 0.0).astype(BF16)
        qz[1, span, :] = jnp.where(left, 0.0, pair).astype(BF16)
        qz[2, span, :] = jnp.concatenate(
            [block[:, 128:], jnp.zeros((HALF, 64), BF16)], axis=1
        )

    place_queries(0, q_ref[pl.ds(0, HALF), :])

    def tiles(device, units):
        chains = []
        for slot, halves, masked in units:
            span = pl.ds(slot * HALF, HALF)
            first, second, third = (
                cat([held[device, pl.ds(CARGO * x, HALF), pl.ds(128 * k, 128)] for x in halves])
                for k in range(3)
            )
            second_t, third_t = second.T, third.T
            values = (second_t[64:], third_t[:64], third_t[64:])
            for n, keys in enumerate((first, first, second)):
                scores = nt(keys, qz[n, span, :])
                if masked:
                    scores = jnp.where(diagonal(), scores, NEG)
                chains.append((slot, n, values[n], scores))
        ready = []
        for slot, n, value, scores in chains:
            line = pl.ds(8 * slot + n, 1)
            old = top[line, :]
            new = jnp.maximum(old, jnp.max(scores, axis=0, keepdims=True))
            weights = jnp.exp(scores - new)
            fade = jnp.exp(old - new)
            top[line, :] = new
            total[line, :] = total[line, :] * fade + jnp.sum(weights, axis=0, keepdims=True)
            ready.append((slot, n, value, weights.astype(BF16), fade))
        for slot, n, value, weights, fade in ready:
            accum[slot, n] = accum[slot, n] * fade + matmul(value, weights)

    def keep(slot):
        return pltpu.make_async_copy(held.at[slot], all_ref.at[slot], out_sems.at[slot])

    def work(device):
        keep(device).start()

        low, high = device < g, device < GROUPS - 1 - g

        @pl.when(low & high)
        def _():
            tiles(device, [(0, (0,), False), (1, (0, 1), False)])

        @pl.when(low & ~high)
        def _():
            tiles(device, [(0, (0,), False), (1, (0,), False)])

        @pl.when(~low & high)
        def _():
            tiles(device, [(1, (0, 1), False)])

        @pl.when(~low & ~high)
        def _():
            tiles(device, [(1, (0,), False)])

        @pl.when(device == g)
        def _():
            tiles(device, [(0, (0,), True)])

        @pl.when(device == GROUPS - 1 - g)
        def _():
            tiles(device, [(1, (1,), True)])

    lax.fori_loop(0, 1, lambda n, carry: (depart(n), carry)[1], 0)
    cot_copies = [send(cot_ref, cot.at[rank], team_sems, k, device) for k, device in enumerate(team)]
    swap.wait_recv()
    place_queries(1, upper[...])
    far_ref[pl.ds(0, HALF), :] = q_ref[pl.ds(0, HALF), :]
    far_ref[pl.ds(HALF, HALF), :] = upper[...]

    def step(m, carry):
        n, other = m // 2, m % 2

        @pl.when((other == 0) & (n > 0))
        def _():
            arrive(n)

        @pl.when(other == 1)
        def _():
            arrive_across(n)

        work(place_of(n, other))
        return carry

    lax.fori_loop(0, 32, step, 0)
    for slot in range(2):
        for n in range(3):
            line = pl.ds(8 * slot + n, 1)
            att_ref[slot, pl.ds(64 * n, 64), :] = accum[slot, n] / total[line, :]
        span = pl.ds(slot * HALF, HALF)
        nat_ref[span, :] = att_ref[slot].T.astype(BF16)
        lines = pl.ds(8 * slot, 8)
        lse_ref[:, span] = (top[lines, :] + jnp.log(jnp.maximum(total[lines, :], 1e-30))) * LOG2E
    cot[rank] = cot_ref[...]
    for copy in cot_copies:
        copy.wait_recv()
    for t in range(4):
        cot_all_ref[pl.ds(128 * t, 128), :] = cot[t]
    for copy in cot_copies + [swap]:
        copy.wait_send()
    finish()
    for slot in range(GROUPS):
        keep(slot).wait()


def fused_forward(*args):
    vmem = pl.BlockSpec(memory_space=pltpu.VMEM)
    return pl.pallas_call(
        fused_forward_kernel,
        out_shape=[
            jax.ShapeDtypeStruct((2, LOCAL, HALF), F32),
            jax.ShapeDtypeStruct((512, LOCAL), BF16),
            jax.ShapeDtypeStruct((8, 512), F32),
            jax.ShapeDtypeStruct((512, LOCAL), BF16),
            jax.ShapeDtypeStruct((512, D), BF16),
            jax.ShapeDtypeStruct((GROUPS, 2 * CARGO, 2 * LOCAL), BF16),
        ],
        in_specs=[vmem, vmem, vmem],
        out_specs=[vmem, vmem, vmem, vmem, vmem, pl.BlockSpec(memory_space=pl.ANY)],
        scratch_shapes=[
            pltpu.VMEM((GROUPS, 2 * CARGO, 2 * LOCAL), BF16),
            pltpu.VMEM((3, 512, 128), BF16),
            pltpu.VMEM((HALF, LOCAL), BF16),
            pltpu.VMEM((4, 128, D), BF16),
            pltpu.VMEM((16, HALF), F32),
            pltpu.VMEM((16, HALF), F32),
            pltpu.VMEM((2, 3, 64, HALF), F32),
            pltpu.SemaphoreType.DMA((2, 2, 16)),
            pltpu.SemaphoreType.DMA((2, 16)),
            pltpu.SemaphoreType.DMA((2, 1)),
            pltpu.SemaphoreType.DMA((2, 3)),
            pltpu.SemaphoreType.DMA((GROUPS,)),
        ],
        compiler_params=pltpu.CompilerParams(
            vmem_limit_bytes=VMEM_BYTES, collective_id=2, has_side_effects=True
        ),
        cost_estimate=pl.CostEstimate(
            flops=65 * 3 * HALF * HALF * 1024, bytes_accessed=32 << 20, transcendentals=65 * 3 * HALF * HALF
        ),
    )(*args)


def place_sides(first, second, span, block):
    left = lax.broadcasted_iota(jnp.int32, (HALF, 128), 1) < 64
    a, b, c = (block[:, 128 * k : 128 * k + 128].astype(F32) for k in range(3))
    for refs, n, part, side in (
        (first, 0, a, left),
        (first, 1, a, ~left),
        (first, 2, b, left),
        (second, 0, b, ~left),
        (second, 1, c, left),
        (second, 2, c, ~left),
    ):
        refs[n, span, :] = jnp.where(side, part, 0.0).astype(BF16)


def backward_kernel(
    q_ref, do_ref, att_ref, lse_ref, kv_ref, mid_parts_ref, mid_own_ref, out_parts_ref, out_own_ref,
    late_ref, dq_ref, dkv_ref, hidden_ref, grad_mid_ref, grad_attn_ref, late_all_ref,
    held, stats, qz, dz, kz, vz, acc_q, acc_k, acc_v, whole, mid_in, out_in, attn,
    pair_in, pair_sum, first_in, first_sum, second_in, late_all,
    near_sems, pair_sems, mid_sems, out_sems, attn_sems, late_sems, late_team_sems,
):
    c, g, h = lax.axis_index("c"), lax.axis_index("g"), lax.axis_index("h")
    plane = Plane(c, g, h)
    rank = 2 * c + h
    team = [(pc, g, ph) for pc, ph in (team_peer(c, h, k) for k in (1, 2, 3))]
    greet(
        team
        + [plane.sibling()]
        + [plane.device(k, 0) for k in (1, 2, 3)]
        + [plane.device(0, k) for k in (1, 2, 3)]
    )

    def late_copy(src, dst, slot, device):
        return pltpu.make_async_remote_copy(
            src_ref=src,
            dst_ref=dst,
            send_sem=late_sems.at[0, slot],
            recv_sem=late_sems.at[1, slot],
            device_id=device,
            device_id_type=MESH,
        )

    core = plane.core

    def block_at(first, second, core_of):
        return plane.place(first, second, core) + core_of - core

    pair_copies = [
        late_copy(
            late_ref.at[block_at(a, b, 1 - core)], pair_in.at[4 * b + a], 4 * b + a, plane.sibling()
        )
        for b in range(4)
        for a in range(4)
    ]
    first_copies = [
        late_copy(pair_sum.at[a], first_in.at[a], 16 + a, plane.device(a, 0)) for a in (1, 2, 3)
    ]
    second_copies = [
        late_copy(first_sum.at[b], second_in.at[b], 20 + b, plane.device(0, b)) for b in (1, 2, 3)
    ]
    late_team = [
        pltpu.make_async_remote_copy(
            src_ref=late_all.at[rank],
            dst_ref=late_all.at[rank],
            send_sem=late_team_sems.at[0, k],
            recv_sem=late_team_sems.at[1, k],
            device_id=team[k - 1],
            device_id_type=MESH,
        )
        for k in (1, 2, 3)
    ]
    mid_copies = [
        send(mid_parts_ref.at[k], mid_in.at[k], mid_sems, k, team[k - 1]) for k in (1, 2, 3)
    ]
    low_rows, high_rows = pl.ds(0, HALF), pl.ds(HALF, HALF)
    for slot, span in enumerate((low_rows, high_rows)):
        block = jnp.concatenate([q_ref[span, :], do_ref[span, :]], axis=1)
        held[g, pl.ds(TALL * slot, HALF), :] = block
        place_sides(qz, dz, span, block)
        grads = block[:, LOCAL:].astype(F32).T
        product = grads * att_ref[slot]
        delta = [jnp.sum(product[64 * n : 64 * n + 64], axis=0, keepdims=True) for n in range(3)]
        lines = jnp.concatenate([lse_ref[0:3, span], *delta, jnp.zeros((2, HALF), F32)], axis=0)
        stats[:, span] = lines
        head = lines.astype(BF16).astype(F32)
        body = (lines - head).astype(BF16).astype(F32)
        tail = lines - head - body
        packed = jnp.concatenate([head, body, tail, jnp.zeros_like(tail)], axis=0)
        held[g, pl.ds(TALL * slot + HALF, 32), pl.ds(0, HALF)] = packed.astype(BF16)
    depart, arrive, arrive_across, place_of, finish = travel(
        plane, held, near_sems, pair_sems, TALL
    )
    lax.fori_loop(0, 1, lambda n, carry: (depart(n), carry)[1], 0)
    for copy in pair_copies:
        copy.start()
    place_sides(kz, vz, low_rows, kv_ref[g, low_rows, :])
    place_sides(kz, vz, high_rows, kv_ref[GROUPS - 1 - g, pl.ds(CARGO, HALF), :])
    for ref in (acc_q, acc_k, acc_v):
        ref[...] = jnp.zeros_like(ref)

    def groups(block_of):
        return [block_of(pl.ds(128 * k, 128)) for k in range(3)]

    def query_tiles(device, units):
        chains = []
        for slot, halves, masked in units:
            span = pl.ds(slot * HALF, HALF)

            def rows_of(lanes):
                return cat([kv_ref[device, pl.ds(CARGO * x, HALF), lanes] for x in halves])

            a, b, c = groups(rows_of)
            a_t, b_t = a.T, b.T
            for n, (keys, values, keys_t) in enumerate(
                ((a, b, a_t[:64]), (a, c, a_t[64:]), (b, c, b_t[:64]))
            ):
                chains.append(
                    (slot, n, masked, keys_t, nt(keys, qz[n, span, :]), nt(values, dz[n, span, :]))
                )
        ready = []
        for slot, n, masked, keys_t, scores, pull in chains:
            span = pl.ds(slot * HALF, HALF)
            scores = scores * LOG2E - stats[pl.ds(n, 1), span]
            if masked:
                scores = jnp.where(diagonal(), scores, NEG)
            pull = pull - stats[pl.ds(3 + n, 1), span]
            ready.append((slot, n, keys_t, (jnp.exp2(scores) * pull).astype(BF16)))
        for slot, n, keys_t, grad in ready:
            acc_q[slot, n] += matmul(keys_t, grad)

    def key_tiles(device, units):
        chains = []
        for slot, halves, masked in units:
            span = pl.ds(slot * HALF, HALF)

            def rows_of(lanes):
                return cat([held[device, pl.ds(TALL * half, HALF), lanes] for half in halves])

            a, b, c = groups(rows_of)
            lines = cat(
                [
                    held[device, pl.ds(TALL * half + HALF, 32), pl.ds(0, HALF)].astype(F32)
                    for half in halves
                ],
                1,
            )
            lines = lines[0:8] + lines[8:16] + lines[16:24]
            for n, (queries, grads) in enumerate(((a, b), (a, c), (b, c))):
                chains.append(
                    (
                        slot,
                        n,
                        masked,
                        queries,
                        grads,
                        lines,
                        nt(kz[n, span, :], queries),
                        nt(vz[n, span, :], grads),
                    )
                )
        ready = []
        for slot, n, masked, queries, grads, lines, scores, pull in chains:
            scores = scores * LOG2E - lines[n : n + 1]
            if masked:
                scores = jnp.where(diagonal(), scores, NEG)
            weights = jnp.exp2(scores)
            pull = weights * (pull - lines[3 + n : 4 + n])
            ready.append((slot, n, queries, grads, weights.astype(BF16), pull.astype(BF16)))
        for slot, n, queries, grads, weights, pull in ready:
            acc_v[slot, n] += matmul(weights, grads)
            acc_k[slot, n] += matmul(pull, queries)

    def planned(src, dst, sems, k):
        return pltpu.make_async_remote_copy(
            src_ref=src,
            dst_ref=dst,
            send_sem=sems.at[0, k],
            recv_sem=sems.at[1, k],
            device_id=team[k - 1],
            device_id_type=MESH,
        )

    attn_copies = [planned(attn.at[rank], attn.at[rank], attn_sems, k) for k in (1, 2, 3)]
    out_copies = [planned(out_parts_ref.at[k], out_in.at[k], out_sems, k) for k in (1, 2, 3)]

    def step(m, carry):
        n, other = m // 2, m % 2

        @pl.when((other == 0) & (n > 0))
        def _():
            arrive(n)

        @pl.when(other == 1)
        def _():
            arrive_across(n)

        @pl.when(m == 6)
        def _():
            for copy in mid_copies:
                copy.wait_recv()
            grad_mid = mid_own_ref[...]
            for k in (1, 2, 3):
                grad_mid += mid_in[k].astype(F32)
            grad_mid_ref[...] = grad_mid
            attn[rank] = grad_mid.astype(BF16)
            for copy in attn_copies:
                copy.start()

        @pl.when(m == 12)
        def _():
            for copy in out_copies:
                copy.start()

        @pl.when(m == 4)
        def _():
            for copy in pair_copies:
                copy.wait_recv()
            for b in range(4):
                for a in range(4):
                    mine = late_ref[block_at(a, b, core)].astype(F32)
                    pair_sum[a, b] = (mine + pair_in[4 * a + b].astype(F32)).astype(BF16)
            for copy in first_copies:
                copy.start()

        @pl.when(m == 12)
        def _():
            for copy in first_copies:
                copy.wait_recv()
            for b in range(4):
                sofar = pair_sum[0, b].astype(F32)
                for a in (1, 2, 3):
                    sofar += first_in[a, b].astype(F32)
                first_sum[b] = sofar.astype(BF16)
            for copy in second_copies:
                copy.start()

        @pl.when(m == 18)
        def _():
            for copy in second_copies:
                copy.wait_recv()
            sofar = first_sum[0].astype(F32)
            for b in (1, 2, 3):
                sofar += second_in[b].astype(F32)
            late_all[rank] = sofar.astype(BF16)
            for copy in late_team:
                copy.start()

        def for_queries(which, carry):
            index = 2 * m + which
            device = place_of(index // 2, index % 2)
            low, high = device < g, device < GROUPS - 1 - g

            @pl.when(low & high)
            def _():
                query_tiles(device, [(0, (0,), False), (1, (0, 1), False)])

            @pl.when(low & ~high)
            def _():
                query_tiles(device, [(0, (0,), False), (1, (0,), False)])

            @pl.when(~low & high)
            def _():
                query_tiles(device, [(1, (0, 1), False)])

            @pl.when(~low & ~high)
            def _():
                query_tiles(device, [(1, (0,), False)])

            @pl.when(device == GROUPS - 1 - g)
            def _():
                query_tiles(device, [(1, (1,), True)])

            @pl.when(device == g)
            def _():
                query_tiles(device, [(0, (0,), True)])

            return carry

        def for_keys(which, carry):
            index = 2 * (m - 16) + which
            device = place_of(index // 2, index % 2)

            @pl.when(device > g)
            def _():
                key_tiles(device, [(0, (0, 1), False)])

            @pl.when(device < g)
            def _():
                key_tiles(device, [(0, (1,), False), (1, (1,), False)])

            @pl.when(device == g)
            def _():
                key_tiles(device, [(0, (0,), True), (1, (1,), True)])
                key_tiles(device, [(0, (1,), False)])

            return carry

        @pl.when(m < 16)
        def _():
            lax.fori_loop(0, 2, for_queries, 0)

        @pl.when(m >= 16)
        def _():
            lax.fori_loop(0, 2, for_keys, 0)

        return carry

    lax.fori_loop(0, 32, step, 0)
    left = lax.broadcasted_iota(jnp.int32, (HALF, 128), 1) < 64
    for slot, span in enumerate((low_rows, high_rows)):
        for n in range(3):
            whole[pl.ds(64 * n, 64), :] = acc_q[slot, n] * 0.125
        dq_ref[span, :] = whole[...].T.astype(BF16)
        for k, (one, two) in enumerate(
            (
                (acc_k[slot, 0], acc_k[slot, 1]),
                (acc_k[slot, 2], acc_v[slot, 0]),
                (acc_v[slot, 1], acc_v[slot, 2]),
            )
        ):
            dkv_ref[span, pl.ds(128 * k, 128)] = jnp.where(left, one, two).astype(BF16)
    for copy in attn_copies + out_copies + late_team:
        copy.wait_recv()
    late_all_ref[...] = late_all[...]
    for t in range(4):
        grad_attn_ref[pl.ds(128 * t, 128), :] = attn[t]
    output = out_own_ref[...]
    for k in (1, 2, 3):
        output += out_in[k].astype(F32)
    hidden_ref[...] = output.astype(BF16)
    for copy in mid_copies + attn_copies + out_copies:
        copy.wait_send()
    for copy in pair_copies + first_copies + second_copies + late_team:
        copy.wait_send()
    finish()


def backward(*args):
    vmem = pl.BlockSpec(memory_space=pltpu.VMEM)
    sides_shape = pltpu.VMEM((3, 512, 128), BF16)
    return pl.pallas_call(
        backward_kernel,
        out_shape=[
            jax.ShapeDtypeStruct((512, LOCAL), BF16),
            jax.ShapeDtypeStruct((512, 2 * LOCAL), BF16),
            jax.ShapeDtypeStruct((128, D), BF16),
            jax.ShapeDtypeStruct((128, D), F32),
            jax.ShapeDtypeStruct((512, D), BF16),
            jax.ShapeDtypeStruct((4, 64, D), BF16),
        ],
        in_specs=[vmem] * len(args),
        out_specs=[vmem] * 6,
        scratch_shapes=[
            pltpu.VMEM((GROUPS, 2 * TALL, 2 * LOCAL), BF16),
            pltpu.VMEM((8, 512), F32),
            sides_shape,
            sides_shape,
            sides_shape,
            sides_shape,
            pltpu.VMEM((2, 3, 64, HALF), F32),
            pltpu.VMEM((2, 3, HALF, 128), F32),
            pltpu.VMEM((2, 3, HALF, 128), F32),
            pltpu.VMEM((LOCAL, HALF), F32),
            pltpu.VMEM((4, 128, D), BF16),
            pltpu.VMEM((4, 128, D), BF16),
            pltpu.VMEM((4, 128, D), BF16),
            pltpu.VMEM((16, 64, D), BF16),
            pltpu.VMEM((4, 4, 64, D), BF16),
            pltpu.VMEM((4, 4, 64, D), BF16),
            pltpu.VMEM((4, 64, D), BF16),
            pltpu.VMEM((4, 64, D), BF16),
            pltpu.VMEM((4, 64, D), BF16),
            pltpu.SemaphoreType.DMA((2, 2, 16)),
            pltpu.SemaphoreType.DMA((2, 16)),
            pltpu.SemaphoreType.DMA((2, 4)),
            pltpu.SemaphoreType.DMA((2, 4)),
            pltpu.SemaphoreType.DMA((2, 4)),
            pltpu.SemaphoreType.DMA((2, 24)),
            pltpu.SemaphoreType.DMA((2, 4)),
        ],
        compiler_params=pltpu.CompilerParams(
            vmem_limit_bytes=VMEM_BYTES, collective_id=3, has_side_effects=True
        ),
        cost_estimate=pl.CostEstimate(
            flops=65 * 3 * HALF * HALF * 3584,
            bytes_accessed=32 << 20,
            transcendentals=2 * 65 * 3 * HALF * HALF,
        ),
    )(*args)


def head_kernel(
    hid_ref, mine_ref, theirs_ref, mine_two_ref, theirs_two_ref, hid_all_ref, first_ref, second_ref,
    hid, other, other_two, held, team_sems, near_sems, pair_sems,
):
    c, g, h = lax.axis_index("c"), lax.axis_index("g"), lax.axis_index("h")
    rank = 2 * c + h
    plane = Plane(c, g, h)
    team = [(pc, g, ph) for pc, ph in (team_peer(c, h, k) for k in (1, 2, 3))]
    greet(
        team
        + [plane.sibling(), plane.device(1, 0), plane.device(3, 0)]
        + [plane.device(0, 1), plane.device(0, 3)]
    )
    swaps = [
        send(theirs_ref, other, team_sems, 3, team[1]),
        send(theirs_two_ref, other_two, team_sems, 4, team[1]),
    ]
    copies = [send(hid_ref, hid.at[rank], team_sems, k, device) for k, device in enumerate(team)]
    own_rows = pl.ds(pl.multiple_of(16 * c, 16), 16)
    other_rows = pl.ds(pl.multiple_of(16 - 16 * c, 16), 16)
    held[g, own_rows, :] = mine_ref[...]
    second_ref[own_rows, :] = mine_two_ref[...]
    swaps[0].wait_recv()
    held[g, other_rows, :] = other[...]
    depart, arrive, arrive_across, place_of, finish = travel(plane, held, near_sems, pair_sems, 16)
    lax.fori_loop(0, 1, lambda n, carry: (depart(n), carry)[1], 0)
    lax.fori_loop(1, 16, lambda n, carry: (arrive(n), carry)[1], 0)
    hid[rank] = hid_ref[...]
    for copy in copies:
        copy.wait_recv()
    for t in range(4):
        hid_all_ref[pl.ds(128 * t, 128), :] = hid[t]
    swaps[1].wait_recv()
    second_ref[other_rows, :] = other_two[...]
    lax.fori_loop(0, 16, lambda n, carry: (arrive_across(n), carry)[1], 0)
    first_ref[...] = held[...]
    for copy in copies + swaps:
        copy.wait_send()
    finish()


def head(*args):
    vmem = pl.BlockSpec(memory_space=pltpu.VMEM)
    return pl.pallas_call(
        head_kernel,
        out_shape=[
            jax.ShapeDtypeStruct((512, D), BF16),
            jax.ShapeDtypeStruct((GROUPS, 32, 640), BF16),
            jax.ShapeDtypeStruct((32, 2 * D), BF16),
        ],
        in_specs=[vmem] * 5,
        out_specs=[vmem] * 3,
        scratch_shapes=[
            pltpu.VMEM((4, 128, D), BF16),
            pltpu.VMEM((16, 640), BF16),
            pltpu.VMEM((16, 2 * D), BF16),
            pltpu.VMEM((GROUPS, 32, 640), BF16),
            pltpu.SemaphoreType.DMA((2, 5)),
            pltpu.SemaphoreType.DMA((2, 2, 16)),
            pltpu.SemaphoreType.DMA((2, 16)),
        ],
        compiler_params=pltpu.CompilerParams(
            vmem_limit_bytes=VMEM_BYTES, collective_id=4, has_side_effects=True
        ),
        cost_estimate=pl.CostEstimate(flops=0, bytes_accessed=4 << 20, transcendentals=0),
    )(*args)


def tail_kernel(
    dq_ref, dkv_ref, wq_ref, wkv_ref, norm_t_ref, att_t_ref, attn_ref, attn_own_ref, hid_ref, mid_ref,
    vec_ref, mask_ref, gain_ref, shift_ref, bias_ref, mask_q_ref, put_q_ref, mask_kv_ref, put_kv_ref,
    grad_ref, total_ref, small_ref,
    up_q, up_kv, part, part_out, part_in, out, into, small_out, small_in, team_small, gathered,
    swap_sems, part_sems, out_sems, small_sems, gather_sems, last_sems,
):
    c, g, h = lax.axis_index("c"), lax.axis_index("g"), lax.axis_index("h")
    rank = 2 * c + h
    peers = [team_peer(c, h, k) for k in range(4)]
    team = [(pc, g, ph) for pc, ph in peers[1:]]

    def other(k):
        return (c, lax.rem(g + k, GROUPS), h)

    barrier = pltpu.get_barrier_semaphore()

    def hello(k, carry):
        pl.semaphore_signal(barrier, inc=1, device_id=other(k), device_id_type=MESH)
        return carry

    lax.fori_loop(1, GROUPS, hello, 0)
    for device in team:
        pl.semaphore_signal(barrier, inc=1, device_id=device, device_id_type=MESH)
    pl.semaphore_wait(barrier, GROUPS + 2)

    low, high = pl.ds(0, HALF), pl.ds(HALF, HALF)
    mirror = (c, GROUPS - 1 - g, h)
    swaps = [
        send(dq_ref.at[high], up_q, swap_sems, 0, mirror),
        send(dkv_ref.at[high], up_kv, swap_sems, 1, mirror),
    ]
    dq_low, dkv_low = dq_ref[low, :], dkv_ref[low, :]
    part[low, :] = matmul(dq_low, wq_ref[...]) + matmul(dkv_low, wkv_ref[...])
    for swap in swaps:
        swap.wait_recv()
    dq_high, dkv_high = up_q[...], up_kv[...]
    part[high, :] = matmul(dq_high, wq_ref[...]) + matmul(dkv_high, wkv_ref[...])
    part_copies = []
    for k, (pc, ph) in enumerate(peers):
        if k:
            rows = pl.ds(pl.multiple_of(128 * (2 * pc + ph), 128), 128)
            part_out[k] = part[rows, :].astype(BF16)
            part_copies.append(send(part_out.at[k], part_in.at[k], part_sems, k, team[k - 1]))

    for j in range(4):
        rows = pl.ds(256 * j, 256)
        before, after = norm_t_ref[rows, low], norm_t_ref[rows, high]
        kv = matmul(before, dkv_low) + matmul(after, dkv_high)
        q = matmul(before, dq_low) + matmul(after, dq_high)
        span = pl.ds(8 * j, 8)
        out[span, :, pl.ds(0, 2 * LOCAL)] = kv.reshape(8, 32, 2 * LOCAL).astype(BF16)
        both = jnp.concatenate([q, matmul(att_t_ref[rows, :], attn_ref[...])], axis=1)
        out[span, :, pl.ds(2 * LOCAL, 2 * LOCAL)] = both.reshape(8, 32, 2 * LOCAL).astype(BF16)

    def out_copy(k):
        return pltpu.make_async_remote_copy(
            src_ref=out.at[lax.rem(g + k, GROUPS)],
            dst_ref=into.at[k],
            send_sem=out_sems.at[0, k],
            recv_sem=out_sems.at[1, k],
            device_id=other(k),
            device_id_type=MESH,
        )

    def small_copy(k):
        return pltpu.make_async_remote_copy(
            src_ref=small_out.at[lax.rem(g + k, GROUPS)],
            dst_ref=small_in.at[k],
            send_sem=small_sems.at[0, k],
            recv_sem=small_sems.at[1, k],
            device_id=other(k),
            device_id_type=MESH,
        )

    def for_others(act):
        lax.fori_loop(1, GROUPS, lambda k, carry: (act(k), carry)[1], 0)

    for_others(lambda k: out_copy(k).start())

    own = pl.ds(pl.multiple_of(128 * rank, 128), 128)
    for copy in part_copies:
        copy.wait_recv()
    grad_norm = part[own, :]
    for k in (1, 2, 3):
        grad_norm += part_in[k].astype(F32)
    resid = hid_ref[...].astype(F32)
    centred = resid - jnp.mean(resid, axis=-1, keepdims=True)
    scale = lax.rsqrt(jnp.mean(centred * centred, axis=-1, keepdims=True) + EPS)
    hat = centred * scale
    pull = grad_norm * vec_ref[0:1, :]
    pull = pull - jnp.mean(pull, axis=-1, keepdims=True)
    pull = pull - hat * jnp.mean(pull * hat, axis=-1, keepdims=True)
    grad_ref[...] = mid_ref[...] + scale * pull

    sum_q = column_sum(dq_low.astype(F32)) + column_sum(dq_high.astype(F32))
    sum_kv = column_sum(dkv_low.astype(F32)) + column_sum(dkv_high.astype(F32))
    lines = (
        lay(column_sum(grad_norm * hat), mask_ref[...], gain_ref[...])
        + lay(column_sum(grad_norm), mask_ref[...], shift_ref[...])
        + lay(column_sum(attn_own_ref[...].astype(F32)), mask_ref[...], bias_ref[...])
        + lay(sum_q, mask_q_ref[...], put_q_ref[...])
        + lay(sum_kv, mask_kv_ref[...], put_kv_ref[...])
    )
    for k in range(GROUPS):
        small_out[k] = jnp.broadcast_to(lines[k : k + 1], (8, 128))
    for_others(lambda k: small_copy(k).start())

    for_others(lambda k: out_copy(k).wait_recv())
    total = lax.fori_loop(
        1, GROUPS, lambda k, sofar: sofar + into[k].astype(F32), out[g].astype(F32)
    )
    gathered[rank] = total.astype(BF16)
    gather_copies = [
        send(gathered.at[rank], gathered.at[rank], gather_sems, k, device)
        for k, device in enumerate(team)
    ]
    for_others(lambda k: small_copy(k).wait_recv())
    team_small[rank] = lax.fori_loop(
        1, GROUPS, lambda k, sofar: sofar + small_in[k], small_out[g]
    )
    last_copies = [
        send(team_small.at[rank], team_small.at[rank], last_sems, k, device)
        for k, device in enumerate(team)
    ]
    for copy in gather_copies + last_copies:
        copy.wait_recv()
    total_ref[...] = gathered[...]
    small_ref[...] = team_small[0] + team_small[1] + team_small[2] + team_small[3]
    for copy in swaps + part_copies + gather_copies + last_copies:
        copy.wait_send()
    for_others(lambda k: out_copy(k).wait_send())
    for_others(lambda k: small_copy(k).wait_send())


def tail(*args):
    vmem = pl.BlockSpec(memory_space=pltpu.VMEM)
    dma = pltpu.SemaphoreType.DMA
    return pl.pallas_call(
        tail_kernel,
        out_shape=[
            jax.ShapeDtypeStruct((128, D), F32),
            jax.ShapeDtypeStruct((4, 32, 4 * LOCAL), BF16),
            jax.ShapeDtypeStruct((8, 128), F32),
        ],
        in_specs=[vmem] * len(args),
        out_specs=[vmem] * 3,
        scratch_shapes=[
            pltpu.VMEM((HALF, LOCAL), BF16),
            pltpu.VMEM((HALF, 2 * LOCAL), BF16),
            pltpu.VMEM((512, D), F32),
            pltpu.VMEM((4, 128, D), BF16),
            pltpu.VMEM((4, 128, D), BF16),
            pltpu.VMEM((GROUPS, 32, 4 * LOCAL), BF16),
            pltpu.VMEM((GROUPS, 32, 4 * LOCAL), BF16),
            pltpu.VMEM((GROUPS, 8, 128), F32),
            pltpu.VMEM((GROUPS, 8, 128), F32),
            pltpu.VMEM((4, 8, 128), F32),
            pltpu.VMEM((4, 32, 4 * LOCAL), BF16),
            dma((2, 2)),
            dma((2, 4)),
            dma((2, GROUPS)),
            dma((2, GROUPS)),
            dma((2, 3)),
            dma((2, 3)),
        ],
        compiler_params=pltpu.CompilerParams(
            vmem_limit_bytes=VMEM_BYTES, collective_id=5, has_side_effects=True
        ),
        cost_estimate=pl.CostEstimate(
            flops=4 * 512 * D * 3 * LOCAL, bytes_accessed=8 << 20, transcendentals=0
        ),
    )(*args)


def padded_feature(column):
    g, c, r = column // 32, (column // 16) % 2, column % 16
    return jnp.where(r < 12, 12 * (GROUPS * c + g) + r, -1)


def on_device(
    hidden_in,
    ln1_gain,
    ln1_shift,
    w_qkv,
    qv_bias,
    w_out,
    out_bias,
    ln2_gain,
    ln2_shift,
    w_fc,
    fc_bias,
    w_proj,
    proj_bias,
    out_grad,
):
    c, g, h = lax.axis_index("c"), lax.axis_index("g"), lax.axis_index("h")
    rank = 2 * c + h

    spread_places = one_hot(D, 1024, padded_feature)
    drop_pad = one_hot(D, 1024, lambda k: jnp.where(k % 32 < 24, 24 * (k // 32) + k % 32, -1))
    pick_units = one_hot(1536, D, lambda k: 48 * (k // 24) + 24 * h + k % 24)
    small = jnp.concatenate(
        [ln1_gain, ln1_shift, qv_bias, out_bias, ln2_gain, ln2_shift, fc_bias, proj_bias]
    )
    small = jnp.pad(small.reshape(12, 12), ((0, 0), (0, 52)))
    units = matmul(jnp.concatenate([w_fc[:, :1536], w_fc[:, 1536:]], axis=0), pick_units)
    units = units.astype(BF16)

    def columns_for(of_c):
        r = 2 * of_c + h
        qkv = [lax.dynamic_slice_in_dim(w_qkv, D * k + LOCAL * r, LOCAL, 1) for k in range(3)]
        fc = lax.dynamic_slice_in_dim(units, 12 * of_c, 12, 0)
        parts = (jnp.concatenate([*qkv, small], axis=1), jnp.concatenate([fc, w_out], axis=1))
        return tuple(jnp.pad(p, ((0, 4), (0, 0))) for p in parts)

    mine, theirs = columns_for(c), columns_for(1 - c)
    tokens, first, second = head(hidden_in, mine[0], theirs[0], mine[1], theirs[1])
    resid = tokens.astype(F32)
    proj_rows = lax.dynamic_slice_in_dim(w_proj, 24 * h, 24, 0)
    cargo = jnp.concatenate([second, jnp.pad(proj_rows, ((0, 8), (0, 0)))], axis=1)
    cargo = [cargo[:, 384 * k : 384 * k + 384] for k in range(6)]
    first = first.reshape(1024, 640)
    w_qkv_t = matmul(spread_places, first[:, : 3 * LOCAL]).astype(BF16)

    vectors = first[:, 3 * LOCAL : 3 * LOCAL + 12].reshape(GROUPS, 2, 16, 12)[:, :, :12]
    vectors = vectors.reshape(GROUPS, 2, 144).astype(F32)
    vectors = vectors.transpose(1, 0, 2)
    cut, at = [], 0
    for width in SMALL:
        cut.append(vectors[:, :, at : at + width])
        at += width
    gain_one, shift_one, bias_qv, bias_out, gain_two, shift_two = (
        v.reshape(-1) for v in cut[:6]
    )
    bias_proj = cut[7].reshape(-1)
    bias_fc = lax.dynamic_slice_in_dim(
        lax.dynamic_index_in_dim(cut[6], c, 0, False), 24 * h, 24, 1
    ).reshape(-1)
    bias_q = lax.dynamic_slice_in_dim(bias_qv, LOCAL * rank, LOCAL, 0)
    bias_v = lax.dynamic_slice_in_dim(bias_qv, D + LOCAL * rank, LOCAL, 0)
    bias_here = jnp.concatenate([bias_q, jnp.zeros_like(bias_q), bias_v])

    normed1 = layer_norm(resid, gain_one, shift_one).astype(BF16)
    qkv = (matmul(normed1, w_qkv_t) + bias_here).astype(BF16)
    queries = qkv[:, :LOCAL] * jnp.asarray(0.125, BF16)
    keys_values = qkv[:, LOCAL:]
    load = jnp.concatenate(
        [keys_values[:HALF], *cargo[:3], keys_values[HALF:], *cargo[3:]], axis=0
    )
    att_t, attended_zz, lse, query_far, cotangent, kv_all = fused_forward(queries, load, out_grad)

    def ones(rows, columns, test):
        row = lax.broadcasted_iota(jnp.int32, (rows, columns), 0)
        column = lax.broadcasted_iota(jnp.int32, (rows, columns), 1)
        return test(row, column)

    def mask(columns, group_of):
        return ones(GROUPS, columns, lambda r, k: r == group_of(k)).astype(F32)

    def put(rows, lane_of):
        return ones(rows, 128, lambda k, lane: lane == lane_of(k)).astype(BF16)

    by_feature = mask(D, lambda k: (k // 12) % GROUPS)
    at_gain = put(D, lambda k: 12 * (k // 384) + k % 12)
    at_shift = put(D, lambda k: 24 + 12 * (k // 384) + k % 12)
    vec = jnp.stack([bias_out, gain_two, shift_two, bias_fc, bias_proj])
    (
        grad_zz,
        late,
        attended,
        mid_parts,
        mid_own,
        out_parts,
        out_own,
    ) = middle(
        attended_zz,
        tokens,
        cotangent,
        kv_all,
        spread_places,
        drop_pad,
        jnp.concatenate([vec, jnp.zeros((3, D), F32)], axis=0),
        by_feature,
        at_gain,
        at_shift,
        put(D, lambda k: 48 + 12 * (k // 384) + k % 12),
        mask(D, lambda k: k // 24),
        put(D, lambda k: 72 + k % 24),
    )
    attended = jnp.concatenate([attended[t] for t in range(4)], axis=1)
    dq, dkv, hidden_out, grad_mid, grad_attn, late = backward(
        query_far, grad_zz, att_t, lse, kv_all, mid_parts, mid_own, out_parts, out_own, late
    )

    normed1_t = trans_left_of(spread_places, normed1).astype(BF16)
    w_back = w_qkv_t.T
    input_grad, total_qkv, total_first = tail(
        dq,
        dkv,
        w_back[:LOCAL],
        w_back[LOCAL:],
        normed1_t,
        trans_left_of(spread_places, attended).astype(BF16),
        lax.dynamic_slice_in_dim(grad_attn, LOCAL * rank, LOCAL, 1),
        lax.dynamic_slice_in_dim(grad_attn, 128 * rank, 128, 0),
        hidden_in,
        grad_mid,
        jnp.concatenate([gain_one[None], jnp.zeros((7, D), F32)], axis=0),
        by_feature,
        at_gain,
        at_shift,
        put(D, lambda k: 96 + 12 * (k // 384) + k % 12),
        mask(LOCAL, lambda k: 8 * rank + k // 24),
        put(LOCAL, lambda k: 48 + k % 24),
        mask(2 * LOCAL, lambda k: jnp.where(k < LOCAL, -1, 8 * rank + (k - LOCAL) // 24)),
        put(2 * LOCAL, lambda k: 72 + k % 24),
    )

    fc_rows = lax.dynamic_slice_in_dim(late, 16 * c, 16, 1)[:, :12].astype(F32)
    total_wfc = fc_rows.reshape(2, 2, 12, GROUPS, 24).transpose(2, 0, 3, 1, 4).reshape(12, 3072)
    of_c = lax.dynamic_slice_in_dim(late, 2 * c, 2, 0).astype(F32)
    total_wproj = of_c[:, 32:56].reshape(48, D)
    total_fc = of_c[:, 56, 72:96].reshape(48)
    total_late = jnp.sum(late[:, 56, :72].astype(F32), axis=0)

    def late_part(at):
        return lax.dynamic_slice_in_dim(total_late, at + 12 * c, 12, 0)

    qkv_rows = lax.dynamic_slice_in_dim(total_qkv, 16 * c, 16, 1)[:, :12].astype(F32)
    total_wqkv = jnp.concatenate(
        [qkv_rows[t, :, at : at + LOCAL] for at in (2 * LOCAL, 0, LOCAL) for t in range(4)], axis=1
    )

    total_wout = jnp.concatenate([qkv_rows[t, :, 3 * LOCAL :] for t in range(4)], axis=1)

    def first_part(at, width):
        return lax.dynamic_slice_in_dim(total_first[0], at + width * c, width, 0)

    smalls = (
        first_part(0, 12),
        first_part(24, 12),
        first_part(48, 24),
        first_part(96, 12),
        late_part(0),
        late_part(24),
        total_fc,
        late_part(48),
    )
    return (
        hidden_out,
        input_grad,
        smalls[0],
        smalls[1],
        total_wqkv,
        smalls[2],
        total_wout,
        smalls[3],
        smalls[4],
        smalls[5],
        total_wfc,
        smalls[6],
        total_wproj,
        smalls[7],
    )


def solution(mesh):
    cut = Mesh(mesh.devices.reshape(2, GROUPS, 2), ("c", "g", "h"))
    tokens, rows, line = P(("c", "g", "h"), None), P(("c", "g"), None), P(("c", "g"))
    in_specs = (
        tokens, line, line, rows, line, rows, line, line, line, rows, line, rows, line, tokens,
    )
    out_specs = (
        tokens, tokens, line, line, rows, line, rows, line, line, line, rows, line, rows, line,
    )
    return jax.shard_map(
        on_device, mesh=cut, in_specs=in_specs, out_specs=out_specs, check_vma=False
    )
```

```python
import jax
import jax.numpy as jnp
from jax import lax
from jax.experimental import pallas as pl
from jax.experimental.pallas import tpu as pltpu
from jax.sharding import Mesh
from jax.sharding import PartitionSpec as P

D = 768
HEAD_DIM = 64
EPS = 1e-05
NEG = -1e30
LOG2E = 1.4426950408889634
F32 = jnp.float32
BF16 = jnp.bfloat16
HALF = 256
TALL = HALF + 32
CARGO = HALF + 96
GROUPS = 32
TOKENS = 16384
BLOCKS = 2 * GROUPS
LOCAL = 192
VMEM_BYTES = 56 * 1024 * 1024
TEAM = ("c", "h")
SWAP = [(0, 1), (1, 0)]
MIRROR = [(i, GROUPS - 1 - i) for i in range(GROUPS)]
MESH = pl.DeviceIdType.MESH
GELU_ROOT = 0.7978845608028654
GELU_CUBE = 0.044715
SMALL = (12, 12, 24, 12, 12, 12, 48, 12)


def matmul(left, right):
    return jnp.dot(left, right, preferred_element_type=F32)


def trans_left(left, right):
    return lax.dot_general(left, right, (((0,), (0,)), ((), ())), preferred_element_type=F32)


def trans_left_of(left, right):
    return lax.dot_general(left, right, (((0,), (1,)), ((), ())), preferred_element_type=F32)


def trans_right(left, right):
    return lax.dot_general(left, right, (((1,), (1,)), ((), ())), preferred_element_type=F32)


def layer_norm(values, gain, shift):
    mean = jnp.mean(values, axis=-1, keepdims=True)
    centred = values - mean
    spread = jnp.mean(centred * centred, axis=-1, keepdims=True)
    return centred * lax.rsqrt(spread + EPS) * gain + shift


def gelu_tanh(values):
    return jax.nn.gelu(values, approximate=True)


def nt(left, right):
    return lax.dot_general(left, right, (((1,), (1,)), ((), ())), preferred_element_type=F32)


def diagonal():
    key = lax.broadcasted_iota(jnp.int32, (HALF, HALF), 0)
    query = lax.broadcasted_iota(jnp.int32, (HALF, HALF), 1)
    return key <= query


def cat(parts, axis=0):
    return parts[0] if len(parts) == 1 else jnp.concatenate(parts, axis=axis)

def one_hot(rows, columns, row_of_column):
    row = lax.broadcasted_iota(jnp.int32, (rows, columns), 0)
    column = lax.broadcasted_iota(jnp.int32, (rows, columns), 1)
    return (row == row_of_column(column)).astype(BF16)


def lay(line, mask, put):
    top = line.astype(BF16).astype(F32)
    both = [jnp.where(mask > 0, jnp.broadcast_to(v, mask.shape), 0.0) for v in (top, line - top)]
    return sum(matmul(v.astype(BF16), put) for v in both)


def column_sum(value):
    return jnp.sum(value, axis=0, keepdims=True)


def team_peer(c, h, k):
    return lax.rem(c + k // 2, 2), lax.rem(h + k % 2, 2)


def greet(devices):
    barrier = pltpu.get_barrier_semaphore()
    for device in devices:
        pl.semaphore_signal(barrier, inc=1, device_id=device, device_id_type=MESH)
    pl.semaphore_wait(barrier, len(devices))


def send(src, dst, sems, slot, device):
    copy = pltpu.make_async_remote_copy(
        src_ref=src,
        dst_ref=dst,
        send_sem=sems.at[0, slot],
        recv_sem=sems.at[1, slot],
        device_id=device,
        device_id_type=MESH,
    )
    copy.start()
    return copy


def middle_kernel(
    att_ref,
    hid_ref,
    cot_ref,
    all_ref,
    places_ref,
    drop_ref,
    vec_ref,
    mask_ref,
    gain_ref,
    shift_ref,
    bias_ref,
    mask_fc_ref,
    put_fc_ref,
    grad_ref,
    late_ref,
    attended_ref,
    mid_parts_ref,
    mid_own_ref,
    out_parts_ref,
    out_own_ref,
    far_ref,
    att,
    mid,
    work,
    low_own,
    z_out,
    z_in,
    w_out_ref,
    w_fc_ref,
    w_proj_ref,
    brought,
    norm_ref,
    grad_pre_ref,
    normed_ref,
    activ_ref,
    far,
    att_sems,
    z_sems,
    brought_sems,
    far_sems,
):
    c, g, h = lax.axis_index("c"), lax.axis_index("g"), lax.axis_index("h")
    rank = 2 * c + h
    mirror = GROUPS - 1 - g
    peers = [team_peer(c, h, k) for k in range(4)]
    ranks = [2 * pc + ph for pc, ph in peers]
    team = [(pc, g, ph) for pc, ph in peers[1:]]
    across = [(pc, mirror, ph) for pc, ph in peers]
    fetches = []
    for k in range(6):
        at = HALF + 32 * k if k < 3 else CARGO + HALF + 32 * (k - 3)
        fetches.append(
            pltpu.make_async_copy(
                all_ref.at[:, pl.ds(at, 32), :], brought.at[k], brought_sems.at[k]
            )
        )
        fetches[k].start()
    greet(team + across)

    low, high = pl.ds(0, HALF), pl.ds(HALF, HALF)
    copies = [
        send(att_ref.at[low], att.at[rank, low], att_sems, k, device)
        for k, device in enumerate(team)
    ]
    copies += [
        send(att_ref.at[high], att.at[rank, high], att_sems, 3 + k, device)
        for k, device in enumerate(across)
    ]
    far_copy = send(hid_ref.at[high], far, far_sems, 0, across[0])
    att[rank, low, :] = att_ref[low, :]

    for k, (put_ref, w_ref) in enumerate(
        ((places_ref, w_fc_ref), (places_ref, w_out_ref), (drop_ref, w_proj_ref))
    ):
        for half in (0, 1):
            fetches[2 * k + half].wait()
            block = brought[2 * k + half].reshape(1024, 384)
            w_ref[:, pl.ds(384 * half, 384)] = matmul(put_ref[...], block).astype(BF16)

    cotangent = cot_ref[...]
    thirds = [pl.ds(256 * k, 256) for k in range(3)]
    for part in thirds:
        work[:, part] = trans_right(cotangent, w_proj_ref[part, :])
    for copy in copies:
        copy.wait_recv()

    bias_out, gain, shift, bias_fc, bias_proj = (vec_ref[k : k + 1, :] for k in range(5))

    total = hid_ref[...].astype(F32) + bias_out
    for t in range(4):
        total += matmul(att[t], w_out_ref[pl.ds(LOCAL * t, LOCAL), :])
    mid[...] = total
    normed_ref[...] = layer_norm(total, gain, shift).astype(BF16)
    normed = normed_ref[...]
    for part in thirds:
        pre = matmul(normed, w_fc_ref[:, part]) + bias_fc[:, part.start : part.start + 256]
        square = pre * pre
        bend = jnp.tanh(GELU_ROOT * pre * (1.0 + GELU_CUBE * square))
        activ_ref[:, part] = (0.5 * pre * (1.0 + bend)).astype(BF16)
        slope = 0.5 * (1.0 + bend) + 0.5 * pre * (1.0 - bend * bend) * GELU_ROOT * (
            1.0 + 3.0 * GELU_CUBE * square
        )
        grad_pre_ref[:, part] = (work[:, part] * slope).astype(BF16)

    grad_pre = grad_pre_ref[...]
    for part in thirds:
        work[:, part] = trans_right(grad_pre, w_fc_ref[part, :])
    own = pl.ds(pl.multiple_of(128 * rank, 128), 128)
    norm_ref[...] = jnp.zeros_like(norm_ref)
    for t in range(4):
        rows = pl.ds(128 * t, 128)
        here = mid[rows, :]
        centred = here - jnp.mean(here, axis=-1, keepdims=True)
        scale = lax.rsqrt(jnp.mean(centred * centred, axis=-1, keepdims=True) + EPS)
        hat = centred * scale
        grad_norm = work[rows, :]
        norm_ref[0:1, :] += jnp.sum(grad_norm * hat, axis=0, keepdims=True)
        norm_ref[1:2, :] += jnp.sum(grad_norm, axis=0, keepdims=True)
        pull = grad_norm * gain
        pull = pull - jnp.mean(pull, axis=-1, keepdims=True)
        pull = pull - hat * jnp.mean(pull * hat, axis=-1, keepdims=True)
        work[rows, :] = scale * pull
    work[own, :] += cot_ref[own, :].astype(F32)

    part_low = work[...].astype(BF16)
    z_copies = []
    for k in (1, 2, 3, 0):
        w_rows = w_out_ref[pl.ds(pl.multiple_of(LOCAL * ranks[k], 16), LOCAL), :]
        z = trans_right(part_low, w_rows)
        z_out[k] = z.astype(BF16)
        if k:
            z_copies.append(send(z_out.at[k, low], z_in.at[k, low], z_sems, k, team[k - 1]))
        else:
            low_own[...] = z[:HALF]
        z_copies.append(send(z_out.at[k, high], z_in.at[k, high], z_sems, 4 + k, across[k]))

    mid_own_ref[...] = work[own, :]
    for k in (1, 2, 3):
        rows = pl.ds(pl.multiple_of(128 * ranks[k], 128), 128)
        mid_parts_ref[k] = work[rows, :].astype(BF16)
    activ = activ_ref[...]
    for part in thirds:
        work[:, part] = matmul(activ, w_proj_ref[:, part])
    out_own_ref[...] = mid[own, :] + bias_proj + work[own, :]
    for k in (1, 2, 3):
        rows = pl.ds(pl.multiple_of(128 * ranks[k], 128), 128)
        out_parts_ref[k] = work[rows, :].astype(BF16)
    mid_parts_ref[0] = jnp.zeros((128, D), BF16)
    out_parts_ref[0] = jnp.zeros((128, D), BF16)
    for t in range(4):
        attended_ref[t] = att[t]

    def weight_gradient(left, right, at):
        for j in range(4):
            block = trans_left(left[:, 256 * j : 256 * j + 256], right)
            late_ref[pl.ds(8 * j, 8), pl.ds(at, 32), :] = block.reshape(8, 32, D).astype(BF16)

    weight_gradient(matmul(normed_ref[...], places_ref[...]).astype(BF16), grad_pre_ref[...], 0)
    weight_gradient(matmul(activ, drop_ref[...]).astype(BF16), cot_ref[...], 32)
    mask = mask_ref[...]
    lines = (
        lay(norm_ref[0:1, :], mask, gain_ref[...])
        + lay(norm_ref[1:2, :], mask, shift_ref[...])
        + lay(column_sum(cot_ref[own, :].astype(F32)), mask, bias_ref[...])
        + lay(column_sum(grad_pre_ref[...].astype(F32)), mask_fc_ref[...], put_fc_ref[...])
    )
    for k in range(GROUPS):
        late_ref[k, pl.ds(48, 16), pl.ds(0, 128)] = jnp.concatenate(
            [
                late_ref[k, pl.ds(48, 16), pl.ds(0, 128)].astype(F32)[:8],
                jnp.broadcast_to(lines[k : k + 1], (8, 128)),
            ],
            axis=0,
        ).astype(BF16)
    for copy in z_copies:
        copy.wait_recv()
    far_copy.wait_recv()
    far_ref[...] = far[...]
    grad_low = low_own[...]
    grad_high = z_in[0, high].astype(F32)
    for k in (1, 2, 3):
        grad_low += z_in[k, low].astype(F32)
        grad_high += z_in[k, high].astype(F32)
    grad_ref[low, :] = grad_low.astype(BF16)
    grad_ref[high, :] = grad_high.astype(BF16)
    for copy in copies + z_copies + [far_copy]:
        copy.wait_send()


def middle(*args):
    def out(shape, dtype):
        return jax.ShapeDtypeStruct(shape, dtype)

    vmem = pl.BlockSpec(memory_space=pltpu.VMEM)
    outs = [
        out((512, LOCAL), BF16),
        out((GROUPS, 64, D), BF16),
        out((4, 512, LOCAL), BF16),
        out((4, 128, D), BF16),
        out((128, D), F32),
        out((4, 128, D), BF16),
        out((128, D), F32),
        out((HALF, D), BF16),
    ]
    return pl.pallas_call(
        middle_kernel,
        out_shape=outs,
        in_specs=[vmem] * 3 + [pl.BlockSpec(memory_space=pl.ANY)] + [vmem] * (len(args) - 4),
        out_specs=[vmem] * len(outs),
        scratch_shapes=[
            pltpu.VMEM((4, 512, LOCAL), BF16),
            pltpu.VMEM((512, D), F32),
            pltpu.VMEM((512, D), F32),
            pltpu.VMEM((HALF, LOCAL), F32),
            pltpu.VMEM((4, 512, LOCAL), BF16),
            pltpu.VMEM((4, 512, LOCAL), BF16),
            pltpu.VMEM((D, D), BF16),
            pltpu.VMEM((D, D), BF16),
            pltpu.VMEM((D, D), BF16),
            pltpu.VMEM((6, GROUPS, 32, 384), BF16),
            pltpu.VMEM((8, D), F32),
            pltpu.VMEM((512, D), BF16),
            pltpu.VMEM((512, D), BF16),
            pltpu.VMEM((512, D), BF16),
            pltpu.VMEM((HALF, D), BF16),
            pltpu.SemaphoreType.DMA((2, 7)),
            pltpu.SemaphoreType.DMA((2, 8)),
            pltpu.SemaphoreType.DMA((6,)),
            pltpu.SemaphoreType.DMA((2, 1)),
        ],
        compiler_params=pltpu.CompilerParams(
            vmem_limit_bytes=VMEM_BYTES, collective_id=1, has_side_effects=True
        ),
        cost_estimate=pl.CostEstimate(
            flops=12 * 512 * D * D, bytes_accessed=16 * 512 * D, transcendentals=512 * D
        ),
    )(*args)


def wrap(value, size):
    return lax.rem(value + size, size)


class Plane:
    def __init__(self, c, g, h):
        self.c, self.g, self.h = c, g, h
        self.y, self.z, self.core = g // 8, (g // 2) % 4, g % 2

    def place(self, first, second, core):
        dz = first * (1 - core) + second * core
        dy = first * core + second * (1 - core)
        return 8 * wrap(self.y + dy, 4) + 2 * wrap(self.z + dz, 4) + core

    def device(self, first, second):
        return (self.c, self.place(first, second, self.core), self.h)

    def sibling(self):
        return (self.c, self.g + 1 - 2 * self.core, self.h)


def shift_of(index):
    return ((index + 1) % 3 + 1) * jnp.minimum(index, 1)


def travel(plane, held, near_sems, pair_sems, tall):
    def halves():
        return (pl.ds(0, tall), pl.ds(tall, tall))

    def source(d, e, core):
        return plane.place(shift_of(d), shift_of(e), core)

    def copy(n, half, slot, first, second):
        rows = halves()[half]
        return pltpu.make_async_remote_copy(
            src_ref=held.at[slot, rows],
            dst_ref=held.at[slot, rows],
            send_sem=near_sems.at[0, half, n],
            recv_sem=near_sems.at[1, half, n],
            device_id=plane.device(first, second),
            device_id_type=MESH,
        )

    def across(n, slot):
        return pltpu.make_async_remote_copy(
            src_ref=held.at[slot],
            dst_ref=held.at[slot],
            send_sem=pair_sems.at[0, n],
            recv_sem=pair_sems.at[1, n],
            device_id=plane.sibling(),
            device_id_type=MESH,
        )

    def each(n, act):
        d, e = n % 4, n // 4
        slot = source(d, e, plane.core)
        act(across(n, slot))

        @pl.when(n == 0)
        def _():
            for half in (0, 1):
                act(copy(1, half, slot, 1, 0))
                act(copy(2, half, slot, 3, 0))

        @pl.when(n == 1)
        def _():
            act(copy(3, 0, slot, 1, 0))

        @pl.when(n == 2)
        def _():
            act(copy(3, 1, slot, 3, 0))

        @pl.when(e == 0)
        def _():
            for half in (0, 1):
                act(copy(4 + d, half, slot, 0, 1))
                act(copy(8 + d, half, slot, 0, 3))

        @pl.when(e == 1)
        def _():
            act(copy(12 + d, 0, slot, 0, 1))

        @pl.when(e == 2)
        def _():
            act(copy(12 + d, 1, slot, 0, 3))

    def depart(n):
        each(n, lambda c: c.start())

    def arrive(n):
        for half in (0, 1):
            copy(n, half, source(n % 4, n // 4, plane.core), 0, 1).wait_recv()
        depart(n)

    def arrive_across(n):
        across(n, source(n % 4, n // 4, 1 - plane.core)).wait_recv()

    def finish():
        def sent(n, carry):
            each(n, lambda c: c.wait_send())
            return carry

        lax.fori_loop(0, 16, sent, 0)

    def place_of(n, other):
        return source(n % 4, n // 4, plane.core + other - 2 * plane.core * other)

    return depart, arrive, arrive_across, place_of, finish


def fused_forward_kernel(
    q_ref, kv_ref, cot_ref, att_ref, nat_ref, lse_ref, far_ref, cot_all_ref, all_ref,
    held, qz, upper, cot, top, total, accum, near_sems, pair_sems, upper_sems, team_sems, out_sems,
):
    c, g, h = lax.axis_index("c"), lax.axis_index("g"), lax.axis_index("h")
    plane = Plane(c, g, h)
    mirror = (c, GROUPS - 1 - g, h)
    rank = 2 * c + h
    team = [(pc, g, ph) for pc, ph in (team_peer(c, h, k) for k in (1, 2, 3))]
    greet(
        team
        + [plane.sibling(), plane.device(1, 0), plane.device(3, 0)]
        + [plane.device(0, 1), plane.device(0, 3), mirror]
    )
    swap = send(q_ref.at[pl.ds(HALF, HALF)], upper, upper_sems, 0, mirror)
    held[g] = kv_ref[...]
    depart, arrive, arrive_across, place_of, finish = travel(plane, held, near_sems, pair_sems, CARGO)
    top[...] = jnp.full_like(top, NEG)
    total[...] = jnp.zeros_like(total)
    accum[...] = jnp.zeros_like(accum)
    left = lax.broadcasted_iota(jnp.int32, (HALF, 128), 1) < 64

    def place_queries(slot, block):
        span = pl.ds(slot * HALF, HALF)
        pair = block[:, :128].astype(F32)
        qz[0, span, :] = jnp.where(left, pair, 0.0).astype(BF16)
        qz[1, span, :] = jnp.where(left, 0.0, pair).astype(BF16)
        qz[2, span, :] = jnp.concatenate(
            [block[:, 128:], jnp.zeros((HALF, 64), BF16)], axis=1
        )

    place_queries(0, q_ref[pl.ds(0, HALF), :])

    def tiles(device, units):
        chains = []
        for slot, halves, masked in units:
            span = pl.ds(slot * HALF, HALF)
            first, second, third = (
                cat([held[device, pl.ds(CARGO * x, HALF), pl.ds(128 * k, 128)] for x in halves])
                for k in range(3)
            )
            second_t, third_t = second.T, third.T
            values = (second_t[64:], third_t[:64], third_t[64:])
            for n, keys in enumerate((first, first, second)):
                scores = nt(keys, qz[n, span, :])
                if masked:
                    scores = jnp.where(diagonal(), scores, NEG)
                chains.append((slot, n, values[n], scores))
        ready = []
        for slot, n, value, scores in chains:
            line = pl.ds(8 * slot + n, 1)
            old = top[line, :]
            new = jnp.maximum(old, jnp.max(scores, axis=0, keepdims=True))
            weights = jnp.exp(scores - new)
            fade = jnp.exp(old - new)
            top[line, :] = new
            total[line, :] = total[line, :] * fade + jnp.sum(weights, axis=0, keepdims=True)
            ready.append((slot, n, value, weights.astype(BF16), fade))
        for slot, n, value, weights, fade in ready:
            accum[slot, n] = accum[slot, n] * fade + matmul(value, weights)

    def keep(slot):
        return pltpu.make_async_copy(held.at[slot], all_ref.at[slot], out_sems.at[slot])

    def work(device):
        keep(device).start()

        low, high = device < g, device < GROUPS - 1 - g

        @pl.when(low & high)
        def _():
            tiles(device, [(0, (0,), False), (1, (0, 1), False)])

        @pl.when(low & ~high)
        def _():
            tiles(device, [(0, (0,), False), (1, (0,), False)])

        @pl.when(~low & high)
        def _():
            tiles(device, [(1, (0, 1), False)])

        @pl.when(~low & ~high)
        def _():
            tiles(device, [(1, (0,), False)])

        @pl.when(device == g)
        def _():
            tiles(device, [(0, (0,), True)])

        @pl.when(device == GROUPS - 1 - g)
        def _():
            tiles(device, [(1, (1,), True)])

    lax.fori_loop(0, 1, lambda n, carry: (depart(n), carry)[1], 0)
    cot_copies = [send(cot_ref, cot.at[rank], team_sems, k, device) for k, device in enumerate(team)]
    swap.wait_recv()
    place_queries(1, upper[...])
    far_ref[pl.ds(0, HALF), :] = q_ref[pl.ds(0, HALF), :]
    far_ref[pl.ds(HALF, HALF), :] = upper[...]

    def step(m, carry):
        n, other = m // 2, m % 2

        @pl.when((other == 0) & (n > 0))
        def _():
            arrive(n)

        @pl.when(other == 1)
        def _():
            arrive_across(n)

        work(place_of(n, other))
        return carry

    lax.fori_loop(0, 32, step, 0)
    for slot in range(2):
        for n in range(3):
            line = pl.ds(8 * slot + n, 1)
            att_ref[slot, pl.ds(64 * n, 64), :] = accum[slot, n] / total[line, :]
        span = pl.ds(slot * HALF, HALF)
        nat_ref[span, :] = att_ref[slot].T.astype(BF16)
        lines = pl.ds(8 * slot, 8)
        lse_ref[:, span] = (top[lines, :] + jnp.log(jnp.maximum(total[lines, :], 1e-30))) * LOG2E
    cot[rank] = cot_ref[...]
    for copy in cot_copies:
        copy.wait_recv()
    for t in range(4):
        cot_all_ref[pl.ds(128 * t, 128), :] = cot[t]
    for copy in cot_copies + [swap]:
        copy.wait_send()
    finish()
    for slot in range(GROUPS):
        keep(slot).wait()


def fused_forward(*args):
    vmem = pl.BlockSpec(memory_space=pltpu.VMEM)
    return pl.pallas_call(
        fused_forward_kernel,
        out_shape=[
            jax.ShapeDtypeStruct((2, LOCAL, HALF), F32),
            jax.ShapeDtypeStruct((512, LOCAL), BF16),
            jax.ShapeDtypeStruct((8, 512), F32),
            jax.ShapeDtypeStruct((512, LOCAL), BF16),
            jax.ShapeDtypeStruct((512, D), BF16),
            jax.ShapeDtypeStruct((GROUPS, 2 * CARGO, 2 * LOCAL), BF16),
        ],
        in_specs=[vmem, vmem, vmem],
        out_specs=[vmem, vmem, vmem, vmem, vmem, pl.BlockSpec(memory_space=pl.ANY)],
        scratch_shapes=[
            pltpu.VMEM((GROUPS, 2 * CARGO, 2 * LOCAL), BF16),
            pltpu.VMEM((3, 512, 128), BF16),
            pltpu.VMEM((HALF, LOCAL), BF16),
            pltpu.VMEM((4, 128, D), BF16),
            pltpu.VMEM((16, HALF), F32),
            pltpu.VMEM((16, HALF), F32),
            pltpu.VMEM((2, 3, 64, HALF), F32),
            pltpu.SemaphoreType.DMA((2, 2, 16)),
            pltpu.SemaphoreType.DMA((2, 16)),
            pltpu.SemaphoreType.DMA((2, 1)),
            pltpu.SemaphoreType.DMA((2, 3)),
            pltpu.SemaphoreType.DMA((GROUPS,)),
        ],
        compiler_params=pltpu.CompilerParams(
            vmem_limit_bytes=VMEM_BYTES, collective_id=2, has_side_effects=True
        ),
        cost_estimate=pl.CostEstimate(
            flops=65 * 3 * HALF * HALF * 1024, bytes_accessed=32 << 20, transcendentals=65 * 3 * HALF * HALF
        ),
    )(*args)


class Lattice:
    def __init__(self, plane, src, pair_in, pair_sum, first_in, first_sum, second_in, sems):
        self.plane, self.src = plane, src
        self.pair_in, self.pair_sum = pair_in, pair_sum
        self.first_in, self.first_sum, self.second_in = first_in, first_sum, second_in

        def copy(src, dst, slot, device):
            return pltpu.make_async_remote_copy(
                src_ref=src,
                dst_ref=dst,
                send_sem=sems.at[0, slot],
                recv_sem=sems.at[1, slot],
                device_id=device,
                device_id_type=MESH,
            )

        self.pair = [
            copy(
                src.at[self.block(a, b, 1 - plane.core)],
                pair_in.at[4 * b + a],
                4 * b + a,
                plane.sibling(),
            )
            for b in range(4)
            for a in range(4)
        ]
        self.first = [
            copy(pair_sum.at[a], first_in.at[a], 16 + a, plane.device(a, 0)) for a in (1, 2, 3)
        ]
        self.second = [
            copy(first_sum.at[b], second_in.at[b], 20 + b, plane.device(0, b)) for b in (1, 2, 3)
        ]

    def block(self, first, second, core):
        return self.plane.place(first, second, self.plane.core) + core - self.plane.core

    def start(self):
        for copy in self.pair:
            copy.start()

    def along_first(self):
        for copy in self.pair:
            copy.wait_recv()
        for a in (1, 2, 3, 0):
            for b in range(4):
                mine = self.src[self.block(a, b, self.plane.core)].astype(F32)
                theirs = self.pair_in[4 * a + b].astype(F32)
                self.pair_sum[a, b] = (mine + theirs).astype(BF16)
            if a:
                self.first[a - 1].start()

    def along_second(self):
        for copy in self.first:
            copy.wait_recv()
        for b in (1, 2, 3, 0):
            total = self.pair_sum[0, b].astype(F32)
            for a in (1, 2, 3):
                total += self.first_in[a, b].astype(F32)
            self.first_sum[b] = total.astype(BF16)
            if b:
                self.second[b - 1].start()

    def result(self):
        for copy in self.second:
            copy.wait_recv()
        total = self.first_sum[0].astype(F32)
        for b in (1, 2, 3):
            total += self.second_in[b].astype(F32)
        return total.astype(BF16)

    def finish(self):
        for copy in self.pair + self.first + self.second:
            copy.wait_send()


def lattice_shapes(rows):
    return [
        pltpu.VMEM((16, rows, D), BF16),
        pltpu.VMEM((4, 4, rows, D), BF16),
        pltpu.VMEM((4, 4, rows, D), BF16),
        pltpu.VMEM((4, rows, D), BF16),
        pltpu.VMEM((4, rows, D), BF16),
        pltpu.SemaphoreType.DMA((2, 24)),
    ]


def place_sides(first, second, span, block):
    left = lax.broadcasted_iota(jnp.int32, (HALF, 128), 1) < 64
    a, b, c = (block[:, 128 * k : 128 * k + 128].astype(F32) for k in range(3))
    for refs, n, part, side in (
        (first, 0, a, left),
        (first, 1, a, ~left),
        (first, 2, b, left),
        (second, 0, b, ~left),
        (second, 1, c, left),
        (second, 2, c, ~left),
    ):
        refs[n, span, :] = jnp.where(side, part, 0.0).astype(BF16)


def backward_kernel(
    q_ref, do_ref, att_ref, lse_ref, kv_ref, mid_parts_ref, mid_own_ref, out_parts_ref, out_own_ref,
    late_ref, dq_ref, dkv_ref, hidden_ref, grad_mid_ref, grad_attn_ref, late_all_ref,
    held, stats, qz, dz, kz, vz, acc_q, acc_k, acc_v, whole, mid_in, out_in, attn,
    pair_in, pair_sum, first_in, first_sum, second_in, late_sems, late_all,
    near_sems, pair_sems, mid_sems, out_sems, attn_sems, late_team_sems,
):
    c, g, h = lax.axis_index("c"), lax.axis_index("g"), lax.axis_index("h")
    plane = Plane(c, g, h)
    rank = 2 * c + h
    team = [(pc, g, ph) for pc, ph in (team_peer(c, h, k) for k in (1, 2, 3))]
    greet(
        team
        + [plane.sibling()]
        + [plane.device(k, 0) for k in (1, 2, 3)]
        + [plane.device(0, k) for k in (1, 2, 3)]
    )

    lattice = Lattice(
        plane, late_ref, pair_in, pair_sum, first_in, first_sum, second_in, late_sems
    )
    late_team = [
        pltpu.make_async_remote_copy(
            src_ref=late_all.at[rank],
            dst_ref=late_all.at[rank],
            send_sem=late_team_sems.at[0, k],
            recv_sem=late_team_sems.at[1, k],
            device_id=team[k - 1],
            device_id_type=MESH,
        )
        for k in (1, 2, 3)
    ]
    mid_copies = [
        send(mid_parts_ref.at[k], mid_in.at[k], mid_sems, k, team[k - 1]) for k in (1, 2, 3)
    ]
    low_rows, high_rows = pl.ds(0, HALF), pl.ds(HALF, HALF)
    for slot, span in enumerate((low_rows, high_rows)):
        block = jnp.concatenate([q_ref[span, :], do_ref[span, :]], axis=1)
        held[g, pl.ds(TALL * slot, HALF), :] = block
        place_sides(qz, dz, span, block)
        grads = block[:, LOCAL:].astype(F32).T
        product = grads * att_ref[slot]
        delta = [jnp.sum(product[64 * n : 64 * n + 64], axis=0, keepdims=True) for n in range(3)]
        lines = jnp.concatenate([lse_ref[0:3, span], *delta, jnp.zeros((2, HALF), F32)], axis=0)
        stats[:, span] = lines
        head = lines.astype(BF16).astype(F32)
        body = (lines - head).astype(BF16).astype(F32)
        tail = lines - head - body
        packed = jnp.concatenate([head, body, tail, jnp.zeros_like(tail)], axis=0)
        held[g, pl.ds(TALL * slot + HALF, 32), pl.ds(0, HALF)] = packed.astype(BF16)
    depart, arrive, arrive_across, place_of, finish = travel(
        plane, held, near_sems, pair_sems, TALL
    )
    lax.fori_loop(0, 1, lambda n, carry: (depart(n), carry)[1], 0)
    lattice.start()
    place_sides(kz, vz, low_rows, kv_ref[g, low_rows, :])
    place_sides(kz, vz, high_rows, kv_ref[GROUPS - 1 - g, pl.ds(CARGO, HALF), :])
    for ref in (acc_q, acc_k, acc_v):
        ref[...] = jnp.zeros_like(ref)

    def groups(block_of):
        return [block_of(pl.ds(128 * k, 128)) for k in range(3)]

    def query_tiles(device, units):
        chains = []
        for slot, halves, masked in units:
            span = pl.ds(slot * HALF, HALF)

            def rows_of(lanes):
                return cat([kv_ref[device, pl.ds(CARGO * x, HALF), lanes] for x in halves])

            a, b, c = groups(rows_of)
            a_t, b_t = a.T, b.T
            for n, (keys, values, keys_t) in enumerate(
                ((a, b, a_t[:64]), (a, c, a_t[64:]), (b, c, b_t[:64]))
            ):
                chains.append(
                    (slot, n, masked, keys_t, nt(keys, qz[n, span, :]), nt(values, dz[n, span, :]))
                )
        ready = []
        for slot, n, masked, keys_t, scores, pull in chains:
            span = pl.ds(slot * HALF, HALF)
            scores = scores * LOG2E - stats[pl.ds(n, 1), span]
            if masked:
                scores = jnp.where(diagonal(), scores, NEG)
            pull = pull - stats[pl.ds(3 + n, 1), span]
            ready.append((slot, n, keys_t, (jnp.exp2(scores) * pull).astype(BF16)))
        for slot, n, keys_t, grad in ready:
            acc_q[slot, n] += matmul(keys_t, grad)

    def key_tiles(device, units):
        chains = []
        for slot, halves, masked in units:
            span = pl.ds(slot * HALF, HALF)

            def rows_of(lanes):
                return cat([held[device, pl.ds(TALL * half, HALF), lanes] for half in halves])

            a, b, c = groups(rows_of)
            lines = cat(
                [
                    held[device, pl.ds(TALL * half + HALF, 32), pl.ds(0, HALF)].astype(F32)
                    for half in halves
                ],
                1,
            )
            lines = lines[0:8] + lines[8:16] + lines[16:24]
            for n, (queries, grads) in enumerate(((a, b), (a, c), (b, c))):
                chains.append(
                    (
                        slot,
                        n,
                        masked,
                        queries,
                        grads,
                        lines,
                        nt(kz[n, span, :], queries),
                        nt(vz[n, span, :], grads),
                    )
                )
        ready = []
        for slot, n, masked, queries, grads, lines, scores, pull in chains:
            scores = scores * LOG2E - lines[n : n + 1]
            if masked:
                scores = jnp.where(diagonal(), scores, NEG)
            weights = jnp.exp2(scores)
            pull = weights * (pull - lines[3 + n : 4 + n])
            ready.append((slot, n, queries, grads, weights.astype(BF16), pull.astype(BF16)))
        for slot, n, queries, grads, weights, pull in ready:
            acc_v[slot, n] += matmul(weights, grads)
            acc_k[slot, n] += matmul(pull, queries)

    def planned(src, dst, sems, k):
        return pltpu.make_async_remote_copy(
            src_ref=src,
            dst_ref=dst,
            send_sem=sems.at[0, k],
            recv_sem=sems.at[1, k],
            device_id=team[k - 1],
            device_id_type=MESH,
        )

    attn_copies = [planned(attn.at[rank], attn.at[rank], attn_sems, k) for k in (1, 2, 3)]
    out_copies = [planned(out_parts_ref.at[k], out_in.at[k], out_sems, k) for k in (1, 2, 3)]

    def step(m, carry):
        n, other = m // 2, m % 2

        @pl.when((other == 0) & (n > 0))
        def _():
            arrive(n)

        @pl.when(other == 1)
        def _():
            arrive_across(n)

        @pl.when(m == 6)
        def _():
            for copy in mid_copies:
                copy.wait_recv()
            grad_mid = mid_own_ref[...]
            for k in (1, 2, 3):
                grad_mid += mid_in[k].astype(F32)
            grad_mid_ref[...] = grad_mid
            attn[rank] = grad_mid.astype(BF16)
            for copy in attn_copies:
                copy.start()

        @pl.when(m == 12)
        def _():
            for copy in out_copies:
                copy.start()

        @pl.when(m == 8)
        def _():
            lattice.along_first()

        @pl.when(m == 18)
        def _():
            lattice.along_second()

        @pl.when(m == 25)
        def _():
            late_all[rank] = lattice.result()
            for copy in late_team:
                copy.start()

        def for_queries(which, carry):
            index = 2 * m + which
            device = place_of(index // 2, index % 2)
            low, high = device < g, device < GROUPS - 1 - g

            @pl.when(low & high)
            def _():
                query_tiles(device, [(0, (0,), False), (1, (0, 1), False)])

            @pl.when(low & ~high)
            def _():
                query_tiles(device, [(0, (0,), False), (1, (0,), False)])

            @pl.when(~low & high)
            def _():
                query_tiles(device, [(1, (0, 1), False)])

            @pl.when(~low & ~high)
            def _():
                query_tiles(device, [(1, (0,), False)])

            @pl.when(device == GROUPS - 1 - g)
            def _():
                query_tiles(device, [(1, (1,), True)])

            @pl.when(device == g)
            def _():
                query_tiles(device, [(0, (0,), True)])

            return carry

        def for_keys(which, carry):
            index = 2 * (m - 16) + which
            device = place_of(index // 2, index % 2)

            @pl.when(device > g)
            def _():
                key_tiles(device, [(0, (0, 1), False)])

            @pl.when(device < g)
            def _():
                key_tiles(device, [(0, (1,), False), (1, (1,), False)])

            @pl.when(device == g)
            def _():
                key_tiles(device, [(0, (0,), True), (1, (1,), True)])
                key_tiles(device, [(0, (1,), False)])

            return carry

        @pl.when(m < 16)
        def _():
            lax.fori_loop(0, 2, for_queries, 0)

        @pl.when(m >= 16)
        def _():
            lax.fori_loop(0, 2, for_keys, 0)

        return carry

    lax.fori_loop(0, 32, step, 0)
    left = lax.broadcasted_iota(jnp.int32, (HALF, 128), 1) < 64
    for slot, span in enumerate((low_rows, high_rows)):
        for n in range(3):
            whole[pl.ds(64 * n, 64), :] = acc_q[slot, n] * 0.125
        dq_ref[span, :] = whole[...].T.astype(BF16)
        for k, (one, two) in enumerate(
            (
                (acc_k[slot, 0], acc_k[slot, 1]),
                (acc_k[slot, 2], acc_v[slot, 0]),
                (acc_v[slot, 1], acc_v[slot, 2]),
            )
        ):
            dkv_ref[span, pl.ds(128 * k, 128)] = jnp.where(left, one, two).astype(BF16)
    for copy in attn_copies + out_copies + late_team:
        copy.wait_recv()
    late_all_ref[...] = late_all[...]
    for t in range(4):
        grad_attn_ref[pl.ds(128 * t, 128), :] = attn[t]
    output = out_own_ref[...]
    for k in (1, 2, 3):
        output += out_in[k].astype(F32)
    hidden_ref[...] = output.astype(BF16)
    for copy in mid_copies + attn_copies + out_copies:
        copy.wait_send()
    for copy in late_team:
        copy.wait_send()
    lattice.finish()
    finish()


def backward(*args):
    vmem = pl.BlockSpec(memory_space=pltpu.VMEM)
    sides_shape = pltpu.VMEM((3, 512, 128), BF16)
    return pl.pallas_call(
        backward_kernel,
        out_shape=[
            jax.ShapeDtypeStruct((512, LOCAL), BF16),
            jax.ShapeDtypeStruct((512, 2 * LOCAL), BF16),
            jax.ShapeDtypeStruct((128, D), BF16),
            jax.ShapeDtypeStruct((128, D), F32),
            jax.ShapeDtypeStruct((512, D), BF16),
            jax.ShapeDtypeStruct((4, 64, D), BF16),
        ],
        in_specs=[vmem] * len(args),
        out_specs=[vmem] * 6,
        scratch_shapes=[
            pltpu.VMEM((GROUPS, 2 * TALL, 2 * LOCAL), BF16),
            pltpu.VMEM((8, 512), F32),
            sides_shape,
            sides_shape,
            sides_shape,
            sides_shape,
            pltpu.VMEM((2, 3, 64, HALF), F32),
            pltpu.VMEM((2, 3, HALF, 128), F32),
            pltpu.VMEM((2, 3, HALF, 128), F32),
            pltpu.VMEM((LOCAL, HALF), F32),
            pltpu.VMEM((4, 128, D), BF16),
            pltpu.VMEM((4, 128, D), BF16),
            pltpu.VMEM((4, 128, D), BF16),
            *lattice_shapes(64),
            pltpu.VMEM((4, 64, D), BF16),
            pltpu.SemaphoreType.DMA((2, 2, 16)),
            pltpu.SemaphoreType.DMA((2, 16)),
            pltpu.SemaphoreType.DMA((2, 4)),
            pltpu.SemaphoreType.DMA((2, 4)),
            pltpu.SemaphoreType.DMA((2, 4)),
            pltpu.SemaphoreType.DMA((2, 4)),
        ],
        compiler_params=pltpu.CompilerParams(
            vmem_limit_bytes=VMEM_BYTES, collective_id=3, has_side_effects=True
        ),
        cost_estimate=pl.CostEstimate(
            flops=65 * 3 * HALF * HALF * 3584,
            bytes_accessed=32 << 20,
            transcendentals=2 * 65 * 3 * HALF * HALF,
        ),
    )(*args)


def head_kernel(
    hid_ref, mine_ref, theirs_ref, mine_two_ref, theirs_two_ref, hid_all_ref, first_ref, second_ref,
    hid, other, other_two, held, team_sems, near_sems, pair_sems,
):
    c, g, h = lax.axis_index("c"), lax.axis_index("g"), lax.axis_index("h")
    rank = 2 * c + h
    plane = Plane(c, g, h)
    team = [(pc, g, ph) for pc, ph in (team_peer(c, h, k) for k in (1, 2, 3))]
    greet(
        team
        + [plane.sibling(), plane.device(1, 0), plane.device(3, 0)]
        + [plane.device(0, 1), plane.device(0, 3)]
    )
    swaps = [
        send(theirs_ref, other, team_sems, 3, team[1]),
        send(theirs_two_ref, other_two, team_sems, 4, team[1]),
    ]
    copies = [send(hid_ref, hid.at[rank], team_sems, k, device) for k, device in enumerate(team)]
    own_rows = pl.ds(pl.multiple_of(16 * c, 16), 16)
    other_rows = pl.ds(pl.multiple_of(16 - 16 * c, 16), 16)
    held[g, own_rows, :] = mine_ref[...]
    second_ref[own_rows, :] = mine_two_ref[...]
    swaps[0].wait_recv()
    held[g, other_rows, :] = other[...]
    depart, arrive, arrive_across, place_of, finish = travel(plane, held, near_sems, pair_sems, 16)
    lax.fori_loop(0, 1, lambda n, carry: (depart(n), carry)[1], 0)
    lax.fori_loop(1, 16, lambda n, carry: (arrive(n), carry)[1], 0)
    hid[rank] = hid_ref[...]
    for copy in copies:
        copy.wait_recv()
    for t in range(4):
        hid_all_ref[pl.ds(128 * t, 128), :] = hid[t]
    swaps[1].wait_recv()
    second_ref[other_rows, :] = other_two[...]
    lax.fori_loop(0, 16, lambda n, carry: (arrive_across(n), carry)[1], 0)
    first_ref[...] = held[...]
    for copy in copies + swaps:
        copy.wait_send()
    finish()


def head(*args):
    vmem = pl.BlockSpec(memory_space=pltpu.VMEM)
    return pl.pallas_call(
        head_kernel,
        out_shape=[
            jax.ShapeDtypeStruct((512, D), BF16),
            jax.ShapeDtypeStruct((GROUPS, 32, 640), BF16),
            jax.ShapeDtypeStruct((32, 2 * D), BF16),
        ],
        in_specs=[vmem] * 5,
        out_specs=[vmem] * 3,
        scratch_shapes=[
            pltpu.VMEM((4, 128, D), BF16),
            pltpu.VMEM((16, 640), BF16),
            pltpu.VMEM((16, 2 * D), BF16),
            pltpu.VMEM((GROUPS, 32, 640), BF16),
            pltpu.SemaphoreType.DMA((2, 5)),
            pltpu.SemaphoreType.DMA((2, 2, 16)),
            pltpu.SemaphoreType.DMA((2, 16)),
        ],
        compiler_params=pltpu.CompilerParams(
            vmem_limit_bytes=VMEM_BYTES, collective_id=4, has_side_effects=True
        ),
        cost_estimate=pl.CostEstimate(flops=0, bytes_accessed=4 << 20, transcendentals=0),
    )(*args)


def tail_kernel(
    dq_ref, dkv_ref, wq_ref, wkv_ref, near_ref, far_ref, places_ref, att_t_ref, attn_ref,
    attn_own_ref, mid_ref, vec_ref,
    mask_ref, gain_ref, shift_ref, bias_ref, mask_q_ref, put_q_ref, mask_kv_ref, put_kv_ref,
    grad_ref, total_ref,
    resid, part, part_out, part_in, out, gathered,
    pair_in, pair_sum, first_in, first_sum, second_in, lattice_sems,
    part_sems, gather_sems,
):
    c, g, h = lax.axis_index("c"), lax.axis_index("g"), lax.axis_index("h")
    rank = 2 * c + h
    mirror = GROUPS - 1 - g
    plane = Plane(c, g, h)
    peers = [team_peer(c, h, k) for k in range(4)]
    team = [(pc, g, ph) for pc, ph in peers[1:]]
    greet(
        team
        + [(pc, mirror, ph) for pc, ph in peers]
        + [plane.sibling()]
        + [plane.device(k, 0) for k in (1, 2, 3)]
        + [plane.device(0, k) for k in (1, 2, 3)]
    )

    low, high = pl.ds(0, HALF), pl.ds(HALF, HALF)
    dq, dkv = dq_ref[...], dkv_ref[...]
    part[...] = matmul(dq, wq_ref[...]) + matmul(dkv, wkv_ref[...])
    for r in range(4):
        part_out[r] = part[pl.ds(128 * r, 128), :].astype(BF16)

    def part_copy(r):
        return pltpu.make_async_remote_copy(
            src_ref=part_out.at[r],
            dst_ref=part_in.at[rank],
            send_sem=part_sems.at[0, r],
            recv_sem=part_sems.at[1, rank],
            device_id=(r // 2, g if r < 2 else mirror, r % 2),
            device_id_type=MESH,
        )

    def each_part(act):
        for r in range(4):
            if r < 2:
                pl.when(rank != r)(lambda r=r: act(part_copy(r)))
            else:
                act(part_copy(r))

    each_part(lambda copy: copy.start())

    resid[low, :] = near_ref[low, :].astype(F32)
    resid[high, :] = far_ref[...].astype(F32)
    gain, shift = vec_ref[0:1, :], vec_ref[1:2, :]

    def normalised(values):
        centred = values - jnp.mean(values, axis=-1, keepdims=True)
        scale = lax.rsqrt(jnp.mean(centred * centred, axis=-1, keepdims=True) + EPS)
        return centred * scale, scale

    hat, _ = normalised(resid[...])
    grads = part[...]
    gain_line, shift_line = column_sum(grads * hat), column_sum(grads)
    normed = (hat * gain + shift).astype(BF16)
    placed = matmul(normed, places_ref[...]).astype(BF16)
    lines = (
        lay(gain_line, mask_ref[...], gain_ref[...])
        + lay(shift_line, mask_ref[...], shift_ref[...])
        + lay(column_sum(attn_own_ref[...].astype(F32)), mask_ref[...], bias_ref[...])
        + lay(column_sum(dq.astype(F32)), mask_q_ref[...], put_q_ref[...])
        + lay(column_sum(dkv.astype(F32)), mask_kv_ref[...], put_kv_ref[...])
    )
    for j in range(4):
        rows = pl.ds(256 * j, 256)
        left = placed[:, 256 * j : 256 * j + 256]
        span = pl.ds(8 * j, 8)
        out[span, :, pl.ds(0, 2 * LOCAL)] = (
            trans_left(left, dkv).reshape(8, 32, 2 * LOCAL).astype(BF16)
        )
        both = jnp.concatenate(
            [trans_left(left, dq), matmul(att_t_ref[rows, :], attn_ref[...])], axis=1
        )
        out[span, :, pl.ds(2 * LOCAL, 2 * LOCAL)] = both.reshape(8, 32, 2 * LOCAL).astype(BF16)
    spare = lax.broadcasted_iota(jnp.int32, (16, 128), 0) >= 12
    for k in range(GROUPS):
        corner = (k, pl.ds(16, 16), pl.ds(0, 128))
        line = jnp.broadcast_to(lines[k : k + 1], (16, 128))
        out[corner] = jnp.where(spare, line, out[corner].astype(F32)).astype(BF16)

    lattice = Lattice(
        plane, out, pair_in, pair_sum, first_in, first_sum, second_in, lattice_sems
    )
    lattice.start()

    def arrived(s):
        return pltpu.make_async_remote_copy(
            src_ref=part_out.at[s],
            dst_ref=part_in.at[s],
            send_sem=part_sems.at[0, s],
            recv_sem=part_sems.at[1, s],
            device_id=(c, mirror, h),
            device_id_type=MESH,
        )

    def input_gradient(own):
        hat, scale = normalised(own)
        pull = sum(part_in[s].astype(F32) for s in range(4)) * gain
        pull = pull - jnp.mean(pull, axis=-1, keepdims=True)
        pull = pull - hat * jnp.mean(pull * hat, axis=-1, keepdims=True)
        grad_ref[...] = mid_ref[...] + scale * pull

    lattice.along_first()

    @pl.when(c == 0)
    def _():
        part_in[rank] = part_out[rank]
        for s in range(4):
            pl.when(rank != s)(lambda s=s: arrived(s).wait_recv())

    @pl.when(c == 1)
    def _():
        for s in range(4):
            arrived(s).wait_recv()

    own = pl.ds(pl.multiple_of(128 * rank, 128), 128)
    input_gradient(near_ref[own, :].astype(F32))
    lattice.along_second()
    gathered[rank] = lattice.result()
    gather_copies = [
        send(gathered.at[rank], gathered.at[rank], gather_sems, k, device)
        for k, device in enumerate(team)
    ]
    for copy in gather_copies:
        copy.wait_recv()
    total_ref[...] = gathered[...]
    each_part(lambda copy: copy.wait_send())
    for copy in gather_copies:
        copy.wait_send()
    lattice.finish()


def tail(*args):
    vmem = pl.BlockSpec(memory_space=pltpu.VMEM)
    dma = pltpu.SemaphoreType.DMA
    return pl.pallas_call(
        tail_kernel,
        out_shape=[
            jax.ShapeDtypeStruct((128, D), F32),
            jax.ShapeDtypeStruct((4, 32, D), BF16),
        ],
        in_specs=[vmem] * len(args),
        out_specs=[vmem] * 2,
        scratch_shapes=[
            pltpu.VMEM((512, D), F32),
            pltpu.VMEM((512, D), F32),
            pltpu.VMEM((4, 128, D), BF16),
            pltpu.VMEM((4, 128, D), BF16),
            pltpu.VMEM((GROUPS, 32, D), BF16),
            pltpu.VMEM((4, 32, D), BF16),
            *lattice_shapes(32),
            dma((2, 4)),
            dma((2, 3)),
        ],
        compiler_params=pltpu.CompilerParams(
            vmem_limit_bytes=VMEM_BYTES, collective_id=5, has_side_effects=True
        ),
        cost_estimate=pl.CostEstimate(
            flops=4 * 512 * D * 3 * LOCAL, bytes_accessed=8 << 20, transcendentals=0
        ),
    )(*args)


def padded_feature(column):
    g, c, r = column // 32, (column // 16) % 2, column % 16
    return jnp.where(r < 12, 12 * (GROUPS * c + g) + r, -1)


def on_device(
    hidden_in,
    ln1_gain,
    ln1_shift,
    w_qkv,
    qv_bias,
    w_out,
    out_bias,
    ln2_gain,
    ln2_shift,
    w_fc,
    fc_bias,
    w_proj,
    proj_bias,
    out_grad,
):
    c, g, h = lax.axis_index("c"), lax.axis_index("g"), lax.axis_index("h")
    rank = 2 * c + h

    spread_places = one_hot(D, 1024, padded_feature)
    drop_pad = one_hot(D, 1024, lambda k: jnp.where(k % 32 < 24, 24 * (k // 32) + k % 32, -1))
    pick_units = one_hot(1536, D, lambda k: 48 * (k // 24) + 24 * h + k % 24)
    small = [ln1_gain, ln1_shift, qv_bias, out_bias, ln2_gain, ln2_shift, fc_bias, proj_bias]
    small = jnp.concatenate([jnp.pad(v.reshape(-1, 12), ((0, 0), (0, 52))) for v in small], axis=0)
    units = matmul(jnp.concatenate([w_fc[:, :1536], w_fc[:, 1536:]], axis=0), pick_units)
    units = units.astype(BF16)

    def columns_for(of_c):
        r = 2 * of_c + h
        qkv = [lax.dynamic_slice_in_dim(w_qkv, D * k + LOCAL * r, LOCAL, 1) for k in range(3)]
        fc = lax.dynamic_slice_in_dim(units, 12 * of_c, 12, 0)
        parts = (jnp.concatenate([*qkv, small], axis=1), jnp.concatenate([fc, w_out], axis=1))
        return tuple(jnp.pad(p, ((0, 4), (0, 0))) for p in parts)

    mine, theirs = columns_for(c), columns_for(1 - c)
    tokens, first, second = head(hidden_in, mine[0], theirs[0], mine[1], theirs[1])
    resid = tokens.astype(F32)
    proj_rows = lax.dynamic_slice_in_dim(w_proj, 24 * h, 24, 0)
    cargo = jnp.concatenate([second, jnp.pad(proj_rows, ((0, 8), (0, 0)))], axis=1)
    cargo = [cargo[:, 384 * k : 384 * k + 384] for k in range(6)]
    first = first.reshape(1024, 640)
    w_qkv_t = matmul(spread_places, first[:, : 3 * LOCAL]).astype(BF16)

    vectors = first[:, 3 * LOCAL : 3 * LOCAL + 12].reshape(GROUPS, 2, 16, 12)[:, :, :12]
    vectors = vectors.reshape(GROUPS, 2, 144).astype(F32)
    vectors = vectors.transpose(1, 0, 2)
    cut, at = [], 0
    for width in SMALL:
        cut.append(vectors[:, :, at : at + width])
        at += width
    gain_one, shift_one, bias_qv, bias_out, gain_two, shift_two = (
        v.reshape(-1) for v in cut[:6]
    )
    bias_proj = cut[7].reshape(-1)
    bias_fc = lax.dynamic_slice_in_dim(
        lax.dynamic_index_in_dim(cut[6], c, 0, False), 24 * h, 24, 1
    ).reshape(-1)
    bias_q = lax.dynamic_slice_in_dim(bias_qv, LOCAL * rank, LOCAL, 0)
    bias_v = lax.dynamic_slice_in_dim(bias_qv, D + LOCAL * rank, LOCAL, 0)
    bias_here = jnp.concatenate([bias_q, jnp.zeros_like(bias_q), bias_v])

    normed1 = layer_norm(resid, gain_one, shift_one).astype(BF16)
    qkv = (matmul(normed1, w_qkv_t) + bias_here).astype(BF16)
    queries = qkv[:, :LOCAL] * jnp.asarray(0.125, BF16)
    keys_values = qkv[:, LOCAL:]
    load = jnp.concatenate(
        [keys_values[:HALF], *cargo[:3], keys_values[HALF:], *cargo[3:]], axis=0
    )
    att_t, attended_zz, lse, query_far, cotangent, kv_all = fused_forward(queries, load, out_grad)

    def ones(rows, columns, test):
        row = lax.broadcasted_iota(jnp.int32, (rows, columns), 0)
        column = lax.broadcasted_iota(jnp.int32, (rows, columns), 1)
        return test(row, column)

    def mask(columns, group_of):
        return ones(GROUPS, columns, lambda r, k: r == group_of(k)).astype(F32)

    def put(rows, lane_of):
        return ones(rows, 128, lambda k, lane: lane == lane_of(k)).astype(BF16)

    by_feature = mask(D, lambda k: (k // 12) % GROUPS)
    at_gain = put(D, lambda k: 12 * (k // 384) + k % 12)
    at_shift = put(D, lambda k: 24 + 12 * (k // 384) + k % 12)
    vec = jnp.stack([bias_out, gain_two, shift_two, bias_fc, bias_proj])
    (
        grad_zz,
        late,
        attended,
        mid_parts,
        mid_own,
        out_parts,
        out_own,
        far_tokens,
    ) = middle(
        attended_zz,
        tokens,
        cotangent,
        kv_all,
        spread_places,
        drop_pad,
        jnp.concatenate([vec, jnp.zeros((3, D), F32)], axis=0),
        by_feature,
        at_gain,
        at_shift,
        put(D, lambda k: 48 + 12 * (k // 384) + k % 12),
        mask(D, lambda k: k // 24),
        put(D, lambda k: 72 + k % 24),
    )
    attended = jnp.concatenate([attended[t] for t in range(4)], axis=1)
    dq, dkv, hidden_out, grad_mid, grad_attn, late = backward(
        query_far, grad_zz, att_t, lse, kv_all, mid_parts, mid_own, out_parts, out_own, late
    )

    w_back = w_qkv_t.T
    input_grad, total_qkv = tail(
        dq,
        dkv,
        w_back[:LOCAL],
        w_back[LOCAL:],
        tokens,
        far_tokens,
        spread_places,
        trans_left_of(spread_places, attended).astype(BF16),
        lax.dynamic_slice_in_dim(grad_attn, LOCAL * rank, LOCAL, 1),
        lax.dynamic_slice_in_dim(grad_attn, 128 * rank, 128, 0),
        grad_mid,
        jnp.concatenate([gain_one[None], shift_one[None], jnp.zeros((6, D), F32)], axis=0),
        by_feature,
        at_gain,
        at_shift,
        put(D, lambda k: 96 + 12 * (k // 384) + k % 12),
        mask(LOCAL, lambda k: 8 * rank + k // 24),
        put(LOCAL, lambda k: 48 + k % 24),
        mask(2 * LOCAL, lambda k: jnp.where(k < LOCAL, -1, 8 * rank + (k - LOCAL) // 24)),
        put(2 * LOCAL, lambda k: 72 + k % 24),
    )

    fc_rows = lax.dynamic_slice_in_dim(late, 16 * c, 16, 1)[:, :12].astype(F32)
    total_wfc = fc_rows.reshape(2, 2, 12, GROUPS, 24).transpose(2, 0, 3, 1, 4).reshape(12, 3072)
    of_c = lax.dynamic_slice_in_dim(late, 2 * c, 2, 0).astype(F32)
    total_wproj = of_c[:, 32:56].reshape(48, D)
    total_fc = of_c[:, 56, 72:96].reshape(48)
    total_late = jnp.sum(late[:, 56, :72].astype(F32), axis=0)

    def late_part(at):
        return lax.dynamic_slice_in_dim(total_late, at + 12 * c, 12, 0)

    qkv_rows = lax.dynamic_slice_in_dim(total_qkv, 16 * c, 16, 1)[:, :12].astype(F32)
    total_wqkv = jnp.concatenate(
        [qkv_rows[t, :, at : at + LOCAL] for at in (2 * LOCAL, 0, LOCAL) for t in range(4)], axis=1
    )

    total_first = jnp.sum(total_qkv[:, 28, :128].astype(F32), axis=0)
    total_wout = jnp.concatenate([qkv_rows[t, :, 3 * LOCAL :] for t in range(4)], axis=1)

    def first_part(at, width):
        return lax.dynamic_slice_in_dim(total_first, at + width * c, width, 0)

    smalls = (
        first_part(0, 12),
        first_part(24, 12),
        first_part(48, 24),
        first_part(96, 12),
        late_part(0),
        late_part(24),
        total_fc,
        late_part(48),
    )
    return (
        hidden_out,
        input_grad,
        smalls[0],
        smalls[1],
        total_wqkv,
        smalls[2],
        total_wout,
        smalls[3],
        smalls[4],
        smalls[5],
        total_wfc,
        smalls[6],
        total_wproj,
        smalls[7],
    )


def solution(mesh):
    cut = Mesh(mesh.devices.reshape(2, GROUPS, 2), ("c", "g", "h"))
    tokens, rows, line = P(("c", "g", "h"), None), P(("c", "g"), None), P(("c", "g"))
    in_specs = (
        tokens, line, line, rows, line, rows, line, line, line, rows, line, rows, line, tokens,
    )
    out_specs = (
        tokens, tokens, line, line, rows, line, rows, line, line, line, rows, line, rows, line,
    )
    return jax.shard_map(
        on_device, mesh=cut, in_specs=in_specs, out_specs=out_specs, check_vma=False
    )
```

```python
import jax
import jax.numpy as jnp
from jax import lax
from jax.experimental import pallas as pl
from jax.experimental.pallas import tpu as pltpu
from jax.sharding import Mesh
from jax.sharding import PartitionSpec as P

D = 768
HEAD_DIM = 64
EPS = 1e-05
NEG = -1e30
LOG2E = 1.4426950408889634
F32 = jnp.float32
BF16 = jnp.bfloat16
HALF = 256
TALL = HALF + 32
CARGO = HALF + 96
GROUPS = 32
TOKENS = 16384
BLOCKS = 2 * GROUPS
LATE_START = 6
LOCAL = 192
VMEM_BYTES = 56 * 1024 * 1024
TEAM = ("c", "h")
SWAP = [(0, 1), (1, 0)]
MIRROR = [(i, GROUPS - 1 - i) for i in range(GROUPS)]
MESH = pl.DeviceIdType.MESH
GELU_ROOT = 0.7978845608028654
GELU_CUBE = 0.044715
SMALL = (12, 12, 24, 12, 12, 12, 48, 12)


def matmul(left, right):
    return jnp.dot(left, right, preferred_element_type=F32)


def trans_left(left, right):
    return lax.dot_general(left, right, (((0,), (0,)), ((), ())), preferred_element_type=F32)


def trans_left_of(left, right):
    return lax.dot_general(left, right, (((0,), (1,)), ((), ())), preferred_element_type=F32)


def trans_right(left, right):
    return lax.dot_general(left, right, (((1,), (1,)), ((), ())), preferred_element_type=F32)


def layer_norm(values, gain, shift):
    mean = jnp.mean(values, axis=-1, keepdims=True)
    centred = values - mean
    spread = jnp.mean(centred * centred, axis=-1, keepdims=True)
    return centred * lax.rsqrt(spread + EPS) * gain + shift


def gelu_tanh(values):
    return jax.nn.gelu(values, approximate=True)


def nt(left, right):
    return lax.dot_general(left, right, (((1,), (1,)), ((), ())), preferred_element_type=F32)


def diagonal():
    key = lax.broadcasted_iota(jnp.int32, (HALF, HALF), 0)
    query = lax.broadcasted_iota(jnp.int32, (HALF, HALF), 1)
    return key <= query


def cat(parts, axis=0):
    return parts[0] if len(parts) == 1 else jnp.concatenate(parts, axis=axis)

def one_hot(rows, columns, row_of_column):
    row = lax.broadcasted_iota(jnp.int32, (rows, columns), 0)
    column = lax.broadcasted_iota(jnp.int32, (rows, columns), 1)
    return (row == row_of_column(column)).astype(BF16)


def lay(line, mask, put):
    top = line.astype(BF16).astype(F32)
    both = [jnp.where(mask > 0, jnp.broadcast_to(v, mask.shape), 0.0) for v in (top, line - top)]
    return sum(matmul(v.astype(BF16), put) for v in both)


def column_sum(value):
    return jnp.sum(value, axis=0, keepdims=True)


def team_peer(c, h, k):
    return lax.rem(c + k // 2, 2), lax.rem(h + k % 2, 2)


def greet(devices):
    barrier = pltpu.get_barrier_semaphore()
    for device in devices:
        pl.semaphore_signal(barrier, inc=1, device_id=device, device_id_type=MESH)
    pl.semaphore_wait(barrier, len(devices))


def send(src, dst, sems, slot, device):
    copy = pltpu.make_async_remote_copy(
        src_ref=src,
        dst_ref=dst,
        send_sem=sems.at[0, slot],
        recv_sem=sems.at[1, slot],
        device_id=device,
        device_id_type=MESH,
    )
    copy.start()
    return copy


def middle_kernel(
    att_ref,
    hid_ref,
    cot_ref,
    all_ref,
    places_ref,
    drop_ref,
    vec_ref,
    mask_ref,
    gain_ref,
    shift_ref,
    bias_ref,
    mask_fc_ref,
    put_fc_ref,
    grad_ref,
    late_ref,
    attended_ref,
    mid_parts_ref,
    mid_own_ref,
    out_parts_ref,
    out_own_ref,
    far_ref,
    att,
    mid,
    work,
    low_own,
    z_out,
    z_in,
    w_out_ref,
    w_fc_ref,
    w_proj_ref,
    brought,
    norm_ref,
    grad_pre_ref,
    normed_ref,
    activ_ref,
    far,
    att_sems,
    z_sems,
    brought_sems,
    far_sems,
):
    c, g, h = lax.axis_index("c"), lax.axis_index("g"), lax.axis_index("h")
    rank = 2 * c + h
    mirror = GROUPS - 1 - g
    peers = [team_peer(c, h, k) for k in range(4)]
    ranks = [2 * pc + ph for pc, ph in peers]
    team = [(pc, g, ph) for pc, ph in peers[1:]]
    across = [(pc, mirror, ph) for pc, ph in peers]
    fetches = []
    for k in range(6):
        at = HALF + 32 * k if k < 3 else CARGO + HALF + 32 * (k - 3)
        fetches.append(
            pltpu.make_async_copy(
                all_ref.at[:, pl.ds(at, 32), :], brought.at[k], brought_sems.at[k]
            )
        )
        fetches[k].start()
    greet(team + across)

    low, high = pl.ds(0, HALF), pl.ds(HALF, HALF)
    copies = [
        send(att_ref.at[low], att.at[rank, low], att_sems, k, device)
        for k, device in enumerate(team)
    ]
    copies += [
        send(att_ref.at[high], att.at[rank, high], att_sems, 3 + k, device)
        for k, device in enumerate(across)
    ]
    far_copy = send(hid_ref.at[high], far, far_sems, 0, across[0])
    att[rank, low, :] = att_ref[low, :]

    for k, (put_ref, w_ref) in enumerate(
        ((places_ref, w_fc_ref), (places_ref, w_out_ref), (drop_ref, w_proj_ref))
    ):
        for half in (0, 1):
            fetches[2 * k + half].wait()
            block = brought[2 * k + half].reshape(1024, 384)
            w_ref[:, pl.ds(384 * half, 384)] = matmul(put_ref[...], block).astype(BF16)

    cotangent = cot_ref[...]
    thirds = [pl.ds(256 * k, 256) for k in range(3)]
    for part in thirds:
        work[:, part] = trans_right(cotangent, w_proj_ref[part, :])
    for copy in copies:
        copy.wait_recv()

    bias_out, gain, shift, bias_fc, bias_proj = (vec_ref[k : k + 1, :] for k in range(5))

    total = hid_ref[...].astype(F32) + bias_out
    for t in range(4):
        total += matmul(att[t], w_out_ref[pl.ds(LOCAL * t, LOCAL), :])
    mid[...] = total
    normed_ref[...] = layer_norm(total, gain, shift).astype(BF16)
    normed = normed_ref[...]
    for part in thirds:
        pre = matmul(normed, w_fc_ref[:, part]) + bias_fc[:, part.start : part.start + 256]
        square = pre * pre
        bend = jnp.tanh(GELU_ROOT * pre * (1.0 + GELU_CUBE * square))
        activ_ref[:, part] = (0.5 * pre * (1.0 + bend)).astype(BF16)
        slope = 0.5 * (1.0 + bend) + 0.5 * pre * (1.0 - bend * bend) * GELU_ROOT * (
            1.0 + 3.0 * GELU_CUBE * square
        )
        grad_pre_ref[:, part] = (work[:, part] * slope).astype(BF16)

    grad_pre = grad_pre_ref[...]
    for part in thirds:
        work[:, part] = trans_right(grad_pre, w_fc_ref[part, :])
    own = pl.ds(pl.multiple_of(128 * rank, 128), 128)
    norm_ref[...] = jnp.zeros_like(norm_ref)
    for t in range(4):
        rows = pl.ds(128 * t, 128)
        here = mid[rows, :]
        centred = here - jnp.mean(here, axis=-1, keepdims=True)
        scale = lax.rsqrt(jnp.mean(centred * centred, axis=-1, keepdims=True) + EPS)
        hat = centred * scale
        grad_norm = work[rows, :]
        norm_ref[0:1, :] += jnp.sum(grad_norm * hat, axis=0, keepdims=True)
        norm_ref[1:2, :] += jnp.sum(grad_norm, axis=0, keepdims=True)
        pull = grad_norm * gain
        pull = pull - jnp.mean(pull, axis=-1, keepdims=True)
        pull = pull - hat * jnp.mean(pull * hat, axis=-1, keepdims=True)
        work[rows, :] = scale * pull
    work[own, :] += cot_ref[own, :].astype(F32)

    part_low = work[...].astype(BF16)
    z_copies = []
    for k in (1, 2, 3, 0):
        w_rows = w_out_ref[pl.ds(pl.multiple_of(LOCAL * ranks[k], 16), LOCAL), :]
        z = trans_right(part_low, w_rows)
        z_out[k] = z.astype(BF16)
        if k:
            z_copies.append(send(z_out.at[k, low], z_in.at[k, low], z_sems, k, team[k - 1]))
        else:
            low_own[...] = z[:HALF]
        z_copies.append(send(z_out.at[k, high], z_in.at[k, high], z_sems, 4 + k, across[k]))

    mid_own_ref[...] = work[own, :]
    for k in (1, 2, 3):
        rows = pl.ds(pl.multiple_of(128 * ranks[k], 128), 128)
        mid_parts_ref[k] = work[rows, :].astype(BF16)
    activ = activ_ref[...]
    for part in thirds:
        work[:, part] = matmul(activ, w_proj_ref[:, part])
    out_own_ref[...] = mid[own, :] + bias_proj + work[own, :]
    for k in (1, 2, 3):
        rows = pl.ds(pl.multiple_of(128 * ranks[k], 128), 128)
        out_parts_ref[k] = work[rows, :].astype(BF16)
    mid_parts_ref[0] = jnp.zeros((128, D), BF16)
    out_parts_ref[0] = jnp.zeros((128, D), BF16)
    for t in range(4):
        attended_ref[t] = att[t]

    def weight_gradient(left, right, at):
        for j in range(4):
            block = trans_left(left[:, 256 * j : 256 * j + 256], right)
            late_ref[pl.ds(8 * j, 8), pl.ds(at, 32), :] = block.reshape(8, 32, D).astype(BF16)

    weight_gradient(matmul(normed_ref[...], places_ref[...]).astype(BF16), grad_pre_ref[...], 0)
    weight_gradient(matmul(activ, drop_ref[...]).astype(BF16), cot_ref[...], 32)
    mask = mask_ref[...]
    lines = (
        lay(norm_ref[0:1, :], mask, gain_ref[...])
        + lay(norm_ref[1:2, :], mask, shift_ref[...])
        + lay(column_sum(cot_ref[own, :].astype(F32)), mask, bias_ref[...])
        + lay(column_sum(grad_pre_ref[...].astype(F32)), mask_fc_ref[...], put_fc_ref[...])
    )
    for k in range(GROUPS):
        late_ref[k, pl.ds(48, 16), pl.ds(0, 128)] = jnp.concatenate(
            [
                late_ref[k, pl.ds(48, 16), pl.ds(0, 128)].astype(F32)[:8],
                jnp.broadcast_to(lines[k : k + 1], (8, 128)),
            ],
            axis=0,
        ).astype(BF16)
    for copy in z_copies:
        copy.wait_recv()
    far_copy.wait_recv()
    far_ref[...] = far[...]
    grad_low = low_own[...]
    grad_high = z_in[0, high].astype(F32)
    for k in (1, 2, 3):
        grad_low += z_in[k, low].astype(F32)
        grad_high += z_in[k, high].astype(F32)
    grad_ref[low, :] = grad_low.astype(BF16)
    grad_ref[high, :] = grad_high.astype(BF16)
    for copy in copies + z_copies + [far_copy]:
        copy.wait_send()


def middle(*args):
    def out(shape, dtype):
        return jax.ShapeDtypeStruct(shape, dtype)

    vmem = pl.BlockSpec(memory_space=pltpu.VMEM)
    outs = [
        out((512, LOCAL), BF16),
        out((GROUPS, 64, D), BF16),
        out((4, 512, LOCAL), BF16),
        out((4, 128, D), BF16),
        out((128, D), F32),
        out((4, 128, D), BF16),
        out((128, D), F32),
        out((HALF, D), BF16),
    ]
    return pl.pallas_call(
        middle_kernel,
        out_shape=outs,
        in_specs=[vmem] * 3 + [pl.BlockSpec(memory_space=pl.ANY)] + [vmem] * (len(args) - 4),
        out_specs=[vmem] * len(outs),
        scratch_shapes=[
            pltpu.VMEM((4, 512, LOCAL), BF16),
            pltpu.VMEM((512, D), F32),
            pltpu.VMEM((512, D), F32),
            pltpu.VMEM((HALF, LOCAL), F32),
            pltpu.VMEM((4, 512, LOCAL), BF16),
            pltpu.VMEM((4, 512, LOCAL), BF16),
            pltpu.VMEM((D, D), BF16),
            pltpu.VMEM((D, D), BF16),
            pltpu.VMEM((D, D), BF16),
            pltpu.VMEM((6, GROUPS, 32, 384), BF16),
            pltpu.VMEM((8, D), F32),
            pltpu.VMEM((512, D), BF16),
            pltpu.VMEM((512, D), BF16),
            pltpu.VMEM((512, D), BF16),
            pltpu.VMEM((HALF, D), BF16),
            pltpu.SemaphoreType.DMA((2, 7)),
            pltpu.SemaphoreType.DMA((2, 8)),
            pltpu.SemaphoreType.DMA((6,)),
            pltpu.SemaphoreType.DMA((2, 1)),
        ],
        compiler_params=pltpu.CompilerParams(
            vmem_limit_bytes=VMEM_BYTES, collective_id=1, has_side_effects=True
        ),
        cost_estimate=pl.CostEstimate(
            flops=12 * 512 * D * D, bytes_accessed=16 * 512 * D, transcendentals=512 * D
        ),
    )(*args)


def wrap(value, size):
    return lax.rem(value + size, size)


class Plane:
    def __init__(self, c, g, h):
        self.c, self.g, self.h = c, g, h
        self.y, self.z, self.core = g // 8, (g // 2) % 4, g % 2

    def place(self, first, second, core):
        dz = first * (1 - core) + second * core
        dy = first * core + second * (1 - core)
        return 8 * wrap(self.y + dy, 4) + 2 * wrap(self.z + dz, 4) + core

    def device(self, first, second):
        return (self.c, self.place(first, second, self.core), self.h)

    def sibling(self):
        return (self.c, self.g + 1 - 2 * self.core, self.h)


def shift_of(index):
    return ((index + 1) % 3 + 1) * jnp.minimum(index, 1)


def travel(plane, held, near_sems, pair_sems, tall):
    def halves():
        return (pl.ds(0, tall), pl.ds(tall, tall))

    def source(d, e, core):
        return plane.place(shift_of(d), shift_of(e), core)

    def copy(n, half, slot, first, second):
        rows = halves()[half]
        return pltpu.make_async_remote_copy(
            src_ref=held.at[slot, rows],
            dst_ref=held.at[slot, rows],
            send_sem=near_sems.at[0, half, n],
            recv_sem=near_sems.at[1, half, n],
            device_id=plane.device(first, second),
            device_id_type=MESH,
        )

    def across(n, slot):
        return pltpu.make_async_remote_copy(
            src_ref=held.at[slot],
            dst_ref=held.at[slot],
            send_sem=pair_sems.at[0, n],
            recv_sem=pair_sems.at[1, n],
            device_id=plane.sibling(),
            device_id_type=MESH,
        )

    def each(n, act):
        d, e = n % 4, n // 4
        slot = source(d, e, plane.core)
        act(across(n, slot))

        @pl.when(n == 0)
        def _():
            for half in (0, 1):
                act(copy(1, half, slot, 1, 0))
                act(copy(2, half, slot, 3, 0))

        @pl.when(n == 1)
        def _():
            act(copy(3, 0, slot, 1, 0))

        @pl.when(n == 2)
        def _():
            act(copy(3, 1, slot, 3, 0))

        @pl.when(e == 0)
        def _():
            for half in (0, 1):
                act(copy(4 + d, half, slot, 0, 1))
                act(copy(8 + d, half, slot, 0, 3))

        @pl.when(e == 1)
        def _():
            act(copy(12 + d, 0, slot, 0, 1))

        @pl.when(e == 2)
        def _():
            act(copy(12 + d, 1, slot, 0, 3))

    def depart(n):
        each(n, lambda c: c.start())

    def arrive(n):
        for half in (0, 1):
            copy(n, half, source(n % 4, n // 4, plane.core), 0, 1).wait_recv()
        depart(n)

    def arrive_across(n):
        across(n, source(n % 4, n // 4, 1 - plane.core)).wait_recv()

    def finish():
        def sent(n, carry):
            each(n, lambda c: c.wait_send())
            return carry

        lax.fori_loop(0, 16, sent, 0)

    def place_of(n, other):
        return source(n % 4, n // 4, plane.core + other - 2 * plane.core * other)

    return depart, arrive, arrive_across, place_of, finish


def fused_forward_kernel(
    q_ref, kv_ref, cot_ref, att_ref, nat_ref, lse_ref, far_ref, cot_all_ref, all_ref,
    held, qz, upper, cot, top, total, accum, near_sems, pair_sems, upper_sems, team_sems, out_sems,
):
    c, g, h = lax.axis_index("c"), lax.axis_index("g"), lax.axis_index("h")
    plane = Plane(c, g, h)
    mirror = (c, GROUPS - 1 - g, h)
    rank = 2 * c + h
    team = [(pc, g, ph) for pc, ph in (team_peer(c, h, k) for k in (1, 2, 3))]
    greet(
        team
        + [plane.sibling(), plane.device(1, 0), plane.device(3, 0)]
        + [plane.device(0, 1), plane.device(0, 3), mirror]
    )
    swap = send(q_ref.at[pl.ds(HALF, HALF)], upper, upper_sems, 0, mirror)
    held[g] = kv_ref[...]
    depart, arrive, arrive_across, place_of, finish = travel(plane, held, near_sems, pair_sems, CARGO)
    top[...] = jnp.full_like(top, NEG)
    total[...] = jnp.zeros_like(total)
    accum[...] = jnp.zeros_like(accum)
    left = lax.broadcasted_iota(jnp.int32, (HALF, 128), 1) < 64

    def place_queries(slot, block):
        span = pl.ds(slot * HALF, HALF)
        pair = block[:, :128].astype(F32)
        qz[0, span, :] = jnp.where(left, pair, 0.0).astype(BF16)
        qz[1, span, :] = jnp.where(left, 0.0, pair).astype(BF16)
        qz[2, span, :] = jnp.concatenate(
            [block[:, 128:], jnp.zeros((HALF, 64), BF16)], axis=1
        )

    place_queries(0, q_ref[pl.ds(0, HALF), :])

    def tiles(device, units):
        chains = []
        for slot, halves, masked in units:
            span = pl.ds(slot * HALF, HALF)
            first, second, third = (
                cat([held[device, pl.ds(CARGO * x, HALF), pl.ds(128 * k, 128)] for x in halves])
                for k in range(3)
            )
            second_t, third_t = second.T, third.T
            values = (second_t[64:], third_t[:64], third_t[64:])
            for n, keys in enumerate((first, first, second)):
                scores = nt(keys, qz[n, span, :])
                if masked:
                    scores = jnp.where(diagonal(), scores, NEG)
                chains.append((slot, n, values[n], scores))
        ready = []
        for slot, n, value, scores in chains:
            line = pl.ds(8 * slot + n, 1)
            old = top[line, :]
            new = jnp.maximum(old, jnp.max(scores, axis=0, keepdims=True))
            weights = jnp.exp(scores - new)
            fade = jnp.exp(old - new)
            top[line, :] = new
            total[line, :] = total[line, :] * fade + jnp.sum(weights, axis=0, keepdims=True)
            ready.append((slot, n, value, weights.astype(BF16), fade))
        for slot, n, value, weights, fade in ready:
            accum[slot, n] = accum[slot, n] * fade + matmul(value, weights)

    def keep(slot):
        return pltpu.make_async_copy(held.at[slot], all_ref.at[slot], out_sems.at[slot])

    def work(device):
        keep(device).start()

        low, high = device < g, device < GROUPS - 1 - g

        @pl.when(low & high)
        def _():
            tiles(device, [(0, (0,), False), (1, (0, 1), False)])

        @pl.when(low & ~high)
        def _():
            tiles(device, [(0, (0,), False), (1, (0,), False)])

        @pl.when(~low & high)
        def _():
            tiles(device, [(1, (0, 1), False)])

        @pl.when(~low & ~high)
        def _():
            tiles(device, [(1, (0,), False)])

        @pl.when(device == g)
        def _():
            tiles(device, [(0, (0,), True)])

        @pl.when(device == GROUPS - 1 - g)
        def _():
            tiles(device, [(1, (1,), True)])

    lax.fori_loop(0, 1, lambda n, carry: (depart(n), carry)[1], 0)
    cot_copies = [send(cot_ref, cot.at[rank], team_sems, k, device) for k, device in enumerate(team)]
    swap.wait_recv()
    place_queries(1, upper[...])
    far_ref[pl.ds(0, HALF), :] = q_ref[pl.ds(0, HALF), :]
    far_ref[pl.ds(HALF, HALF), :] = upper[...]

    def step(m, carry):
        n, other = m // 2, m % 2

        @pl.when((other == 0) & (n > 0))
        def _():
            arrive(n)

        @pl.when(other == 1)
        def _():
            arrive_across(n)

        work(place_of(n, other))
        return carry

    lax.fori_loop(0, 32, step, 0)
    for slot in range(2):
        for n in range(3):
            line = pl.ds(8 * slot + n, 1)
            att_ref[slot, pl.ds(64 * n, 64), :] = accum[slot, n] / total[line, :]
        span = pl.ds(slot * HALF, HALF)
        nat_ref[span, :] = att_ref[slot].T.astype(BF16)
        lines = pl.ds(8 * slot, 8)
        lse_ref[:, span] = (top[lines, :] + jnp.log(jnp.maximum(total[lines, :], 1e-30))) * LOG2E
    cot[rank] = cot_ref[...]
    for copy in cot_copies:
        copy.wait_recv()
    for t in range(4):
        cot_all_ref[pl.ds(128 * t, 128), :] = cot[t]
    for copy in cot_copies + [swap]:
        copy.wait_send()
    finish()
    for slot in range(GROUPS):
        keep(slot).wait()


def fused_forward(*args):
    vmem = pl.BlockSpec(memory_space=pltpu.VMEM)
    return pl.pallas_call(
        fused_forward_kernel,
        out_shape=[
            jax.ShapeDtypeStruct((2, LOCAL, HALF), F32),
            jax.ShapeDtypeStruct((512, LOCAL), BF16),
            jax.ShapeDtypeStruct((8, 512), F32),
            jax.ShapeDtypeStruct((512, LOCAL), BF16),
            jax.ShapeDtypeStruct((512, D), BF16),
            jax.ShapeDtypeStruct((GROUPS, 2 * CARGO, 2 * LOCAL), BF16),
        ],
        in_specs=[vmem, vmem, vmem],
        out_specs=[vmem, vmem, vmem, vmem, vmem, pl.BlockSpec(memory_space=pl.ANY)],
        scratch_shapes=[
            pltpu.VMEM((GROUPS, 2 * CARGO, 2 * LOCAL), BF16),
            pltpu.VMEM((3, 512, 128), BF16),
            pltpu.VMEM((HALF, LOCAL), BF16),
            pltpu.VMEM((4, 128, D), BF16),
            pltpu.VMEM((16, HALF), F32),
            pltpu.VMEM((16, HALF), F32),
            pltpu.VMEM((2, 3, 64, HALF), F32),
            pltpu.SemaphoreType.DMA((2, 2, 16)),
            pltpu.SemaphoreType.DMA((2, 16)),
            pltpu.SemaphoreType.DMA((2, 1)),
            pltpu.SemaphoreType.DMA((2, 3)),
            pltpu.SemaphoreType.DMA((GROUPS,)),
        ],
        compiler_params=pltpu.CompilerParams(
            vmem_limit_bytes=VMEM_BYTES, collective_id=2, has_side_effects=True
        ),
        cost_estimate=pl.CostEstimate(
            flops=65 * 3 * HALF * HALF * 1024, bytes_accessed=32 << 20, transcendentals=65 * 3 * HALF * HALF
        ),
    )(*args)


class Lattice:
    def __init__(self, plane, src, pair_in, pair_sum, first_in, first_sum, second_in, sems):
        self.plane, self.src = plane, src
        self.pair_in, self.pair_sum = pair_in, pair_sum
        self.first_in, self.first_sum, self.second_in = first_in, first_sum, second_in

        def copy(src, dst, slot, device):
            return pltpu.make_async_remote_copy(
                src_ref=src,
                dst_ref=dst,
                send_sem=sems.at[0, slot],
                recv_sem=sems.at[1, slot],
                device_id=device,
                device_id_type=MESH,
            )

        self.pair = [
            copy(
                src.at[self.block(a, b, 1 - plane.core)],
                pair_in.at[4 * b + a],
                4 * b + a,
                plane.sibling(),
            )
            for b in range(4)
            for a in range(4)
        ]
        self.first = [
            copy(pair_sum.at[a], first_in.at[a], 16 + a, plane.device(a, 0)) for a in (1, 2, 3)
        ]
        self.second = [
            copy(first_sum.at[b], second_in.at[b], 20 + b, plane.device(0, b)) for b in (1, 2, 3)
        ]

    def block(self, first, second, core):
        return self.plane.place(first, second, self.plane.core) + core - self.plane.core

    def start(self):
        for copy in self.pair:
            copy.start()

    def along_first(self):
        for copy in self.pair:
            copy.wait_recv()
        for a in (1, 2, 3, 0):
            for b in range(4):
                mine = self.src[self.block(a, b, self.plane.core)].astype(F32)
                theirs = self.pair_in[4 * a + b].astype(F32)
                self.pair_sum[a, b] = (mine + theirs).astype(BF16)
            if a:
                self.first[a - 1].start()

    def along_second(self):
        for copy in self.first:
            copy.wait_recv()
        for b in (1, 2, 3, 0):
            total = self.pair_sum[0, b].astype(F32)
            for a in (1, 2, 3):
                total += self.first_in[a, b].astype(F32)
            self.first_sum[b] = total.astype(BF16)
            if b:
                self.second[b - 1].start()

    def result(self):
        for copy in self.second:
            copy.wait_recv()
        total = self.first_sum[0].astype(F32)
        for b in (1, 2, 3):
            total += self.second_in[b].astype(F32)
        return total.astype(BF16)

    def finish(self):
        for copy in self.pair + self.first + self.second:
            copy.wait_send()


def lattice_shapes(rows):
    return [
        pltpu.VMEM((16, rows, D), BF16),
        pltpu.VMEM((4, 4, rows, D), BF16),
        pltpu.VMEM((4, 4, rows, D), BF16),
        pltpu.VMEM((4, rows, D), BF16),
        pltpu.VMEM((4, rows, D), BF16),
        pltpu.SemaphoreType.DMA((2, 24)),
    ]


def place_sides(first, second, span, block):
    left = lax.broadcasted_iota(jnp.int32, (HALF, 128), 1) < 64
    a, b, c = (block[:, 128 * k : 128 * k + 128].astype(F32) for k in range(3))
    for refs, n, part, side in (
        (first, 0, a, left),
        (first, 1, a, ~left),
        (first, 2, b, left),
        (second, 0, b, ~left),
        (second, 1, c, left),
        (second, 2, c, ~left),
    ):
        refs[n, span, :] = jnp.where(side, part, 0.0).astype(BF16)


def backward_kernel(
    q_ref, do_ref, att_ref, lse_ref, kv_ref, mid_parts_ref, mid_own_ref, out_parts_ref, out_own_ref,
    late_ref, dq_ref, dkv_ref, hidden_ref, grad_mid_ref, grad_attn_ref, late_all_ref,
    held, stats, qz, dz, kz, vz, acc_q, acc_k, acc_v, whole, mid_in, out_in, attn,
    pair_in, pair_sum, first_in, first_sum, second_in, late_sems, late_all,
    near_sems, pair_sems, mid_sems, out_sems, attn_sems, late_team_sems,
):
    c, g, h = lax.axis_index("c"), lax.axis_index("g"), lax.axis_index("h")
    plane = Plane(c, g, h)
    rank = 2 * c + h
    team = [(pc, g, ph) for pc, ph in (team_peer(c, h, k) for k in (1, 2, 3))]
    greet(
        team
        + [plane.sibling()]
        + [plane.device(k, 0) for k in (1, 2, 3)]
        + [plane.device(0, k) for k in (1, 2, 3)]
    )

    lattice = Lattice(
        plane, late_ref, pair_in, pair_sum, first_in, first_sum, second_in, late_sems
    )
    late_team = [
        pltpu.make_async_remote_copy(
            src_ref=late_all.at[rank],
            dst_ref=late_all.at[rank],
            send_sem=late_team_sems.at[0, k],
            recv_sem=late_team_sems.at[1, k],
            device_id=team[k - 1],
            device_id_type=MESH,
        )
        for k in (1, 2, 3)
    ]
    mid_copies = [
        send(mid_parts_ref.at[k], mid_in.at[k], mid_sems, k, team[k - 1]) for k in (1, 2, 3)
    ]
    low_rows, high_rows = pl.ds(0, HALF), pl.ds(HALF, HALF)
    for slot, span in enumerate((low_rows, high_rows)):
        block = jnp.concatenate([q_ref[span, :], do_ref[span, :]], axis=1)
        held[g, pl.ds(TALL * slot, HALF), :] = block
        place_sides(qz, dz, span, block)
        grads = block[:, LOCAL:].astype(F32).T
        product = grads * att_ref[slot]
        delta = [jnp.sum(product[64 * n : 64 * n + 64], axis=0, keepdims=True) for n in range(3)]
        lines = jnp.concatenate([lse_ref[0:3, span], *delta, jnp.zeros((2, HALF), F32)], axis=0)
        stats[:, span] = lines
        head = lines.astype(BF16).astype(F32)
        body = (lines - head).astype(BF16).astype(F32)
        tail = lines - head - body
        packed = jnp.concatenate([head, body, tail, jnp.zeros_like(tail)], axis=0)
        held[g, pl.ds(TALL * slot + HALF, 32), pl.ds(0, HALF)] = packed.astype(BF16)
    depart, arrive, arrive_across, place_of, finish = travel(
        plane, held, near_sems, pair_sems, TALL
    )
    lax.fori_loop(0, 1, lambda n, carry: (depart(n), carry)[1], 0)
    lattice.start()
    place_sides(kz, vz, low_rows, kv_ref[g, low_rows, :])
    place_sides(kz, vz, high_rows, kv_ref[GROUPS - 1 - g, pl.ds(CARGO, HALF), :])
    for ref in (acc_q, acc_k, acc_v):
        ref[...] = jnp.zeros_like(ref)

    def groups(block_of):
        return [block_of(pl.ds(128 * k, 128)) for k in range(3)]

    def query_tiles(device, units):
        chains = []
        for slot, halves, masked in units:
            span = pl.ds(slot * HALF, HALF)

            def rows_of(lanes):
                return cat([kv_ref[device, pl.ds(CARGO * x, HALF), lanes] for x in halves])

            a, b, c = groups(rows_of)
            a_t, b_t = a.T, b.T
            for n, (keys, values, keys_t) in enumerate(
                ((a, b, a_t[:64]), (a, c, a_t[64:]), (b, c, b_t[:64]))
            ):
                chains.append(
                    (slot, n, masked, keys_t, nt(keys, qz[n, span, :]), nt(values, dz[n, span, :]))
                )
        ready = []
        for slot, n, masked, keys_t, scores, pull in chains:
            span = pl.ds(slot * HALF, HALF)
            scores = scores * LOG2E - stats[pl.ds(n, 1), span]
            if masked:
                scores = jnp.where(diagonal(), scores, NEG)
            pull = pull - stats[pl.ds(3 + n, 1), span]
            ready.append((slot, n, keys_t, (jnp.exp2(scores) * pull).astype(BF16)))
        for slot, n, keys_t, grad in ready:
            acc_q[slot, n] += matmul(keys_t, grad)

    def key_tiles(device, units):
        chains = []
        for slot, halves, masked in units:
            span = pl.ds(slot * HALF, HALF)

            def rows_of(lanes):
                return cat([held[device, pl.ds(TALL * half, HALF), lanes] for half in halves])

            a, b, c = groups(rows_of)
            lines = cat(
                [
                    held[device, pl.ds(TALL * half + HALF, 32), pl.ds(0, HALF)].astype(F32)
                    for half in halves
                ],
                1,
            )
            lines = lines[0:8] + lines[8:16] + lines[16:24]
            for n, (queries, grads) in enumerate(((a, b), (a, c), (b, c))):
                chains.append(
                    (
                        slot,
                        n,
                        masked,
                        queries,
                        grads,
                        lines,
                        nt(kz[n, span, :], queries),
                        nt(vz[n, span, :], grads),
                    )
                )
        ready = []
        for slot, n, masked, queries, grads, lines, scores, pull in chains:
            scores = scores * LOG2E - lines[n : n + 1]
            if masked:
                scores = jnp.where(diagonal(), scores, NEG)
            weights = jnp.exp2(scores)
            pull = weights * (pull - lines[3 + n : 4 + n])
            ready.append((slot, n, queries, grads, weights.astype(BF16), pull.astype(BF16)))
        for slot, n, queries, grads, weights, pull in ready:
            acc_v[slot, n] += matmul(weights, grads)
            acc_k[slot, n] += matmul(pull, queries)

    def planned(src, dst, sems, k):
        return pltpu.make_async_remote_copy(
            src_ref=src,
            dst_ref=dst,
            send_sem=sems.at[0, k],
            recv_sem=sems.at[1, k],
            device_id=team[k - 1],
            device_id_type=MESH,
        )

    attn_copies = [planned(attn.at[rank], attn.at[rank], attn_sems, k) for k in (1, 2, 3)]
    out_copies = [planned(out_parts_ref.at[k], out_in.at[k], out_sems, k) for k in (1, 2, 3)]

    def step(u, carry):
        late = jnp.maximum(u - LATE_START, 0)
        m = (4 * late + 3) // 7
        due = (u >= LATE_START) & ((7 * m) // 4 == late) & (m < 32)
        n, other = m // 2, m % 2

        @pl.when(due & (other == 0) & (n > 0))
        def _():
            arrive(n)

        @pl.when(due & (other == 1))
        def _():
            arrive_across(n)

        @pl.when(u == 14)
        def _():
            for copy in mid_copies:
                copy.wait_recv()
            grad_mid = mid_own_ref[...]
            for k in (1, 2, 3):
                grad_mid += mid_in[k].astype(F32)
            grad_mid_ref[...] = grad_mid
            attn[rank] = grad_mid.astype(BF16)
            for copy in attn_copies:
                copy.start()

        @pl.when(u == 26)
        def _():
            for copy in out_copies:
                copy.start()

        @pl.when(u == 20)
        def _():
            lattice.along_first()

        @pl.when(u == 38)
        def _():
            lattice.along_second()

        @pl.when(u == 52)
        def _():
            late_all[rank] = lattice.result()
            for copy in late_team:
                copy.start()

        @pl.when(u < GROUPS)
        def _():
            device = place_of(u // 2, u % 2)
            low, high = device < g, device < GROUPS - 1 - g

            @pl.when(low & high)
            def _():
                query_tiles(device, [(0, (0,), False), (1, (0, 1), False)])

            @pl.when(low & ~high)
            def _():
                query_tiles(device, [(0, (0,), False), (1, (0,), False)])

            @pl.when(~low & high)
            def _():
                query_tiles(device, [(1, (0, 1), False)])

            @pl.when(~low & ~high)
            def _():
                query_tiles(device, [(1, (0,), False)])

            @pl.when(device == GROUPS - 1 - g)
            def _():
                query_tiles(device, [(1, (1,), True)])

            @pl.when(device == g)
            def _():
                query_tiles(device, [(0, (0,), True)])

        @pl.when(u >= GROUPS)
        def _():
            device = place_of((u - GROUPS) // 2, u % 2)

            @pl.when(device > g)
            def _():
                key_tiles(device, [(0, (0, 1), False)])

            @pl.when(device < g)
            def _():
                key_tiles(device, [(0, (1,), False), (1, (1,), False)])

            @pl.when(device == g)
            def _():
                key_tiles(device, [(0, (0,), True), (1, (1,), True)])
                key_tiles(device, [(0, (1,), False)])

        return carry

    lax.fori_loop(0, 2 * GROUPS, step, 0)
    left = lax.broadcasted_iota(jnp.int32, (HALF, 128), 1) < 64
    for slot, span in enumerate((low_rows, high_rows)):
        for n in range(3):
            whole[pl.ds(64 * n, 64), :] = acc_q[slot, n] * 0.125
        dq_ref[span, :] = whole[...].T.astype(BF16)
        for k, (one, two) in enumerate(
            (
                (acc_k[slot, 0], acc_k[slot, 1]),
                (acc_k[slot, 2], acc_v[slot, 0]),
                (acc_v[slot, 1], acc_v[slot, 2]),
            )
        ):
            dkv_ref[span, pl.ds(128 * k, 128)] = jnp.where(left, one, two).astype(BF16)
    for copy in attn_copies + out_copies + late_team:
        copy.wait_recv()
    late_all_ref[...] = late_all[...]
    for t in range(4):
        grad_attn_ref[pl.ds(128 * t, 128), :] = attn[t]
    output = out_own_ref[...]
    for k in (1, 2, 3):
        output += out_in[k].astype(F32)
    hidden_ref[...] = output.astype(BF16)
    for copy in mid_copies + attn_copies + out_copies:
        copy.wait_send()
    for copy in late_team:
        copy.wait_send()
    lattice.finish()
    finish()


def backward(*args):
    vmem = pl.BlockSpec(memory_space=pltpu.VMEM)
    sides_shape = pltpu.VMEM((3, 512, 128), BF16)
    return pl.pallas_call(
        backward_kernel,
        out_shape=[
            jax.ShapeDtypeStruct((512, LOCAL), BF16),
            jax.ShapeDtypeStruct((512, 2 * LOCAL), BF16),
            jax.ShapeDtypeStruct((128, D), BF16),
            jax.ShapeDtypeStruct((128, D), F32),
            jax.ShapeDtypeStruct((512, D), BF16),
            jax.ShapeDtypeStruct((4, 64, D), BF16),
        ],
        in_specs=[vmem] * len(args),
        out_specs=[vmem] * 6,
        scratch_shapes=[
            pltpu.VMEM((GROUPS, 2 * TALL, 2 * LOCAL), BF16),
            pltpu.VMEM((8, 512), F32),
            sides_shape,
            sides_shape,
            sides_shape,
            sides_shape,
            pltpu.VMEM((2, 3, 64, HALF), F32),
            pltpu.VMEM((2, 3, HALF, 128), F32),
            pltpu.VMEM((2, 3, HALF, 128), F32),
            pltpu.VMEM((LOCAL, HALF), F32),
            pltpu.VMEM((4, 128, D), BF16),
            pltpu.VMEM((4, 128, D), BF16),
            pltpu.VMEM((4, 128, D), BF16),
            *lattice_shapes(64),
            pltpu.VMEM((4, 64, D), BF16),
            pltpu.SemaphoreType.DMA((2, 2, 16)),
            pltpu.SemaphoreType.DMA((2, 16)),
            pltpu.SemaphoreType.DMA((2, 4)),
            pltpu.SemaphoreType.DMA((2, 4)),
            pltpu.SemaphoreType.DMA((2, 4)),
            pltpu.SemaphoreType.DMA((2, 4)),
        ],
        compiler_params=pltpu.CompilerParams(
            vmem_limit_bytes=VMEM_BYTES, collective_id=3, has_side_effects=True
        ),
        cost_estimate=pl.CostEstimate(
            flops=65 * 3 * HALF * HALF * 3584,
            bytes_accessed=32 << 20,
            transcendentals=2 * 65 * 3 * HALF * HALF,
        ),
    )(*args)


def head_kernel(
    hid_ref, mine_ref, theirs_ref, mine_two_ref, theirs_two_ref, hid_all_ref, first_ref, second_ref,
    hid, other, other_two, held, team_sems, near_sems, pair_sems,
):
    c, g, h = lax.axis_index("c"), lax.axis_index("g"), lax.axis_index("h")
    rank = 2 * c + h
    plane = Plane(c, g, h)
    team = [(pc, g, ph) for pc, ph in (team_peer(c, h, k) for k in (1, 2, 3))]
    greet(
        team
        + [plane.sibling(), plane.device(1, 0), plane.device(3, 0)]
        + [plane.device(0, 1), plane.device(0, 3)]
    )
    swaps = [
        send(theirs_ref, other, team_sems, 3, team[1]),
        send(theirs_two_ref, other_two, team_sems, 4, team[1]),
    ]
    copies = [send(hid_ref, hid.at[rank], team_sems, k, device) for k, device in enumerate(team)]
    own_rows = pl.ds(pl.multiple_of(16 * c, 16), 16)
    other_rows = pl.ds(pl.multiple_of(16 - 16 * c, 16), 16)
    held[g, own_rows, :] = mine_ref[...]
    second_ref[own_rows, :] = mine_two_ref[...]
    swaps[0].wait_recv()
    held[g, other_rows, :] = other[...]
    depart, arrive, arrive_across, place_of, finish = travel(plane, held, near_sems, pair_sems, 16)
    lax.fori_loop(0, 1, lambda n, carry: (depart(n), carry)[1], 0)
    lax.fori_loop(1, 16, lambda n, carry: (arrive(n), carry)[1], 0)
    hid[rank] = hid_ref[...]
    for copy in copies:
        copy.wait_recv()
    for t in range(4):
        hid_all_ref[pl.ds(128 * t, 128), :] = hid[t]
    swaps[1].wait_recv()
    second_ref[other_rows, :] = other_two[...]
    lax.fori_loop(0, 16, lambda n, carry: (arrive_across(n), carry)[1], 0)
    first_ref[...] = held[...]
    for copy in copies + swaps:
        copy.wait_send()
    finish()


def head(*args):
    vmem = pl.BlockSpec(memory_space=pltpu.VMEM)
    return pl.pallas_call(
        head_kernel,
        out_shape=[
            jax.ShapeDtypeStruct((512, D), BF16),
            jax.ShapeDtypeStruct((GROUPS, 32, 640), BF16),
            jax.ShapeDtypeStruct((32, 2 * D), BF16),
        ],
        in_specs=[vmem] * 5,
        out_specs=[vmem] * 3,
        scratch_shapes=[
            pltpu.VMEM((4, 128, D), BF16),
            pltpu.VMEM((16, 640), BF16),
            pltpu.VMEM((16, 2 * D), BF16),
            pltpu.VMEM((GROUPS, 32, 640), BF16),
            pltpu.SemaphoreType.DMA((2, 5)),
            pltpu.SemaphoreType.DMA((2, 2, 16)),
            pltpu.SemaphoreType.DMA((2, 16)),
        ],
        compiler_params=pltpu.CompilerParams(
            vmem_limit_bytes=VMEM_BYTES, collective_id=4, has_side_effects=True
        ),
        cost_estimate=pl.CostEstimate(flops=0, bytes_accessed=4 << 20, transcendentals=0),
    )(*args)


def tail_kernel(
    dq_ref, dkv_ref, wq_ref, wkv_ref, near_ref, far_ref, places_ref, att_t_ref, attn_ref,
    attn_own_ref, mid_ref, vec_ref,
    mask_ref, gain_ref, shift_ref, bias_ref, mask_q_ref, put_q_ref, mask_kv_ref, put_kv_ref,
    grad_ref, total_ref,
    resid, part, part_out, part_in, out, gathered,
    pair_in, pair_sum, first_in, first_sum, second_in, lattice_sems,
    part_sems, gather_sems,
):
    c, g, h = lax.axis_index("c"), lax.axis_index("g"), lax.axis_index("h")
    rank = 2 * c + h
    mirror = GROUPS - 1 - g
    plane = Plane(c, g, h)
    peers = [team_peer(c, h, k) for k in range(4)]
    team = [(pc, g, ph) for pc, ph in peers[1:]]
    greet(
        team
        + [(pc, mirror, ph) for pc, ph in peers]
        + [plane.sibling()]
        + [plane.device(k, 0) for k in (1, 2, 3)]
        + [plane.device(0, k) for k in (1, 2, 3)]
    )

    low, high = pl.ds(0, HALF), pl.ds(HALF, HALF)
    dq, dkv = dq_ref[...], dkv_ref[...]
    part[...] = matmul(dq, wq_ref[...]) + matmul(dkv, wkv_ref[...])
    for r in range(4):
        part_out[r] = part[pl.ds(128 * r, 128), :].astype(BF16)

    def part_copy(r):
        return pltpu.make_async_remote_copy(
            src_ref=part_out.at[r],
            dst_ref=part_in.at[rank],
            send_sem=part_sems.at[0, r],
            recv_sem=part_sems.at[1, rank],
            device_id=(r // 2, g if r < 2 else mirror, r % 2),
            device_id_type=MESH,
        )

    def each_part(act):
        for r in range(4):
            if r < 2:
                pl.when(rank != r)(lambda r=r: act(part_copy(r)))
            else:
                act(part_copy(r))

    each_part(lambda copy: copy.start())

    resid[low, :] = near_ref[low, :].astype(F32)
    resid[high, :] = far_ref[...].astype(F32)
    gain, shift = vec_ref[0:1, :], vec_ref[1:2, :]

    def normalised(values):
        centred = values - jnp.mean(values, axis=-1, keepdims=True)
        scale = lax.rsqrt(jnp.mean(centred * centred, axis=-1, keepdims=True) + EPS)
        return centred * scale, scale

    hat, _ = normalised(resid[...])
    grads = part[...]
    gain_line, shift_line = column_sum(grads * hat), column_sum(grads)
    normed = (hat * gain + shift).astype(BF16)
    placed = matmul(normed, places_ref[...]).astype(BF16)
    lines = (
        lay(gain_line, mask_ref[...], gain_ref[...])
        + lay(shift_line, mask_ref[...], shift_ref[...])
        + lay(column_sum(attn_own_ref[...].astype(F32)), mask_ref[...], bias_ref[...])
        + lay(column_sum(dq.astype(F32)), mask_q_ref[...], put_q_ref[...])
        + lay(column_sum(dkv.astype(F32)), mask_kv_ref[...], put_kv_ref[...])
    )
    for j in range(4):
        rows = pl.ds(256 * j, 256)
        left = placed[:, 256 * j : 256 * j + 256]
        span = pl.ds(8 * j, 8)
        out[span, :, pl.ds(0, 2 * LOCAL)] = (
            trans_left(left, dkv).reshape(8, 32, 2 * LOCAL).astype(BF16)
        )
        both = jnp.concatenate(
            [trans_left(left, dq), matmul(att_t_ref[rows, :], attn_ref[...])], axis=1
        )
        out[span, :, pl.ds(2 * LOCAL, 2 * LOCAL)] = both.reshape(8, 32, 2 * LOCAL).astype(BF16)
    spare = lax.broadcasted_iota(jnp.int32, (16, 128), 0) >= 12
    for k in range(GROUPS):
        corner = (k, pl.ds(16, 16), pl.ds(0, 128))
        line = jnp.broadcast_to(lines[k : k + 1], (16, 128))
        out[corner] = jnp.where(spare, line, out[corner].astype(F32)).astype(BF16)

    lattice = Lattice(
        plane, out, pair_in, pair_sum, first_in, first_sum, second_in, lattice_sems
    )
    lattice.start()

    def arrived(s):
        return pltpu.make_async_remote_copy(
            src_ref=part_out.at[s],
            dst_ref=part_in.at[s],
            send_sem=part_sems.at[0, s],
            recv_sem=part_sems.at[1, s],
            device_id=(c, mirror, h),
            device_id_type=MESH,
        )

    def input_gradient(own):
        hat, scale = normalised(own)
        pull = sum(part_in[s].astype(F32) for s in range(4)) * gain
        pull = pull - jnp.mean(pull, axis=-1, keepdims=True)
        pull = pull - hat * jnp.mean(pull * hat, axis=-1, keepdims=True)
        grad_ref[...] = mid_ref[...] + scale * pull

    lattice.along_first()

    @pl.when(c == 0)
    def _():
        part_in[rank] = part_out[rank]
        for s in range(4):
            pl.when(rank != s)(lambda s=s: arrived(s).wait_recv())

    @pl.when(c == 1)
    def _():
        for s in range(4):
            arrived(s).wait_recv()

    own = pl.ds(pl.multiple_of(128 * rank, 128), 128)
    input_gradient(near_ref[own, :].astype(F32))
    lattice.along_second()
    gathered[rank] = lattice.result()
    gather_copies = [
        send(gathered.at[rank], gathered.at[rank], gather_sems, k, device)
        for k, device in enumerate(team)
    ]
    for copy in gather_copies:
        copy.wait_recv()
    total_ref[...] = gathered[...]
    each_part(lambda copy: copy.wait_send())
    for copy in gather_copies:
        copy.wait_send()
    lattice.finish()


def tail(*args):
    vmem = pl.BlockSpec(memory_space=pltpu.VMEM)
    dma = pltpu.SemaphoreType.DMA
    return pl.pallas_call(
        tail_kernel,
        out_shape=[
            jax.ShapeDtypeStruct((128, D), F32),
            jax.ShapeDtypeStruct((4, 32, D), BF16),
        ],
        in_specs=[vmem] * len(args),
        out_specs=[vmem] * 2,
        scratch_shapes=[
            pltpu.VMEM((512, D), F32),
            pltpu.VMEM((512, D), F32),
            pltpu.VMEM((4, 128, D), BF16),
            pltpu.VMEM((4, 128, D), BF16),
            pltpu.VMEM((GROUPS, 32, D), BF16),
            pltpu.VMEM((4, 32, D), BF16),
            *lattice_shapes(32),
            dma((2, 4)),
            dma((2, 3)),
        ],
        compiler_params=pltpu.CompilerParams(
            vmem_limit_bytes=VMEM_BYTES, collective_id=5, has_side_effects=True
        ),
        cost_estimate=pl.CostEstimate(
            flops=4 * 512 * D * 3 * LOCAL, bytes_accessed=8 << 20, transcendentals=0
        ),
    )(*args)


def padded_feature(column):
    g, c, r = column // 32, (column // 16) % 2, column % 16
    return jnp.where(r < 12, 12 * (GROUPS * c + g) + r, -1)


def on_device(
    hidden_in,
    ln1_gain,
    ln1_shift,
    w_qkv,
    qv_bias,
    w_out,
    out_bias,
    ln2_gain,
    ln2_shift,
    w_fc,
    fc_bias,
    w_proj,
    proj_bias,
    out_grad,
):
    c, g, h = lax.axis_index("c"), lax.axis_index("g"), lax.axis_index("h")
    rank = 2 * c + h

    spread_places = one_hot(D, 1024, padded_feature)
    drop_pad = one_hot(D, 1024, lambda k: jnp.where(k % 32 < 24, 24 * (k // 32) + k % 32, -1))
    pick_units = one_hot(1536, D, lambda k: 48 * (k // 24) + 24 * h + k % 24)
    small = [ln1_gain, ln1_shift, qv_bias, out_bias, ln2_gain, ln2_shift, fc_bias, proj_bias]
    small = jnp.concatenate([jnp.pad(v.reshape(-1, 12), ((0, 0), (0, 52))) for v in small], axis=0)
    units = matmul(jnp.concatenate([w_fc[:, :1536], w_fc[:, 1536:]], axis=0), pick_units)
    units = units.astype(BF16)

    def columns_for(of_c):
        r = 2 * of_c + h
        qkv = [lax.dynamic_slice_in_dim(w_qkv, D * k + LOCAL * r, LOCAL, 1) for k in range(3)]
        fc = lax.dynamic_slice_in_dim(units, 12 * of_c, 12, 0)
        parts = (jnp.concatenate([*qkv, small], axis=1), jnp.concatenate([fc, w_out], axis=1))
        return tuple(jnp.pad(p, ((0, 4), (0, 0))) for p in parts)

    mine, theirs = columns_for(c), columns_for(1 - c)
    tokens, first, second = head(hidden_in, mine[0], theirs[0], mine[1], theirs[1])
    resid = tokens.astype(F32)
    proj_rows = lax.dynamic_slice_in_dim(w_proj, 24 * h, 24, 0)
    cargo = jnp.concatenate([second, jnp.pad(proj_rows, ((0, 8), (0, 0)))], axis=1)
    cargo = [cargo[:, 384 * k : 384 * k + 384] for k in range(6)]
    first = first.reshape(1024, 640)
    w_qkv_t = matmul(spread_places, first[:, : 3 * LOCAL]).astype(BF16)

    vectors = first[:, 3 * LOCAL : 3 * LOCAL + 12].reshape(GROUPS, 2, 16, 12)[:, :, :12]
    vectors = vectors.reshape(GROUPS, 2, 144).astype(F32)
    vectors = vectors.transpose(1, 0, 2)
    cut, at = [], 0
    for width in SMALL:
        cut.append(vectors[:, :, at : at + width])
        at += width
    gain_one, shift_one, bias_qv, bias_out, gain_two, shift_two = (
        v.reshape(-1) for v in cut[:6]
    )
    bias_proj = cut[7].reshape(-1)
    bias_fc = lax.dynamic_slice_in_dim(
        lax.dynamic_index_in_dim(cut[6], c, 0, False), 24 * h, 24, 1
    ).reshape(-1)
    bias_q = lax.dynamic_slice_in_dim(bias_qv, LOCAL * rank, LOCAL, 0)
    bias_v = lax.dynamic_slice_in_dim(bias_qv, D + LOCAL * rank, LOCAL, 0)
    bias_here = jnp.concatenate([bias_q, jnp.zeros_like(bias_q), bias_v])

    normed1 = layer_norm(resid, gain_one, shift_one).astype(BF16)
    qkv = (matmul(normed1, w_qkv_t) + bias_here).astype(BF16)
    queries = qkv[:, :LOCAL] * jnp.asarray(0.125, BF16)
    keys_values = qkv[:, LOCAL:]
    load = jnp.concatenate(
        [keys_values[:HALF], *cargo[:3], keys_values[HALF:], *cargo[3:]], axis=0
    )
    att_t, attended_zz, lse, query_far, cotangent, kv_all = fused_forward(queries, load, out_grad)

    def ones(rows, columns, test):
        row = lax.broadcasted_iota(jnp.int32, (rows, columns), 0)
        column = lax.broadcasted_iota(jnp.int32, (rows, columns), 1)
        return test(row, column)

    def mask(columns, group_of):
        return ones(GROUPS, columns, lambda r, k: r == group_of(k)).astype(F32)

    def put(rows, lane_of):
        return ones(rows, 128, lambda k, lane: lane == lane_of(k)).astype(BF16)

    by_feature = mask(D, lambda k: (k // 12) % GROUPS)
    at_gain = put(D, lambda k: 12 * (k // 384) + k % 12)
    at_shift = put(D, lambda k: 24 + 12 * (k // 384) + k % 12)
    vec = jnp.stack([bias_out, gain_two, shift_two, bias_fc, bias_proj])
    (
        grad_zz,
        late,
        attended,
        mid_parts,
        mid_own,
        out_parts,
        out_own,
        far_tokens,
    ) = middle(
        attended_zz,
        tokens,
        cotangent,
        kv_all,
        spread_places,
        drop_pad,
        jnp.concatenate([vec, jnp.zeros((3, D), F32)], axis=0),
        by_feature,
        at_gain,
        at_shift,
        put(D, lambda k: 48 + 12 * (k // 384) + k % 12),
        mask(D, lambda k: k // 24),
        put(D, lambda k: 72 + k % 24),
    )
    attended = jnp.concatenate([attended[t] for t in range(4)], axis=1)
    dq, dkv, hidden_out, grad_mid, grad_attn, late = backward(
        query_far, grad_zz, att_t, lse, kv_all, mid_parts, mid_own, out_parts, out_own, late
    )

    w_back = w_qkv_t.T
    input_grad, total_qkv = tail(
        dq,
        dkv,
        w_back[:LOCAL],
        w_back[LOCAL:],
        tokens,
        far_tokens,
        spread_places,
        trans_left_of(spread_places, attended).astype(BF16),
        lax.dynamic_slice_in_dim(grad_attn, LOCAL * rank, LOCAL, 1),
        lax.dynamic_slice_in_dim(grad_attn, 128 * rank, 128, 0),
        grad_mid,
        jnp.concatenate([gain_one[None], shift_one[None], jnp.zeros((6, D), F32)], axis=0),
        by_feature,
        at_gain,
        at_shift,
        put(D, lambda k: 96 + 12 * (k // 384) + k % 12),
        mask(LOCAL, lambda k: 8 * rank + k // 24),
        put(LOCAL, lambda k: 48 + k % 24),
        mask(2 * LOCAL, lambda k: jnp.where(k < LOCAL, -1, 8 * rank + (k - LOCAL) // 24)),
        put(2 * LOCAL, lambda k: 72 + k % 24),
    )

    fc_rows = lax.dynamic_slice_in_dim(late, 16 * c, 16, 1)[:, :12].astype(F32)
    total_wfc = fc_rows.reshape(2, 2, 12, GROUPS, 24).transpose(2, 0, 3, 1, 4).reshape(12, 3072)
    of_c = lax.dynamic_slice_in_dim(late, 2 * c, 2, 0).astype(F32)
    total_wproj = of_c[:, 32:56].reshape(48, D)
    total_fc = of_c[:, 56, 72:96].reshape(48)
    total_late = jnp.sum(late[:, 56, :72].astype(F32), axis=0)

    def late_part(at):
        return lax.dynamic_slice_in_dim(total_late, at + 12 * c, 12, 0)

    qkv_rows = lax.dynamic_slice_in_dim(total_qkv, 16 * c, 16, 1)[:, :12].astype(F32)
    total_wqkv = jnp.concatenate(
        [qkv_rows[t, :, at : at + LOCAL] for at in (2 * LOCAL, 0, LOCAL) for t in range(4)], axis=1
    )

    total_first = jnp.sum(total_qkv[:, 28, :128].astype(F32), axis=0)
    total_wout = jnp.concatenate([qkv_rows[t, :, 3 * LOCAL :] for t in range(4)], axis=1)

    def first_part(at, width):
        return lax.dynamic_slice_in_dim(total_first, at + width * c, width, 0)

    smalls = (
        first_part(0, 12),
        first_part(24, 12),
        first_part(48, 24),
        first_part(96, 12),
        late_part(0),
        late_part(24),
        total_fc,
        late_part(48),
    )
    return (
        hidden_out,
        input_grad,
        smalls[0],
        smalls[1],
        total_wqkv,
        smalls[2],
        total_wout,
        smalls[3],
        smalls[4],
        smalls[5],
        total_wfc,
        smalls[6],
        total_wproj,
        smalls[7],
    )


def solution(mesh):
    cut = Mesh(mesh.devices.reshape(2, GROUPS, 2), ("c", "g", "h"))
    tokens, rows, line = P(("c", "g", "h"), None), P(("c", "g"), None), P(("c", "g"))
    in_specs = (
        tokens, line, line, rows, line, rows, line, line, line, rows, line, rows, line, tokens,
    )
    out_specs = (
        tokens, tokens, line, line, rows, line, rows, line, line, line, rows, line, rows, line,
    )
    return jax.shard_map(
        on_device, mesh=cut, in_specs=in_specs, out_specs=out_specs, check_vma=False
    )
```
